32 devices in a mesh: sec: 2 (over core), row: 8 (over z, y), col: 2 (over x).
Axes of the slice: x: 2, y: 2, z: 4, core: 2. Of those that a mesh axis runs over, the one named last changes fastest.
Arguments:
- grid_terms: float32 [768, 1536, 128], P(('row', 'col'), 'sec'), may hold values from -6 to 6
- pair_orders: int32 [32], replicated, may hold values from 0 to 31, each once
- legendre: bfloat16 [32, 65, 768], P(('sec', 'row', 'col')), may hold values from -0.21875 to 0.21875
- state: bfloat16 [32, 65, 256], P(('sec', 'row', 'col')), may hold values from -6 to 6
- kappa: float32 [128], replicated, may hold values from 0.05 to 5
- right_op: bfloat16 [128, 128], replicated, may hold values from -0.5 to 0.5
- left_op: bfloat16 [128, 128], replicated, may hold values from -0.5 to 0.5
Outputs:
- evolved: float32 [768, 1536, 128], P(('row', 'col'), 'sec')
- new_state: bfloat16 [32, 65, 256], P(('sec', 'row', 'col'))
The draws below stay inside these ranges and needn't reach their ends.
Inputs may be any that keep to these rules, and one draw needn't show every extreme that they name: pair_orders is a permutation: each order below 32 is the lower order of exactly one pair.
All inputs are finite; a program needn't handle non-finite values.
Results may differ from the reference program's by a relative error of at most 0.0085.
Values may be sent and summed in bfloat16 or wider, within the bound.
No kernel may reach another device: no remote copies, remote signals or barrier semaphores. Data moves between devices by JAX's collectives and lax.ppermute only.
A program may use at most 128 MiB of HBM per device.

```python
import math
import jax
import jax.numpy as jnp
from jax import lax

NTH = 768
NPH = 1536
NR = 128
L = 64
PAIRS = 32


def steps_of(rng, extent, shards, least, top_value):
    level = 1.0
    for axis_at, shards_of in shards:
        heights = jax.random.uniform(jax.random.fold_in(jax.random.fold_in(rng, 6), axis_at), (shards_of,), jnp.float32, least / len(shards), top_value / len(shards))
        level = level * jnp.repeat(jnp.exp(heights), extent[axis_at] // shards_of).reshape((-1,) + (1,) * (len(extent) - 1 - axis_at))
    return level


def centred(rng, dims, spread, most, cuts=(), held_as=jnp.bfloat16):
    level = steps_of(rng, dims, cuts, -0.22, 0.18) if cuts else 1.0
    result = jax.random.normal(rng, dims, jnp.float32) * spread * level
    return jnp.minimum(jnp.maximum(result, -most), most).astype(held_as)


def setup_inputs(seed: int = 0) -> dict:
    streams_of = jax.random.split(jax.random.key(seed), 8)
    return {
        "grid_terms": centred(streams_of[0], (NTH, NPH, NR), 1.0, 6.0, ((0, 16), (1, 2)), jnp.float32),
        "pair_orders": jax.random.permutation(streams_of[1], PAIRS).astype(jnp.int32),
        "legendre": centred(streams_of[2], (PAIRS, L + 1, NTH), NTH ** -0.5, 0.21875, ((0, 32),)),
        "state": centred(streams_of[3], (PAIRS, L + 1, 2 * NR), 1.0, 6.0, ((0, 32),)),
        "kappa": jnp.clip(jnp.exp(jax.random.uniform(streams_of[4], (NR,), jnp.float32, math.log(0.05), math.log(5.0))), 0.05, 5.0),
        "right_op": centred(streams_of[5], (NR, NR), NR ** -0.5, 0.5),
        "left_op": centred(streams_of[6], (NR, NR), NR ** -0.5, 0.5),
    }


time_step = 0.5
filter_strength = 36.0
filter_power = 36.0

def reference(grid_terms, pair_orders, legendre, state, kappa, right_op, left_op):
    pair_total = pair_orders.shape[0]
    degrees = 2 * pair_total
    latitudes = grid_terms.shape[0]
    longitudes = grid_terms.shape[1]
    radial = grid_terms.shape[2]
    orders = jnp.stack([pair_orders, degrees - 1 - pair_orders], axis=1).reshape(degrees)
    spectrum = jnp.fft.rfft(grid_terms, axis=1) / math.sqrt(longitudes)
    picked = jnp.take(spectrum, orders, axis=1)
    fourier = jnp.stack([jnp.real(picked), jnp.imag(picked)], axis=2)
    fourier = jnp.transpose(fourier, (1, 0, 2, 3)).reshape(degrees, latitudes, 2 * radial).astype(jnp.bfloat16)
    fourier = lax.optimization_barrier(fourier)
    paired_fourier = fourier.reshape(pair_total, 2, latitudes, 2 * radial)
    row_index = jnp.arange(degrees + 1, dtype=jnp.int32)
    radial_mode = jnp.arange(radial, dtype=jnp.int32).astype(jnp.float32) / radial
    damping = jnp.exp(-filter_strength * radial_mode ** filter_power)
    left_wide = left_op.astype(jnp.float32)
    right_wide = right_op.astype(jnp.float32)

    def one_pair(pieces):
        legend_rows, paired_rows, prior_state, low_order = pieces
        leading = row_index < degrees - low_order
        degree = jnp.where(leading, low_order + row_index, row_index - 1).astype(jnp.float32)
        legend_wide = legend_rows.astype(jnp.float32)
        both_orders = jnp.einsum('it,otx->iox', legend_wide, paired_rows.astype(jnp.float32))
        coefficient = jnp.where(leading[:, None], both_orders[:, 0], both_orders[:, 1])
        right_side = (prior_state.astype(jnp.float32) + time_step * coefficient).astype(jnp.bfloat16)
        right_side = lax.optimization_barrier(right_side).reshape(degrees + 1, 2, radial).astype(jnp.float32)
        eigen_part = jnp.einsum('icr,rk->ick', right_side, right_wide)
        degree_term = degree * (degree + 1.0) / (degrees * degrees)
        factor = damping[None, :] / (1.0 + kappa[None, :] + degree_term[:, None])
        scaled = (eigen_part * factor[:, None, :]).astype(jnp.bfloat16)
        scaled = lax.optimization_barrier(scaled).astype(jnp.float32)
        new_rows = jnp.einsum('ick,kr->icr', scaled, left_wide).astype(jnp.bfloat16).reshape(degrees + 1, 2 * radial)
        new_wide = lax.optimization_barrier(new_rows).astype(jnp.float32)
        split_rows = jnp.stack([jnp.where(leading[:, None], new_wide, 0.0), jnp.where(leading[:, None], 0.0, new_wide)], axis=0)
        synthesis = jnp.einsum('it,oix->otx', legend_wide, split_rows).astype(jnp.bfloat16)
        return (new_rows, synthesis)
    new_state, synthesis = lax.map(one_pair, (legendre, paired_fourier, state, pair_orders))
    values = synthesis.reshape(degrees, latitudes, 2, radial).astype(jnp.float32)
    doubled = jnp.where(orders == 0, 2.0, 1.0).astype(jnp.float32)[:, None, None]
    packed = lax.complex(values[:, :, 0] * doubled, values[:, :, 1] * doubled)
    spectrum_out = jnp.zeros((longitudes // 2 + 1, latitudes, radial), packed.dtype).at[orders].set(packed)
    evolved = jnp.fft.irfft(spectrum_out, n=longitudes, axis=0) * (longitudes / 2.0) / math.sqrt(longitudes)
    evolved = jnp.transpose(evolved, (1, 0, 2)).astype(jnp.float32)
    return (evolved, new_state)
```

```python
import functools
import math

import jax
import jax.numpy as jnp
import numpy as np
from jax import lax
from jax.experimental import pallas as pl
from jax.experimental.pallas import tpu as pltpu
from jax.sharding import PartitionSpec as P

time_step = 0.5
filter_strength = 36.0
filter_power = 36.0


def slot_orders_of(pair_orders):
    order_total = 2 * pair_orders.shape[0]
    return jnp.stack([pair_orders, order_total - 1 - pair_orders], axis=1).reshape(order_total)


def fourier_table(orders, phi_start, phi_count, longitudes):
    longitude = phi_start + lax.iota(jnp.int32, phi_count)
    phase_turns = longitude[:, None] * orders[None, :] % longitudes
    phase_angle = phase_turns.astype(jnp.float32) * (2.0 * math.pi / longitudes)
    norm_scale = 1.0 / math.sqrt(longitudes)
    return jnp.stack(
        [jnp.cos(phase_angle) * norm_scale, -jnp.sin(phase_angle) * norm_scale], axis=-1
    )


def on_device_wide(grid_terms, pair_orders, legendre, state, kappa, right_op, left_op):
    lat_rows, phi_count, radial = grid_terms.shape
    pairs_here = legendre.shape[0]
    degrees = legendre.shape[1] - 1
    latitudes = legendre.shape[2]
    sections = lax.axis_size("sec")
    longitudes = phi_count * sections
    columns = 2 * radial
    section_slots = degrees // sections
    orders = slot_orders_of(pair_orders)
    sec_index = lax.axis_index("sec")
    highest = lax.Precision.HIGHEST
    phi_start = sec_index * phi_count
    sub_orders = orders
    phase_table = fourier_table(sub_orders, phi_start, phi_count, longitudes)
    term = jnp.einsum(
        "tpr,psc->stcr",
        grid_terms,
        phase_table,
        precision=highest,
        preferred_element_type=jnp.float32,
    )
    spectral = lax.psum_scatter(
        term.reshape(section_slots * lax.axis_size("sec"), lat_rows, columns),
        "sec",
        scatter_dimension=0,
        tiled=True,
    ).astype(jnp.bfloat16)
    device = lax.axis_index(("sec", "row", "col"))
    local_orders = lax.dynamic_slice_in_dim(pair_orders, device * pairs_here, pairs_here)
    row_index = lax.iota(jnp.int32, degrees + 1)
    leading = row_index[None, :] < (degrees - local_orders)[:, None]
    degree = jnp.where(leading, local_orders[:, None] + row_index[None, :], row_index[None, :] - 1)
    received = lax.all_to_all(spectral, ("row", "col"), split_axis=0, concat_axis=1, tiled=True)
    item_count = received.shape[2]
    paired = received.reshape(pairs_here, 2, latitudes, item_count)
    both_orders = jnp.einsum("pit,potx->piox", legendre, paired, preferred_element_type=jnp.float32)
    coefficient = jnp.where(leading[:, :, None], both_orders[:, :, 0], both_orders[:, :, 1])
    right_side = (state.astype(jnp.float32) + time_step * coefficient).astype(jnp.bfloat16)
    right_side = right_side.reshape(pairs_here, degrees + 1, 2, radial)
    eigen_part = jnp.einsum(
        "picr,rk->pick", right_side, right_op, preferred_element_type=jnp.float32
    )
    radial_mode = lax.iota(jnp.float32, radial) / radial
    damping = jnp.exp(-filter_strength * radial_mode**filter_power)
    degree_wide = degree.astype(jnp.float32)
    degree_term = degree_wide * (degree_wide + 1.0) / (degrees * degrees)
    factor = damping[None, None, :] / (1.0 + kappa[None, None, :] + degree_term[:, :, None])
    scaled = (eigen_part * factor[:, :, None, :]).astype(jnp.bfloat16)
    new_state = jnp.einsum("pick,kr->picr", scaled, left_op, preferred_element_type=jnp.float32)
    new_state = new_state.astype(jnp.bfloat16).reshape(pairs_here, degrees + 1, columns)
    zero_rows = jnp.zeros_like(new_state)
    split_state = jnp.stack(
        [
            jnp.where(leading[:, :, None], new_state, zero_rows),
            jnp.where(leading[:, :, None], zero_rows, new_state),
        ],
        axis=1,
    )
    synthesis_wide = jnp.einsum(
        "pit,poix->potx", legendre, split_state, preferred_element_type=jnp.float32
    )
    synthesis = synthesis_wide.astype(jnp.bfloat16).reshape(2 * pairs_here, latitudes, columns)
    returned = lax.all_to_all(synthesis, ("row", "col"), split_axis=1, concat_axis=0, tiled=True)
    sub_orders = lax.dynamic_slice_in_dim(orders, sec_index * section_slots, section_slots)
    phase_table = fourier_table(sub_orders, 0, longitudes, longitudes)
    values = returned.astype(jnp.float32).reshape(section_slots, lat_rows, 2, radial)
    partial_value = jnp.einsum(
        "stcr,psc->tpr", values, phase_table, precision=highest, preferred_element_type=jnp.float32
    )
    evolved = lax.psum_scatter(
        partial_value.astype(jnp.bfloat16), "sec", scatter_dimension=1, tiled=True
    ).astype(jnp.float32)
    return (evolved, new_state)


def natural_table(pair_total, sections, phi_count):
    slots = 2 * pair_total
    longitudes = sections * phi_count
    low = np.arange(pair_total)
    orders = np.stack([low, slots - 1 - low], axis=1).reshape(slots)
    turns = orders[:, None] * np.arange(longitudes)[None, :] % longitudes
    angle = turns * (2.0 * np.pi / longitudes)
    table = np.concatenate([np.cos(angle), -np.sin(angle)], axis=0) / np.sqrt(longitudes)
    return table.reshape(2 * slots, sections, phi_count).transpose(1, 0, 2).astype(np.float32)


def params(mib, **more):
    return pltpu.CompilerParams(vmem_limit_bytes=mib * 1024 * 1024, **more)


def whole(memory_space=pltpu.VMEM):
    return pl.BlockSpec(memory_space=memory_space)


def forward_kernel(table_ref, grid_ref, out_ref, held):
    step = pl.program_id(0)
    lat_block, _, radial = grid_ref.shape
    blocks, rows = held.shape[0], held.shape[1]
    slots = rows // 2
    table = table_ref[lax.axis_index("sec")]
    for at in range(0, lat_block, 2):
        two = jnp.concatenate(
            [grid_ref[at].astype(jnp.bfloat16), grid_ref[at + 1].astype(jnp.bfloat16)], axis=1
        )
        sums = jnp.dot(table, two, preferred_element_type=jnp.float32)
        held[step, :, at, :] = sums[:, :radial]
        held[step, :, at + 1, :] = sums[:, radial:]

    @pl.when(step == blocks - 1)
    def _():
        for block in range(0, blocks, 2):
            for part in range(2):
                rows_of = pl.ds(part * slots, slots)
                both = jnp.concatenate([held[block, rows_of], held[block + 1, rows_of]], axis=1)
                out_ref[:, pl.ds(block * lat_block, 2 * lat_block), pl.ds(part * radial, radial)] = (
                    both.astype(jnp.bfloat16)
                )


def forward_sums(table, grid_terms, lat_block):
    sections, rows, phi_count = table.shape
    lat_rows, _, radial = grid_terms.shape
    blocks = lat_rows // lat_block
    return pl.pallas_call(
        forward_kernel,
        grid=(blocks,),
        in_specs=[
            pl.BlockSpec((sections, rows, phi_count), lambda step: (0, 0, 0)),
            pl.BlockSpec((lat_block, phi_count, radial), lambda step: (step, 0, 0)),
        ],
        out_specs=pl.BlockSpec((rows // 2, lat_rows, 2 * radial), lambda step: (0, 0, 0)),
        out_shape=jax.ShapeDtypeStruct((rows // 2, lat_rows, 2 * radial), jnp.bfloat16),
        scratch_shapes=[pltpu.VMEM((blocks, rows, lat_block, radial), jnp.float32)],
        compiler_params=params(40),
        cost_estimate=pl.CostEstimate(
            flops=2 * rows * phi_count * lat_rows * radial,
            bytes_accessed=4 * lat_rows * phi_count * radial,
            transcendentals=0,
        ),
    )(table, grid_terms)


def degrees_kernel(turn, orders_ref, legendre_ref, fourier_ref, out_ref):
    count, rows = out_ref.shape[0], out_ref.shape[1]
    sections = lax.axis_size("sec")
    first = lax.rem(lax.axis_index("sec") + turn, sections) * count
    row_index = lax.broadcasted_iota(jnp.int32, (rows, legendre_ref.shape[2]), 0)
    for at in range(count):
        order = orders_ref[first + at]
        weights = legendre_ref[first + at]
        leading = row_index < rows - 1 - order
        zero = jnp.zeros_like(weights)
        total = jnp.dot(
            jnp.where(leading, weights, zero),
            fourier_ref[2 * order],
            preferred_element_type=jnp.float32,
        ) + jnp.dot(
            jnp.where(leading, zero, weights),
            fourier_ref[2 * order + 1],
            preferred_element_type=jnp.float32,
        )
        out_ref[at] = total.astype(out_ref.dtype)


def degree_sums(turn, pair_orders, legendre, fourier, count):
    pair_total, rows, lat_rows = legendre.shape
    columns = fourier.shape[2]
    return pl.pallas_call(
        functools.partial(degrees_kernel, turn),
        in_specs=[whole(pltpu.SMEM), whole(), whole()],
        out_specs=whole(),
        out_shape=jax.ShapeDtypeStruct((count, rows, columns), jnp.bfloat16),
        compiler_params=params(24),
        cost_estimate=pl.CostEstimate(
            flops=4 * count * rows * lat_rows * columns,
            bytes_accessed=fourier.size * 2 + count * rows * columns * 2,
            transcendentals=0,
        ),
    )(pair_orders, legendre, fourier)


def plane_kernel(plane, kept_ref, taken_ref, *out_refs):
    side_y, side_x = plane
    here_y = lax.rem(lax.axis_index("row"), side_y)
    here_x = lax.axis_index("col")
    at = 0
    for step_y in range(side_y):
        for step_x in range(side_x):
            to = lax.rem(here_y + step_y, side_y) * side_x + lax.rem(here_x + step_x, side_x)
            for deep in range(kept_ref.shape[0]):
                total = kept_ref[deep, to].astype(jnp.float32) + taken_ref[deep, to].astype(jnp.float32)
                out_refs[at][deep] = total.astype(jnp.bfloat16)
            at += 1


def depth_kernel(side_y, depth, *refs):
    takes, outs = refs[: len(refs) - depth], refs[len(refs) - depth :]
    here = lax.axis_index("row") // side_y
    for step in range(depth):
        to = lax.rem(here + step, depth)
        total = takes[0][to].astype(jnp.float32)
        for other in takes[1:]:
            total += other[to].astype(jnp.float32)
        outs[step][...] = total.astype(outs[step].dtype)


def solve_kernel(parts, *refs):
    takes = refs[:parts]
    orders_ref, state_ref, degree_free_ref, damping_ref, right_ref, left_ref, out_ref = refs[parts:]
    rows = state_ref.shape[1]
    radial = right_ref.shape[0]
    degrees = rows - 1
    sec, row, col = (lax.axis_index(name) for name in ("sec", "row", "col"))
    pair = (sec * lax.axis_size("row") + row) * lax.axis_size("col") + col
    order = orders_ref[pair]
    coefficient = takes[0][...].astype(jnp.float32)
    for other in takes[1:]:
        coefficient += other[...].astype(jnp.float32)
    right_side = (state_ref[0].astype(jnp.float32) + time_step * coefficient).astype(jnp.bfloat16)
    row_index = lax.broadcasted_iota(jnp.int32, (rows, radial), 0)
    degree = jnp.where(row_index < degrees - order, order + row_index, row_index - 1)
    degree = degree.astype(jnp.float32)
    factor = damping_ref[...] / (
        1.0 + degree_free_ref[...] + degree * (degree + 1.0) / (degrees * degrees)
    )
    for part in range(2):
        columns = pl.ds(part * radial, radial)
        eigen = jnp.dot(
            right_side[:, part * radial : (part + 1) * radial],
            right_ref[...],
            preferred_element_type=jnp.float32,
        )
        scaled = (eigen * factor).astype(jnp.bfloat16)
        out_ref[0, :, columns] = jnp.dot(
            scaled, left_ref[...], preferred_element_type=jnp.float32
        ).astype(jnp.bfloat16)


def inverse_kernel(orders_ref, legendre_ref, state_ref, table_ref, out_ref, held):
    step = pl.program_id(0)
    pair_total, rows, lat_rows = legendre_ref.shape
    blocks, slot_rows, lat_block, radial = held.shape
    slots = slot_rows // 2

    @pl.when(step == 0)
    def _():
        row_index = lax.broadcasted_iota(jnp.int32, (rows, lat_rows), 0)
        for pair in range(pair_total):
            order = orders_ref[pair]
            weights = legendre_ref[pair]
            leading = row_index < rows - 1 - order
            zero = jnp.zeros_like(weights)
            fields = state_ref[pair]
            for half in range(2):
                kept = jnp.where(leading, weights, zero) if half == 0 else jnp.where(leading, zero, weights)
                rebuilt = lax.dot_general(
                    kept, fields, (((0,), (0,)), ((), ())), preferred_element_type=jnp.float32
                )
                for part in range(2):
                    held[:, part * slots + 2 * order + half] = rebuilt[
                        :, part * radial : (part + 1) * radial
                    ].reshape(blocks, lat_block, radial)

    table = table_ref[lax.axis_index("sec")]
    for at in range(0, lat_block, 2):
        two = jnp.concatenate(
            [
                held[step, :, at, :].astype(jnp.bfloat16),
                held[step, :, at + 1, :].astype(jnp.bfloat16),
            ],
            axis=1,
        )
        values = jnp.dot(table, two, preferred_element_type=jnp.float32)
        out_ref[at] = values[:, :radial]
        out_ref[at + 1] = values[:, radial:]


def inverse_values(pair_orders, legendre, new_states, table, lat_block):
    pair_total, rows, lat_rows = legendre.shape
    sections, phi_count, slot_rows = table.shape
    radial = new_states.shape[2] // 2
    blocks = lat_rows // lat_block
    return pl.pallas_call(
        inverse_kernel,
        grid=(blocks,),
        in_specs=[
            whole(pltpu.SMEM),
            pl.BlockSpec((pair_total, rows, lat_rows), lambda step: (0, 0, 0)),
            pl.BlockSpec(new_states.shape, lambda step: (0, 0, 0)),
            pl.BlockSpec(table.shape, lambda step: (0, 0, 0)),
        ],
        out_specs=pl.BlockSpec((lat_block, phi_count, radial), lambda step: (step, 0, 0)),
        out_shape=jax.ShapeDtypeStruct((lat_rows, phi_count, radial), jnp.float32),
        scratch_shapes=[pltpu.VMEM((blocks, slot_rows, lat_block, radial), jnp.float32)],
        compiler_params=params(40),
        cost_estimate=pl.CostEstimate(
            flops=2 * slot_rows * phi_count * lat_rows * radial,
            bytes_accessed=4 * lat_rows * phi_count * radial,
            transcendentals=0,
        ),
    )(pair_orders, legendre, new_states, table)


names = ("sec", "row", "col")


def shifted(sizes, shift):
    pairs = []
    for source in np.ndindex(*sizes):
        target = tuple((at + by) % size for at, by, size in zip(source, shift, sizes))
        pairs.append((int(np.ravel_multi_index(source, sizes)), int(np.ravel_multi_index(target, sizes))))
    return pairs


def on_device_compact(grid_terms, pair_orders, legendre, state, kappa, right_op, left_op):
    lat_rows, phi_count, radial = grid_terms.shape
    rows = legendre.shape[1]
    columns = 2 * radial
    pair_total = pair_orders.shape[0]
    sections, side_row, side_x = (lax.axis_size(name) for name in names)
    side_y = 2 if side_row % 2 == 0 else 1
    depth = side_row // side_y
    plane = side_y * side_x
    sizes = (sections, depth, side_y, side_x)
    lat_block = 8
    table = natural_table(pair_total, sections, phi_count)
    forward_table = jnp.asarray(table, jnp.bfloat16)
    inverse_table = jnp.asarray(table.transpose(0, 2, 1), jnp.bfloat16)

    cut = legendre.reshape(rows, side_row * side_x, lat_rows).transpose(1, 0, 2)
    cut = jnp.concatenate([cut] * sections, axis=0)
    legendre_here = lax.all_to_all(cut, names, split_axis=0, concat_axis=0, tiled=True)

    fourier = forward_sums(forward_table, grid_terms, lat_block)
    count = pair_total // sections
    sent = degree_sums(1, pair_orders, legendre_here, fourier, count)
    taken = lax.ppermute(sent, names, shifted(sizes, (1, 0, 0, 0)))
    kept = degree_sums(0, pair_orders, legendre_here, fourier, count)

    block = jax.ShapeDtypeStruct((depth, rows, columns), jnp.bfloat16)
    slabs = pl.pallas_call(
        functools.partial(plane_kernel, (side_y, side_x)),
        in_specs=[whole()] * 2,
        out_specs=[whole()] * plane,
        out_shape=[block] * plane,
        compiler_params=params(16),
    )(
        kept.reshape(depth, plane, rows, columns),
        taken.reshape(depth, plane, rows, columns),
    )
    moved = [slabs[0]]
    for at in range(1, plane):
        moved.append(lax.ppermute(slabs[at], names, shifted(sizes, (0, 0, at // side_x, at % side_x))))

    single = jax.ShapeDtypeStruct((rows, columns), jnp.bfloat16)
    lines = pl.pallas_call(
        functools.partial(depth_kernel, side_y, depth),
        in_specs=[whole()] * plane,
        out_specs=[whole()] * depth,
        out_shape=[jax.ShapeDtypeStruct((rows, columns), jnp.float32)] + [single] * (depth - 1),
        compiler_params=params(16),
    )(*moved)
    parts = [lines[0]]
    for at in range(1, depth):
        parts.append(lax.ppermute(lines[at], names, shifted(sizes, (0, at, 0, 0))))

    radial_mode = np.arange(radial, dtype=np.float32) / np.float32(radial)
    damping = np.exp(-filter_strength * radial_mode**filter_power).astype(np.float32)
    new_state = pl.pallas_call(
        functools.partial(solve_kernel, len(parts)),
        in_specs=[whole()] * len(parts) + [whole(pltpu.SMEM)] + [whole()] * 5,
        out_specs=whole(),
        out_shape=jax.ShapeDtypeStruct((1, rows, columns), jnp.bfloat16),
        compiler_params=params(16),
    )(*parts, pair_orders, state, kappa[None, :], jnp.asarray(damping)[None, :], right_op, left_op)
    new_states = lax.all_gather(new_state, names, axis=0, tiled=True)
    evolved = inverse_values(pair_orders, legendre_here, new_states, inverse_table, lat_block)
    return (evolved, new_state)


def on_device(*args):
    lat_rows = args[0].shape[0]
    rows = args[2].shape[1]
    if args[2].shape[0] == 1 and lat_rows % 16 == 0 and rows <= 2 * lat_rows:
        return on_device_compact(*args)
    return on_device_wide(*args)


def solution(mesh):
    return jax.shard_map(
        on_device,
        mesh=mesh,
        in_specs=(
            P(("row", "col"), "sec", None),
            P(),
            P(("sec", "row", "col"), None, None),
            P(("sec", "row", "col"), None, None),
            P(),
            P(),
            P(),
        ),
        out_specs=(P(("row", "col"), "sec", None), P(("sec", "row", "col"), None, None)),
        check_vma=False,
    )
```

```python
import functools
import math

import jax
import jax.numpy as jnp
import numpy as np
from jax import lax
from jax.experimental import pallas as pl
from jax.experimental.pallas import tpu as pltpu
from jax.sharding import PartitionSpec as P

time_step = 0.5
filter_strength = 36.0
filter_power = 36.0


def slot_orders_of(pair_orders):
    order_total = 2 * pair_orders.shape[0]
    return jnp.stack([pair_orders, order_total - 1 - pair_orders], axis=1).reshape(order_total)


def fourier_table(orders, phi_start, phi_count, longitudes):
    longitude = phi_start + lax.iota(jnp.int32, phi_count)
    phase_turns = longitude[:, None] * orders[None, :] % longitudes
    phase_angle = phase_turns.astype(jnp.float32) * (2.0 * math.pi / longitudes)
    norm_scale = 1.0 / math.sqrt(longitudes)
    return jnp.stack(
        [jnp.cos(phase_angle) * norm_scale, -jnp.sin(phase_angle) * norm_scale], axis=-1
    )


def on_device_wide(grid_terms, pair_orders, legendre, state, kappa, right_op, left_op):
    lat_rows, phi_count, radial = grid_terms.shape
    pairs_here = legendre.shape[0]
    degrees = legendre.shape[1] - 1
    latitudes = legendre.shape[2]
    sections = lax.axis_size("sec")
    longitudes = phi_count * sections
    columns = 2 * radial
    section_slots = degrees // sections
    orders = slot_orders_of(pair_orders)
    sec_index = lax.axis_index("sec")
    highest = lax.Precision.HIGHEST
    phi_start = sec_index * phi_count
    sub_orders = orders
    phase_table = fourier_table(sub_orders, phi_start, phi_count, longitudes)
    term = jnp.einsum(
        "tpr,psc->stcr",
        grid_terms,
        phase_table,
        precision=highest,
        preferred_element_type=jnp.float32,
    )
    spectral = lax.psum_scatter(
        term.reshape(section_slots * lax.axis_size("sec"), lat_rows, columns),
        "sec",
        scatter_dimension=0,
        tiled=True,
    ).astype(jnp.bfloat16)
    device = lax.axis_index(("sec", "row", "col"))
    local_orders = lax.dynamic_slice_in_dim(pair_orders, device * pairs_here, pairs_here)
    row_index = lax.iota(jnp.int32, degrees + 1)
    leading = row_index[None, :] < (degrees - local_orders)[:, None]
    degree = jnp.where(leading, local_orders[:, None] + row_index[None, :], row_index[None, :] - 1)
    received = lax.all_to_all(spectral, ("row", "col"), split_axis=0, concat_axis=1, tiled=True)
    item_count = received.shape[2]
    paired = received.reshape(pairs_here, 2, latitudes, item_count)
    both_orders = jnp.einsum("pit,potx->piox", legendre, paired, preferred_element_type=jnp.float32)
    coefficient = jnp.where(leading[:, :, None], both_orders[:, :, 0], both_orders[:, :, 1])
    right_side = (state.astype(jnp.float32) + time_step * coefficient).astype(jnp.bfloat16)
    right_side = right_side.reshape(pairs_here, degrees + 1, 2, radial)
    eigen_part = jnp.einsum(
        "picr,rk->pick", right_side, right_op, preferred_element_type=jnp.float32
    )
    radial_mode = lax.iota(jnp.float32, radial) / radial
    damping = jnp.exp(-filter_strength * radial_mode**filter_power)
    degree_wide = degree.astype(jnp.float32)
    degree_term = degree_wide * (degree_wide + 1.0) / (degrees * degrees)
    factor = damping[None, None, :] / (1.0 + kappa[None, None, :] + degree_term[:, :, None])
    scaled = (eigen_part * factor[:, :, None, :]).astype(jnp.bfloat16)
    new_state = jnp.einsum("pick,kr->picr", scaled, left_op, preferred_element_type=jnp.float32)
    new_state = new_state.astype(jnp.bfloat16).reshape(pairs_here, degrees + 1, columns)
    zero_rows = jnp.zeros_like(new_state)
    split_state = jnp.stack(
        [
            jnp.where(leading[:, :, None], new_state, zero_rows),
            jnp.where(leading[:, :, None], zero_rows, new_state),
        ],
        axis=1,
    )
    synthesis_wide = jnp.einsum(
        "pit,poix->potx", legendre, split_state, preferred_element_type=jnp.float32
    )
    synthesis = synthesis_wide.astype(jnp.bfloat16).reshape(2 * pairs_here, latitudes, columns)
    returned = lax.all_to_all(synthesis, ("row", "col"), split_axis=1, concat_axis=0, tiled=True)
    sub_orders = lax.dynamic_slice_in_dim(orders, sec_index * section_slots, section_slots)
    phase_table = fourier_table(sub_orders, 0, longitudes, longitudes)
    values = returned.astype(jnp.float32).reshape(section_slots, lat_rows, 2, radial)
    partial_value = jnp.einsum(
        "stcr,psc->tpr", values, phase_table, precision=highest, preferred_element_type=jnp.float32
    )
    evolved = lax.psum_scatter(
        partial_value.astype(jnp.bfloat16), "sec", scatter_dimension=1, tiled=True
    ).astype(jnp.float32)
    return (evolved, new_state)


names = ("sec", "row", "col")


def natural_table(pair_total, sections, phi_count):
    slots = 2 * pair_total
    longitudes = sections * phi_count
    low = np.arange(pair_total)
    orders = np.stack([low, slots - 1 - low], axis=1).reshape(slots)
    turns = orders[:, None] * np.arange(longitudes)[None, :] % longitudes
    angle = turns * (2.0 * np.pi / longitudes)
    table = np.concatenate([np.cos(angle), -np.sin(angle)], axis=0) / np.sqrt(longitudes)
    return table.reshape(2 * slots, sections, phi_count).transpose(1, 0, 2).astype(np.float32)


def params(mib):
    return pltpu.CompilerParams(vmem_limit_bytes=mib * 1024 * 1024)


def vmem():
    return pl.BlockSpec(memory_space=pltpu.VMEM)


def smem():
    return pl.BlockSpec(memory_space=pltpu.SMEM)


def anywhere():
    return pl.BlockSpec(memory_space=pl.ANY)


def call(kernel, operands, out_shapes, mib=16, scalars=0, cost=None):
    single = not isinstance(out_shapes, (list, tuple))
    return pl.pallas_call(
        kernel,
        in_specs=[smem()] * scalars + [vmem()] * (len(operands) - scalars),
        out_specs=vmem() if single else [vmem()] * len(out_shapes),
        out_shape=out_shapes,
        compiler_params=params(mib),
        cost_estimate=cost,
    )(*operands)


class Places:
    def __init__(self):
        self.sections, side_row, self.side_x = (lax.axis_size(name) for name in names)
        self.side_y = 2 if side_row % 2 == 0 else 1
        self.depth = side_row // self.side_y
        self.sizes = (self.sections, self.depth, self.side_y, self.side_x)

    def pair(self, sec, deep, y, x):
        at_sec = lax.axis_index("sec") ^ sec
        at_row = lax.axis_index("row") ^ (deep * self.side_y + y)
        at_col = lax.axis_index("col") ^ x
        return (at_sec * (self.depth * self.side_y) + at_row) * self.side_x + at_col

    def move(self, array, sec=0, deep=0, y=0, x=0):
        shift = (sec, deep, y, x)
        pairs = []
        for source in np.ndindex(*self.sizes):
            target = tuple(at ^ by for at, by in zip(source, shift))
            pairs.append(
                (
                    int(np.ravel_multi_index(source, self.sizes)),
                    int(np.ravel_multi_index(target, self.sizes)),
                )
            )
        return lax.ppermute(array, names, pairs)


def cut_kernel(legendre_ref, out_ref):
    copies, lat_rows, rows = out_ref.shape
    turned = jnp.pad(
        legendre_ref[0].astype(jnp.float32), ((0, rows - legendre_ref.shape[1]), (0, 0))
    ).T.astype(jnp.bfloat16)
    parts = turned.shape[0] // lat_rows
    for at in range(copies):
        begin = at % parts * lat_rows
        out_ref[at] = turned[begin : begin + lat_rows]


def forward_kernel(table_ref, grid_ref, out_ref, buffer, held, sems):
    blocks, rows, lat_block, radial = held.shape
    slots = rows // 2
    chunks = sems.shape[0]

    def chunk(at):
        return pltpu.make_async_copy(
            grid_ref.at[pl.ds(2 * at, 2)], buffer.at[pl.ds(2 * at, 2)], sems.at[at]
        )

    for at in range(chunks):
        chunk(at).start()
    table = table_ref[lax.axis_index("sec")]

    def one_block(block, carry):
        for at in range(0, lat_block, 2):
            lat = block * lat_block + at
            chunk(lat // 2).wait()
            two = jnp.concatenate(
                [buffer[lat].astype(jnp.bfloat16), buffer[lat + 1].astype(jnp.bfloat16)], axis=1
            )
            sums = jnp.dot(table, two, preferred_element_type=jnp.float32)
            held[block, :, at, :] = sums[:, :radial]
            held[block, :, at + 1, :] = sums[:, radial:]
        return carry

    lax.fori_loop(0, blocks, one_block, 0)
    for block in range(0, blocks, 2):
        for part in range(2):
            rows_of = pl.ds(part * slots, slots)
            both = jnp.concatenate([held[block, rows_of], held[block + 1, rows_of]], axis=1)
            out_ref[:, pl.ds(block * lat_block, 2 * lat_block), pl.ds(part * radial, radial)] = (
                both.astype(jnp.bfloat16)
            )


def forward_sums(table, grid_terms, lat_block):
    sections, rows, phi_count = table.shape
    lat_rows, _, radial = grid_terms.shape
    blocks = lat_rows // lat_block
    return pl.pallas_call(
        forward_kernel,
        in_specs=[vmem(), anywhere()],
        out_specs=vmem(),
        out_shape=jax.ShapeDtypeStruct((rows // 2, lat_rows, 2 * radial), jnp.bfloat16),
        scratch_shapes=[
            pltpu.VMEM(grid_terms.shape, jnp.float32),
            pltpu.VMEM((blocks, rows, lat_block, radial), jnp.float32),
            pltpu.SemaphoreType.DMA((lat_rows // 2,)),
        ],
        compiler_params=params(36),
        cost_estimate=pl.CostEstimate(
            flops=2 * rows * phi_count * lat_rows * radial,
            bytes_accessed=4 * lat_rows * phi_count * radial,
            transcendentals=0,
        ),
    )(table, grid_terms)


def masked(weights, order, degrees):
    row_index = lax.broadcasted_iota(jnp.int32, weights.shape, 1)
    leading = row_index < degrees - order
    zero = jnp.zeros_like(weights)
    return jnp.where(leading, weights, zero), jnp.where(leading, zero, weights)


def degrees_kernel(places, sec, degrees, orders_ref, legendre_ref, fourier_ref, out_ref):
    side_x, side_y = places.side_x, places.side_y
    contract = (((0,), (0,)), ((), ()))
    for deep, y, x in np.ndindex(places.depth, side_y, side_x):
        pair = places.pair(sec, int(deep), int(y), int(x))
        order = orders_ref[pair]
        lower, upper = masked(legendre_ref[pair], order, degrees)
        total = lax.dot_general(
            lower, fourier_ref[2 * order], contract, preferred_element_type=jnp.float32
        ) + lax.dot_general(
            upper, fourier_ref[2 * order + 1], contract, preferred_element_type=jnp.float32
        )
        out_ref[y, x, deep] = total.astype(out_ref.dtype)


def plane_kernel(kept_ref, taken_ref, keep_a, send_a, keep_b, send_b):
    radial = keep_a.shape[-1]
    for y in range(2):
        for x in range(2):
            total = kept_ref[y, x] + taken_ref[y, x].astype(jnp.float32)
            part_a, part_b = total[..., :radial], total[..., radial:]
            if x == 0:
                keep_a[y] = part_a
            else:
                send_a[y] = part_a.astype(jnp.bfloat16)
            if y == 0:
                keep_b[x] = part_b
            else:
                send_b[x] = part_b.astype(jnp.bfloat16)


def cross_kernel(keep_a, take_a, keep_b, take_b, keep_a2, send_a2, keep_b2, send_b2):
    keep_a2[...] = keep_a[0] + take_a[0].astype(jnp.float32)
    send_a2[...] = (keep_a[1] + take_a[1].astype(jnp.float32)).astype(jnp.bfloat16)
    keep_b2[...] = keep_b[0] + take_b[0].astype(jnp.float32)
    send_b2[...] = (keep_b[1] + take_b[1].astype(jnp.float32)).astype(jnp.bfloat16)


def depth_kernel(keep_a, take_a, keep_b, take_b, *outs):
    radial = keep_a.shape[-1]
    for deep, out in enumerate(outs):
        out[:, :radial] = (keep_a[deep] + take_a[deep].astype(jnp.float32)).astype(out.dtype)
        out[:, radial:] = (keep_b[deep] + take_b[deep].astype(jnp.float32)).astype(out.dtype)


def solve_kernel(places, orders_ref, *refs):
    takes = refs[: places.depth]
    state_ref, kappa_ref, damping_ref, right_ref, left_ref, out_ref, sent_ref = refs[places.depth :]
    rows = state_ref.shape[1]
    radial = right_ref.shape[0]
    degrees = rows - 1
    order = orders_ref[places.pair(0, 0, 0, 0)]
    coefficient = takes[0][...].astype(jnp.float32)
    for other in takes[1:]:
        coefficient += other[...].astype(jnp.float32)
    right_side = state_ref[0].astype(jnp.float32) + time_step * coefficient[:rows]
    right_side = right_side.astype(jnp.bfloat16)
    row_index = lax.broadcasted_iota(jnp.int32, (rows, radial), 0)
    degree = jnp.where(row_index < degrees - order, order + row_index, row_index - 1)
    degree = degree.astype(jnp.float32)
    factor = damping_ref[...] / (
        1.0 + kappa_ref[...] + degree * (degree + 1.0) / (degrees * degrees)
    )
    sent_ref[...] = jnp.zeros_like(sent_ref)
    for part in range(2):
        columns = pl.ds(part * radial, radial)
        eigen = jnp.dot(
            right_side[:, part * radial : (part + 1) * radial],
            right_ref[...],
            preferred_element_type=jnp.float32,
        )
        scaled = (eigen * factor).astype(jnp.bfloat16)
        field = jnp.dot(scaled, left_ref[...], preferred_element_type=jnp.float32)
        field = field.astype(jnp.bfloat16)
        out_ref[0, :, columns] = field
        sent_ref[pl.ds(0, rows), columns] = field


def spread_kernel(*refs):
    fields, (out_a, out_b) = refs[:-2], refs[-2:]
    radial = out_a.shape[-1]
    for deep, field in enumerate(fields):
        out_a[deep] = field[:, :radial]
        out_b[deep] = field[:, radial:]


def join_kernel(own_a, take_a, own_b, take_b, out_a, out_b):
    out_a[0] = own_a[...]
    out_a[1] = take_a[...]
    out_b[0] = own_b[...]
    out_b[1] = take_b[...]


def inverse_kernel(places, degrees, orders_ref, legendre_ref, table_ref, *refs):
    fields, (out_ref, buffer, held, sems) = refs[:-4], refs[-4:]
    blocks, slot_rows, lat_block, radial = held.shape
    slots = slot_rows // 2
    per_section = len(fields) // places.sections

    for sec in range(places.sections):
        own_a, far_a, own_b, far_b = fields[sec * per_section : (sec + 1) * per_section]
        for deep, y, x in np.ndindex(places.depth, places.side_y, places.side_x):
            deep, y, x = int(deep), int(y), int(x)
            pair = places.pair(sec, deep, y, x)
            order = orders_ref[pair]
            weights = masked(legendre_ref[pair], order, degrees)
            both = ((far_a if y else own_a)[x, deep], (far_b if x else own_b)[y, deep])
            field = jnp.concatenate(both, axis=1)
            for half in range(2):
                rebuilt = jnp.dot(weights[half], field, preferred_element_type=jnp.float32)
                for part in range(2):
                    held[:, part * slots + 2 * order + half] = rebuilt[
                        :, part * radial : (part + 1) * radial
                    ].reshape(blocks, lat_block, radial)

    table = table_ref[lax.axis_index("sec")]

    def chunk(at):
        return pltpu.make_async_copy(
            buffer.at[pl.ds(2 * at, 2)], out_ref.at[pl.ds(2 * at, 2)], sems.at[at]
        )

    def one_block(block, carry):
        for at in range(0, lat_block, 2):
            two = jnp.concatenate(
                [
                    held[block, :, at, :].astype(jnp.bfloat16),
                    held[block, :, at + 1, :].astype(jnp.bfloat16),
                ],
                axis=1,
            )
            values = jnp.dot(table, two, preferred_element_type=jnp.float32)
            lat = block * lat_block + at
            buffer[lat] = values[:, :radial]
            buffer[lat + 1] = values[:, radial:]
            chunk(lat // 2).start()
        return carry

    lax.fori_loop(0, blocks, one_block, 0)
    for at in range(sems.shape[0]):
        chunk(at).wait()


def inverse_values(places, degrees, pair_orders, legendre, table, fields, lat_rows, lat_block):
    _, phi_count, slot_rows = table.shape
    radial = fields[0].shape[-1]
    blocks = lat_rows // lat_block
    out = jax.ShapeDtypeStruct((lat_rows, phi_count, radial), jnp.float32)
    return pl.pallas_call(
        functools.partial(inverse_kernel, places, degrees),
        in_specs=[smem()] + [vmem()] * (2 + len(fields)),
        out_specs=anywhere(),
        out_shape=out,
        scratch_shapes=[
            pltpu.VMEM(out.shape, jnp.float32),
            pltpu.VMEM((blocks, slot_rows, lat_block, radial), jnp.float32),
            pltpu.SemaphoreType.DMA((lat_rows // 2,)),
        ],
        compiler_params=params(36),
        cost_estimate=pl.CostEstimate(
            flops=2 * slot_rows * phi_count * lat_rows * radial,
            bytes_accessed=4 * lat_rows * phi_count * radial,
            transcendentals=0,
        ),
    )(pair_orders, legendre, table, *fields)


def on_device_compact(grid_terms, pair_orders, legendre, state, kappa, right_op, left_op):
    lat_rows, phi_count, radial = grid_terms.shape
    rows = legendre.shape[1]
    degrees = rows - 1
    padded = -(-rows // 8) * 8
    columns = 2 * radial
    pair_total = pair_orders.shape[0]
    places = Places()
    depth = places.depth
    lat_block = 8
    table = natural_table(pair_total, places.sections, phi_count)
    forward_table = jnp.asarray(table, jnp.bfloat16)
    inverse_table = jnp.asarray(table.transpose(0, 2, 1), jnp.bfloat16)

    def shape(*sizes, dtype=jnp.bfloat16):
        return jax.ShapeDtypeStruct(sizes, dtype)

    cut = call(cut_kernel, [legendre], shape(pair_total, lat_rows, padded))
    legendre_here = lax.all_to_all(cut, names, split_axis=0, concat_axis=0, tiled=True)

    fourier = forward_sums(forward_table, grid_terms, lat_block)

    def partial_sums(sec, dtype):
        return call(
            functools.partial(degrees_kernel, places, sec, degrees),
            [pair_orders, legendre_here, fourier],
            shape(2, 2, depth, padded, columns, dtype=dtype),
            mib=24,
            scalars=1,
            cost=pl.CostEstimate(
                flops=4 * pair_total * rows * lat_rows * columns // places.sections,
                bytes_accessed=fourier.size * 2,
                transcendentals=0,
            ),
        )

    taken = places.move(partial_sums(1, jnp.bfloat16), sec=1)
    kept = partial_sums(0, jnp.float32)
    wide = shape(2, depth, padded, radial, dtype=jnp.float32)
    half = shape(2, depth, padded, radial)
    keep_a, send_a, keep_b, send_b = call(plane_kernel, [kept, taken], [wide, half, wide, half])
    take_a, take_b = places.move(send_a, x=1), places.move(send_b, y=1)
    wide = shape(depth, padded, radial, dtype=jnp.float32)
    half = shape(depth, padded, radial)
    keep_a, send_a, keep_b, send_b = call(
        cross_kernel, [keep_a, take_a, keep_b, take_b], [wide, half, wide, half]
    )
    take_a, take_b = places.move(send_a, y=1), places.move(send_b, x=1)
    lines = call(
        depth_kernel,
        [keep_a, take_a, keep_b, take_b],
        [shape(padded, columns, dtype=jnp.float32)] + [shape(padded, columns)] * (depth - 1),
    )
    parts = [lines[0]] + [places.move(lines[deep], deep=deep) for deep in range(1, depth)]

    radial_mode = np.arange(radial, dtype=np.float32) / np.float32(radial)
    damping = np.exp(-filter_strength * radial_mode**filter_power).astype(np.float32)
    new_state, field = call(
        functools.partial(solve_kernel, places),
        [pair_orders, *parts, state, kappa[None, :], jnp.asarray(damping)[None, :], right_op, left_op],
        [shape(1, rows, columns), shape(padded, columns)],
        scalars=1,
    )

    fields = [field] + [places.move(field, deep=deep) for deep in range(1, depth)]
    own_a, own_b = call(spread_kernel, fields, [half, half])
    take_a, take_b = places.move(own_a, x=1), places.move(own_b, y=1)
    both = shape(2, depth, padded, radial)
    own_a, own_b = call(join_kernel, [own_a, take_a, own_b, take_b], [both, both])
    far_a, far_b = places.move(own_a, y=1), places.move(own_b, x=1)
    here = [own_a, far_a, own_b, far_b]
    there = [places.move(part, sec=1) for part in (own_a, own_b)]
    there += [places.move(part, sec=1) for part in (far_a, far_b)]
    gathered = here + [there[0], there[2], there[1], there[3]]
    evolved = inverse_values(
        places, degrees, pair_orders, legendre_here, inverse_table, gathered, lat_rows, lat_block
    )
    return (evolved, new_state)


def on_device(*args):
    lat_rows = args[0].shape[0]
    rows = args[2].shape[1]
    sections, side_row, side_x = (lax.axis_size(name) for name in names)
    fits = args[2].shape[0] == 1 and lat_rows % 16 == 0 and rows <= 2 * lat_rows
    fits = fits and args[0].size * 4 <= 24 * 1024 * 1024
    fits = fits and sections == 2 and side_x == 2 and side_row in (2, 4, 8, 16)
    return on_device_compact(*args) if fits else on_device_wide(*args)


def solution(mesh):
    return jax.shard_map(
        on_device,
        mesh=mesh,
        in_specs=(
            P(("row", "col"), "sec", None),
            P(),
            P(("sec", "row", "col"), None, None),
            P(("sec", "row", "col"), None, None),
            P(),
            P(),
            P(),
        ),
        out_specs=(P(("row", "col"), "sec", None), P(("sec", "row", "col"), None, None)),
        check_vma=False,
    )
```

```python
import functools
import math

import jax
import jax.numpy as jnp
import numpy as np
from jax import lax
from jax.experimental import pallas as pl
from jax.experimental.pallas import tpu as pltpu
from jax.sharding import PartitionSpec as P

time_step = 0.5
filter_strength = 36.0
filter_power = 36.0


def slot_orders_of(pair_orders):
    order_total = 2 * pair_orders.shape[0]
    return jnp.stack([pair_orders, order_total - 1 - pair_orders], axis=1).reshape(order_total)


def fourier_table(orders, phi_start, phi_count, longitudes):
    longitude = phi_start + lax.iota(jnp.int32, phi_count)
    phase_turns = longitude[:, None] * orders[None, :] % longitudes
    phase_angle = phase_turns.astype(jnp.float32) * (2.0 * math.pi / longitudes)
    norm_scale = 1.0 / math.sqrt(longitudes)
    return jnp.stack(
        [jnp.cos(phase_angle) * norm_scale, -jnp.sin(phase_angle) * norm_scale], axis=-1
    )


def on_device_wide(grid_terms, pair_orders, legendre, state, kappa, right_op, left_op):
    lat_rows, phi_count, radial = grid_terms.shape
    pairs_here = legendre.shape[0]
    degrees = legendre.shape[1] - 1
    latitudes = legendre.shape[2]
    sections = lax.axis_size("sec")
    longitudes = phi_count * sections
    columns = 2 * radial
    section_slots = degrees // sections
    orders = slot_orders_of(pair_orders)
    sec_index = lax.axis_index("sec")
    highest = lax.Precision.HIGHEST
    phi_start = sec_index * phi_count
    sub_orders = orders
    phase_table = fourier_table(sub_orders, phi_start, phi_count, longitudes)
    term = jnp.einsum(
        "tpr,psc->stcr",
        grid_terms,
        phase_table,
        precision=highest,
        preferred_element_type=jnp.float32,
    )
    spectral = lax.psum_scatter(
        term.reshape(section_slots * lax.axis_size("sec"), lat_rows, columns),
        "sec",
        scatter_dimension=0,
        tiled=True,
    ).astype(jnp.bfloat16)
    device = lax.axis_index(("sec", "row", "col"))
    local_orders = lax.dynamic_slice_in_dim(pair_orders, device * pairs_here, pairs_here)
    row_index = lax.iota(jnp.int32, degrees + 1)
    leading = row_index[None, :] < (degrees - local_orders)[:, None]
    degree = jnp.where(leading, local_orders[:, None] + row_index[None, :], row_index[None, :] - 1)
    received = lax.all_to_all(spectral, ("row", "col"), split_axis=0, concat_axis=1, tiled=True)
    item_count = received.shape[2]
    paired = received.reshape(pairs_here, 2, latitudes, item_count)
    both_orders = jnp.einsum("pit,potx->piox", legendre, paired, preferred_element_type=jnp.float32)
    coefficient = jnp.where(leading[:, :, None], both_orders[:, :, 0], both_orders[:, :, 1])
    right_side = (state.astype(jnp.float32) + time_step * coefficient).astype(jnp.bfloat16)
    right_side = right_side.reshape(pairs_here, degrees + 1, 2, radial)
    eigen_part = jnp.einsum(
        "picr,rk->pick", right_side, right_op, preferred_element_type=jnp.float32
    )
    radial_mode = lax.iota(jnp.float32, radial) / radial
    damping = jnp.exp(-filter_strength * radial_mode**filter_power)
    degree_wide = degree.astype(jnp.float32)
    degree_term = degree_wide * (degree_wide + 1.0) / (degrees * degrees)
    factor = damping[None, None, :] / (1.0 + kappa[None, None, :] + degree_term[:, :, None])
    scaled = (eigen_part * factor[:, :, None, :]).astype(jnp.bfloat16)
    new_state = jnp.einsum("pick,kr->picr", scaled, left_op, preferred_element_type=jnp.float32)
    new_state = new_state.astype(jnp.bfloat16).reshape(pairs_here, degrees + 1, columns)
    zero_rows = jnp.zeros_like(new_state)
    split_state = jnp.stack(
        [
            jnp.where(leading[:, :, None], new_state, zero_rows),
            jnp.where(leading[:, :, None], zero_rows, new_state),
        ],
        axis=1,
    )
    synthesis_wide = jnp.einsum(
        "pit,poix->potx", legendre, split_state, preferred_element_type=jnp.float32
    )
    synthesis = synthesis_wide.astype(jnp.bfloat16).reshape(2 * pairs_here, latitudes, columns)
    returned = lax.all_to_all(synthesis, ("row", "col"), split_axis=1, concat_axis=0, tiled=True)
    sub_orders = lax.dynamic_slice_in_dim(orders, sec_index * section_slots, section_slots)
    phase_table = fourier_table(sub_orders, 0, longitudes, longitudes)
    values = returned.astype(jnp.float32).reshape(section_slots, lat_rows, 2, radial)
    partial_value = jnp.einsum(
        "stcr,psc->tpr", values, phase_table, precision=highest, preferred_element_type=jnp.float32
    )
    evolved = lax.psum_scatter(
        partial_value.astype(jnp.bfloat16), "sec", scatter_dimension=1, tiled=True
    ).astype(jnp.float32)
    return (evolved, new_state)


names = ("sec", "row", "col")


def natural_table(pair_total, sections, phi_count):
    slots = 2 * pair_total
    longitudes = sections * phi_count
    low = np.arange(pair_total)
    orders = np.stack([low, slots - 1 - low], axis=1).reshape(slots)
    turns = orders[:, None] * np.arange(longitudes)[None, :] % longitudes
    angle = turns * (2.0 * np.pi / longitudes)
    table = np.concatenate([np.cos(angle), -np.sin(angle)], axis=0) / np.sqrt(longitudes)
    return table.reshape(2 * slots, sections, phi_count).transpose(1, 0, 2).astype(np.float32)


def params(mib):
    return pltpu.CompilerParams(vmem_limit_bytes=mib * 1024 * 1024)


def vmem():
    return pl.BlockSpec(memory_space=pltpu.VMEM)


def smem():
    return pl.BlockSpec(memory_space=pltpu.SMEM)


def anywhere():
    return pl.BlockSpec(memory_space=pl.ANY)


def call(kernel, operands, out_shapes, mib=16, scalars=0, cost=None, scratch=()):
    single = not isinstance(out_shapes, (list, tuple))
    return pl.pallas_call(
        kernel,
        in_specs=[smem()] * scalars + [vmem()] * (len(operands) - scalars),
        out_specs=vmem() if single else [vmem()] * len(out_shapes),
        out_shape=out_shapes,
        scratch_shapes=scratch,
        compiler_params=params(mib),
        cost_estimate=cost,
    )(*operands)


class Places:
    def __init__(self):
        self.sections, side_row, self.side_x = (lax.axis_size(name) for name in names)
        self.side_y = 2 if side_row % 2 == 0 else 1
        self.depth = side_row // self.side_y
        self.sizes = (self.sections, self.depth, self.side_y, self.side_x)

    def row(self):
        return lax.axis_index("row")

    def pair(self, sec, deep, y, x):
        at_sec = lax.axis_index("sec") ^ sec
        at_row = lax.axis_index("row") ^ (deep * self.side_y + y)
        at_col = lax.axis_index("col") ^ x
        return (at_sec * (self.depth * self.side_y) + at_row) * self.side_x + at_col

    def move(self, array, sec=0, deep=0, y=0, x=0):
        shift = (sec, deep, y, x)
        pairs = []
        for source in np.ndindex(*self.sizes):
            target = tuple(at ^ by for at, by in zip(source, shift))
            pairs.append(
                (
                    int(np.ravel_multi_index(source, self.sizes)),
                    int(np.ravel_multi_index(target, self.sizes)),
                )
            )
        return lax.ppermute(array, names, pairs)


def cut_kernel(places, legendre_ref, *refs):
    outs, turned = refs[:-1], refs[-1]
    parts, lat_rows, rows = turned.shape
    plane = parts // len(outs)
    whole = jnp.pad(
        legendre_ref[0].astype(jnp.float32), ((0, rows - legendre_ref.shape[1]), (0, 0))
    ).T.astype(jnp.bfloat16)
    for at in range(parts):
        turned[at] = whole[at * lat_rows : (at + 1) * lat_rows]
    for deep, out in enumerate(outs):
        begin = (places.row() ^ (deep * places.side_y)) // places.side_y * plane
        out[...] = turned[pl.ds(begin, plane)]


def turn_kernel(places, *refs):
    takes, outs = refs[: places.depth], refs[places.depth :]
    own = places.row() % places.side_y * places.side_x + lax.axis_index("col")
    for at, out in enumerate(outs):
        for deep, take in enumerate(takes):
            out[deep] = take[own ^ at]


def stack_kernel(*refs):
    for at, take in enumerate(refs[:-1]):
        refs[-1][at] = take[...]


def forward_kernel(table_ref, grid_ref, out_ref, held):
    blocks, rows, lat_block, radial = held.shape
    slots = rows // 2
    table = table_ref[lax.axis_index("sec")]

    def one_block(block, carry):
        for at in range(0, lat_block, 2):
            lat = block * lat_block + at
            two = jnp.concatenate(
                [grid_ref[lat].astype(jnp.bfloat16), grid_ref[lat + 1].astype(jnp.bfloat16)], axis=1
            )
            sums = jnp.dot(table, two, preferred_element_type=jnp.float32)
            held[block, :, at, :] = sums[:, :radial]
            held[block, :, at + 1, :] = sums[:, radial:]
        return carry

    lax.fori_loop(0, blocks, one_block, 0)
    for block in range(0, blocks, 2):
        for part in range(2):
            rows_of = pl.ds(part * slots, slots)
            both = jnp.concatenate([held[block, rows_of], held[block + 1, rows_of]], axis=1)
            out_ref[:, pl.ds(block * lat_block, 2 * lat_block), pl.ds(part * radial, radial)] = (
                both.astype(jnp.bfloat16)
            )


def forward_sums(table, grid_terms, lat_block):
    sections, rows, phi_count = table.shape
    lat_rows, _, radial = grid_terms.shape
    blocks = lat_rows // lat_block
    return pl.pallas_call(
        forward_kernel,
        in_specs=[vmem(), vmem()],
        out_specs=vmem(),
        out_shape=jax.ShapeDtypeStruct((rows // 2, lat_rows, 2 * radial), jnp.bfloat16),
        scratch_shapes=[pltpu.VMEM((blocks, rows, lat_block, radial), jnp.float32)],
        compiler_params=params(8),
        cost_estimate=pl.CostEstimate(
            flops=2 * rows * phi_count * lat_rows * radial,
            bytes_accessed=4 * lat_rows * phi_count * radial,
            transcendentals=0,
        ),
    )(table, pltpu.with_memory_space_constraint(grid_terms, pltpu.VMEM))


def masked(weights, order, degrees):
    row_index = lax.broadcasted_iota(jnp.int32, weights.shape, 1)
    leading = row_index < degrees - order
    zero = jnp.zeros_like(weights)
    return jnp.where(leading, weights, zero), jnp.where(leading, zero, weights)


def degrees_kernel(places, sec, degrees, orders_ref, legendre_ref, fourier_ref, out_ref):
    side_x, side_y = places.side_x, places.side_y
    contract = (((0,), (0,)), ((), ()))
    for deep, y, x in np.ndindex(places.depth, side_y, side_x):
        pair = places.pair(sec, int(deep), int(y), int(x))
        order = orders_ref[pair]
        lower, upper = masked(legendre_ref[2 * y + x, deep], order, degrees)
        total = lax.dot_general(
            lower, fourier_ref[2 * order], contract, preferred_element_type=jnp.float32
        ) + lax.dot_general(
            upper, fourier_ref[2 * order + 1], contract, preferred_element_type=jnp.float32
        )
        out_ref[y, x, deep] = total.astype(out_ref.dtype)


def plane_kernel(kept_ref, taken_ref, keep_a, send_a, keep_b, send_b):
    radial = keep_a.shape[-1]
    for y in range(2):
        for x in range(2):
            total = kept_ref[y, x] + taken_ref[y, x].astype(jnp.float32)
            part_a, part_b = total[..., :radial], total[..., radial:]
            if x == 0:
                keep_a[y] = part_a
            else:
                send_a[y] = part_a.astype(jnp.bfloat16)
            if y == 0:
                keep_b[x] = part_b
            else:
                send_b[x] = part_b.astype(jnp.bfloat16)


def cross_kernel(keep_a, take_a, keep_b, take_b, keep_a2, send_a2, keep_b2, send_b2):
    keep_a2[...] = keep_a[0] + take_a[0].astype(jnp.float32)
    send_a2[...] = (keep_a[1] + take_a[1].astype(jnp.float32)).astype(jnp.bfloat16)
    keep_b2[...] = keep_b[0] + take_b[0].astype(jnp.float32)
    send_b2[...] = (keep_b[1] + take_b[1].astype(jnp.float32)).astype(jnp.bfloat16)


def depth_kernel(keep_a, take_a, keep_b, take_b, *outs):
    radial = keep_a.shape[-1]
    for deep, out in enumerate(outs):
        out[:, :radial] = (keep_a[deep] + take_a[deep].astype(jnp.float32)).astype(out.dtype)
        out[:, radial:] = (keep_b[deep] + take_b[deep].astype(jnp.float32)).astype(out.dtype)


def solve_kernel(places, orders_ref, *refs):
    takes = refs[: places.depth]
    state_ref, kappa_ref, damping_ref, right_ref, left_ref, sent_ref = refs[places.depth :]
    rows = state_ref.shape[1]
    radial = right_ref.shape[0]
    degrees = rows - 1
    order = orders_ref[places.pair(0, 0, 0, 0)]
    coefficient = takes[0][...].astype(jnp.float32)
    for other in takes[1:]:
        coefficient += other[...].astype(jnp.float32)
    right_side = state_ref[0].astype(jnp.float32) + time_step * coefficient[:rows]
    right_side = right_side.astype(jnp.bfloat16)
    row_index = lax.broadcasted_iota(jnp.int32, (rows, radial), 0)
    degree = jnp.where(row_index < degrees - order, order + row_index, row_index - 1)
    degree = degree.astype(jnp.float32)
    factor = damping_ref[...] / (
        1.0 + kappa_ref[...] + degree * (degree + 1.0) / (degrees * degrees)
    )
    sent_ref[...] = jnp.zeros_like(sent_ref)
    for part in range(2):
        columns = pl.ds(part * radial, radial)
        eigen = jnp.dot(
            right_side[:, part * radial : (part + 1) * radial],
            right_ref[...],
            preferred_element_type=jnp.float32,
        )
        scaled = (eigen * factor).astype(jnp.bfloat16)
        field = jnp.dot(scaled, left_ref[...], preferred_element_type=jnp.float32)
        field = field.astype(jnp.bfloat16)
        sent_ref[pl.ds(0, rows), columns] = field


def spread_kernel(*refs):
    fields, (out_a, out_b) = refs[:-2], refs[-2:]
    radial = out_a.shape[-1]
    for deep, field in enumerate(fields):
        out_a[deep] = field[:, :radial]
        out_b[deep] = field[:, radial:]


def join_kernel(own_a, take_a, own_b, take_b, out_a, out_b):
    out_a[0] = own_a[...]
    out_a[1] = take_a[...]
    out_b[0] = own_b[...]
    out_b[1] = take_b[...]


def inverse_kernel(places, degrees, orders_ref, here_ref, there_ref, table_ref, *refs):
    fields, (out_ref, buffer, held, sems) = refs[:-4], refs[-4:]
    blocks, slot_rows, lat_block, radial = held.shape
    slots = slot_rows // 2
    per_section = len(fields) // places.sections

    for sec in range(places.sections):
        own_a, far_a, own_b, far_b = fields[sec * per_section : (sec + 1) * per_section]
        for deep, y, x in np.ndindex(places.depth, places.side_y, places.side_x):
            deep, y, x = int(deep), int(y), int(x)
            pair = places.pair(sec, deep, y, x)
            order = orders_ref[pair]
            weights = masked((there_ref if sec else here_ref)[2 * y + x, deep], order, degrees)
            both = ((far_a if y else own_a)[x, deep], (far_b if x else own_b)[y, deep])
            field = jnp.concatenate(both, axis=1)
            for half in range(2):
                rebuilt = jnp.dot(weights[half], field, preferred_element_type=jnp.float32)
                for part in range(2):
                    held[:, part * slots + 2 * order + half] = rebuilt[
                        :, part * radial : (part + 1) * radial
                    ].reshape(blocks, lat_block, radial)

    table = table_ref[lax.axis_index("sec")]

    def chunk(at):
        return pltpu.make_async_copy(
            buffer.at[pl.ds(2 * at, 2)], out_ref.at[pl.ds(2 * at, 2)], sems.at[at]
        )

    def one_block(block, carry):
        for at in range(0, lat_block, 2):
            two = jnp.concatenate(
                [
                    held[block, :, at, :].astype(jnp.bfloat16),
                    held[block, :, at + 1, :].astype(jnp.bfloat16),
                ],
                axis=1,
            )
            values = jnp.dot(table, two, preferred_element_type=jnp.float32)
            lat = block * lat_block + at
            buffer[lat] = values[:, :radial]
            buffer[lat + 1] = values[:, radial:]
            chunk(lat // 2).start()
        return carry

    lax.fori_loop(0, blocks, one_block, 0)
    for at in range(sems.shape[0]):
        chunk(at).wait()


def inverse_values(places, degrees, pair_orders, legendre, table, fields, lat_rows, lat_block):
    _, phi_count, slot_rows = table.shape
    radial = fields[0].shape[-1]
    blocks = lat_rows // lat_block
    out = jax.ShapeDtypeStruct((lat_rows, phi_count, radial), jnp.float32)
    return pl.pallas_call(
        functools.partial(inverse_kernel, places, degrees),
        in_specs=[smem()] + [vmem()] * (1 + len(legendre) + len(fields)),
        out_specs=anywhere(),
        out_shape=out,
        scratch_shapes=[
            pltpu.VMEM(out.shape, jnp.float32),
            pltpu.VMEM((blocks, slot_rows, lat_block, radial), jnp.float32),
            pltpu.SemaphoreType.DMA((lat_rows // 2,)),
        ],
        compiler_params=params(36),
        cost_estimate=pl.CostEstimate(
            flops=2 * slot_rows * phi_count * lat_rows * radial,
            bytes_accessed=4 * lat_rows * phi_count * radial,
            transcendentals=0,
        ),
    )(pair_orders, *legendre, table, *fields)


def on_device_compact(grid_terms, pair_orders, legendre, state, kappa, right_op, left_op):
    lat_rows, phi_count, radial = grid_terms.shape
    rows = legendre.shape[1]
    degrees = rows - 1
    padded = -(-rows // 8) * 8
    columns = 2 * radial
    pair_total = pair_orders.shape[0]
    places = Places()
    depth = places.depth
    lat_block = 8
    table = natural_table(pair_total, places.sections, phi_count)
    forward_table = jnp.asarray(table, jnp.bfloat16)
    inverse_table = jnp.asarray(table.transpose(0, 2, 1), jnp.bfloat16)

    def shape(*sizes, dtype=jnp.bfloat16):
        return jax.ShapeDtypeStruct(sizes, dtype)

    part = shape(places.side_y * places.side_x, lat_rows, padded)
    cuts = call(
        functools.partial(cut_kernel, places),
        [legendre],
        [part] * depth,
        scratch=[pltpu.VMEM((depth * part.shape[0], lat_rows, padded), jnp.bfloat16)],
        cost=pl.CostEstimate(flops=int(1.3e10), bytes_accessed=0, transcendentals=0),
    )
    cuts = [cuts[0]] + [places.move(cuts[deep], deep=deep) for deep in range(1, depth)]
    part = shape(depth, lat_rows, padded)
    cuts = call(functools.partial(turn_kernel, places), cuts, [part] * 4)
    cuts = [cuts[0]] + [places.move(cuts[at], y=at // 2, x=at % 2) for at in range(1, 4)]
    legendre_here = call(stack_kernel, cuts, shape(4, depth, lat_rows, padded))
    legendre_there = places.move(legendre_here, sec=1)
    legendres = (legendre_here, legendre_there)

    fourier = forward_sums(forward_table, grid_terms, lat_block)

    def partial_sums(sec, dtype):
        return call(
            functools.partial(degrees_kernel, places, sec, degrees),
            [pair_orders, legendres[sec], fourier],
            shape(2, 2, depth, padded, columns, dtype=dtype),
            mib=24,
            scalars=1,
            cost=pl.CostEstimate(
                flops=4 * pair_total * rows * lat_rows * columns // places.sections,
                bytes_accessed=fourier.size * 2,
                transcendentals=0,
            ),
        )

    taken = places.move(partial_sums(1, jnp.bfloat16), sec=1)
    kept = partial_sums(0, jnp.float32)
    wide = shape(2, depth, padded, radial, dtype=jnp.float32)
    half = shape(2, depth, padded, radial)
    keep_a, send_a, keep_b, send_b = call(plane_kernel, [kept, taken], [wide, half, wide, half])
    take_a, take_b = places.move(send_a, x=1), places.move(send_b, y=1)
    wide = shape(depth, padded, radial, dtype=jnp.float32)
    half = shape(depth, padded, radial)
    keep_a, send_a, keep_b, send_b = call(
        cross_kernel, [keep_a, take_a, keep_b, take_b], [wide, half, wide, half]
    )
    take_a, take_b = places.move(send_a, y=1), places.move(send_b, x=1)
    lines = call(
        depth_kernel,
        [keep_a, take_a, keep_b, take_b],
        [shape(padded, columns, dtype=jnp.float32)] + [shape(padded, columns)] * (depth - 1),
    )
    parts = [lines[0]] + [places.move(lines[deep], deep=deep) for deep in range(1, depth)]

    radial_mode = np.arange(radial, dtype=np.float32) / np.float32(radial)
    damping = np.exp(-filter_strength * radial_mode**filter_power).astype(np.float32)
    field = call(
        functools.partial(solve_kernel, places),
        [pair_orders, *parts, state, kappa[None, :], jnp.asarray(damping)[None, :], right_op, left_op],
        shape(padded, columns),
        scalars=1,
    )
    new_state = field[None, :rows]

    fields = [field] + [places.move(field, deep=deep) for deep in range(1, depth)]
    own_a, own_b = call(spread_kernel, fields, [half, half])
    take_a, take_b = places.move(own_a, x=1), places.move(own_b, y=1)
    both = shape(2, depth, padded, radial)
    own_a, own_b = call(join_kernel, [own_a, take_a, own_b, take_b], [both, both])
    far_a, far_b = places.move(own_a, y=1), places.move(own_b, x=1)
    here = [own_a, far_a, own_b, far_b]
    there = [places.move(part, sec=1) for part in (own_a, own_b)]
    there += [places.move(part, sec=1) for part in (far_a, far_b)]
    gathered = here + [there[0], there[2], there[1], there[3]]
    evolved = inverse_values(
        places, degrees, pair_orders, legendres, inverse_table, gathered, lat_rows, lat_block
    )
    return (evolved, new_state)


def on_device(*args):
    lat_rows = args[0].shape[0]
    rows = args[2].shape[1]
    sections, side_row, side_x = (lax.axis_size(name) for name in names)
    fits = args[2].shape[0] == 1 and lat_rows % 16 == 0 and rows <= 2 * lat_rows
    fits = fits and args[0].size * 4 <= 24 * 1024 * 1024
    fits = fits and sections == 2 and side_x == 2 and side_row in (2, 4, 8, 16)
    return on_device_compact(*args) if fits else on_device_wide(*args)


def solution(mesh):
    return jax.shard_map(
        on_device,
        mesh=mesh,
        in_specs=(
            P(("row", "col"), "sec", None),
            P(),
            P(("sec", "row", "col"), None, None),
            P(("sec", "row", "col"), None, None),
            P(),
            P(),
            P(),
        ),
        out_specs=(P(("row", "col"), "sec", None), P(("sec", "row", "col"), None, None)),
        check_vma=False,
    )
```

```python
import functools
import math

import jax
import jax.numpy as jnp
import numpy as np
from jax import lax
from jax.experimental import pallas as pl
from jax.experimental.pallas import tpu as pltpu
from jax.sharding import PartitionSpec as P

time_step = 0.5
filter_strength = 36.0
filter_power = 36.0


def slot_orders_of(pair_orders):
    order_total = 2 * pair_orders.shape[0]
    return jnp.stack([pair_orders, order_total - 1 - pair_orders], axis=1).reshape(order_total)


def fourier_table(orders, phi_start, phi_count, longitudes):
    longitude = phi_start + lax.iota(jnp.int32, phi_count)
    phase_turns = longitude[:, None] * orders[None, :] % longitudes
    phase_angle = phase_turns.astype(jnp.float32) * (2.0 * math.pi / longitudes)
    norm_scale = 1.0 / math.sqrt(longitudes)
    return jnp.stack(
        [jnp.cos(phase_angle) * norm_scale, -jnp.sin(phase_angle) * norm_scale], axis=-1
    )


def on_device_wide(grid_terms, pair_orders, legendre, state, kappa, right_op, left_op):
    lat_rows, phi_count, radial = grid_terms.shape
    pairs_here = legendre.shape[0]
    degrees = legendre.shape[1] - 1
    latitudes = legendre.shape[2]
    sections = lax.axis_size("sec")
    longitudes = phi_count * sections
    columns = 2 * radial
    section_slots = degrees // sections
    orders = slot_orders_of(pair_orders)
    sec_index = lax.axis_index("sec")
    highest = lax.Precision.HIGHEST
    phi_start = sec_index * phi_count
    sub_orders = orders
    phase_table = fourier_table(sub_orders, phi_start, phi_count, longitudes)
    term = jnp.einsum(
        "tpr,psc->stcr",
        grid_terms,
        phase_table,
        precision=highest,
        preferred_element_type=jnp.float32,
    )
    spectral = lax.psum_scatter(
        term.reshape(section_slots * lax.axis_size("sec"), lat_rows, columns),
        "sec",
        scatter_dimension=0,
        tiled=True,
    ).astype(jnp.bfloat16)
    device = lax.axis_index(("sec", "row", "col"))
    local_orders = lax.dynamic_slice_in_dim(pair_orders, device * pairs_here, pairs_here)
    row_index = lax.iota(jnp.int32, degrees + 1)
    leading = row_index[None, :] < (degrees - local_orders)[:, None]
    degree = jnp.where(leading, local_orders[:, None] + row_index[None, :], row_index[None, :] - 1)
    received = lax.all_to_all(spectral, ("row", "col"), split_axis=0, concat_axis=1, tiled=True)
    item_count = received.shape[2]
    paired = received.reshape(pairs_here, 2, latitudes, item_count)
    both_orders = jnp.einsum("pit,potx->piox", legendre, paired, preferred_element_type=jnp.float32)
    coefficient = jnp.where(leading[:, :, None], both_orders[:, :, 0], both_orders[:, :, 1])
    right_side = (state.astype(jnp.float32) + time_step * coefficient).astype(jnp.bfloat16)
    right_side = right_side.reshape(pairs_here, degrees + 1, 2, radial)
    eigen_part = jnp.einsum(
        "picr,rk->pick", right_side, right_op, preferred_element_type=jnp.float32
    )
    radial_mode = lax.iota(jnp.float32, radial) / radial
    damping = jnp.exp(-filter_strength * radial_mode**filter_power)
    degree_wide = degree.astype(jnp.float32)
    degree_term = degree_wide * (degree_wide + 1.0) / (degrees * degrees)
    factor = damping[None, None, :] / (1.0 + kappa[None, None, :] + degree_term[:, :, None])
    scaled = (eigen_part * factor[:, :, None, :]).astype(jnp.bfloat16)
    new_state = jnp.einsum("pick,kr->picr", scaled, left_op, preferred_element_type=jnp.float32)
    new_state = new_state.astype(jnp.bfloat16).reshape(pairs_here, degrees + 1, columns)
    zero_rows = jnp.zeros_like(new_state)
    split_state = jnp.stack(
        [
            jnp.where(leading[:, :, None], new_state, zero_rows),
            jnp.where(leading[:, :, None], zero_rows, new_state),
        ],
        axis=1,
    )
    synthesis_wide = jnp.einsum(
        "pit,poix->potx", legendre, split_state, preferred_element_type=jnp.float32
    )
    synthesis = synthesis_wide.astype(jnp.bfloat16).reshape(2 * pairs_here, latitudes, columns)
    returned = lax.all_to_all(synthesis, ("row", "col"), split_axis=1, concat_axis=0, tiled=True)
    sub_orders = lax.dynamic_slice_in_dim(orders, sec_index * section_slots, section_slots)
    phase_table = fourier_table(sub_orders, 0, longitudes, longitudes)
    values = returned.astype(jnp.float32).reshape(section_slots, lat_rows, 2, radial)
    partial_value = jnp.einsum(
        "stcr,psc->tpr", values, phase_table, precision=highest, preferred_element_type=jnp.float32
    )
    evolved = lax.psum_scatter(
        partial_value.astype(jnp.bfloat16), "sec", scatter_dimension=1, tiled=True
    ).astype(jnp.float32)
    return (evolved, new_state)


names = ("sec", "row", "col")


def natural_table(pair_total, sections, phi_count):
    slots = 2 * pair_total
    longitudes = sections * phi_count
    low = np.arange(pair_total)
    orders = np.stack([low, slots - 1 - low], axis=1).reshape(slots)
    turns = orders[:, None] * np.arange(longitudes)[None, :] % longitudes
    angle = turns * (2.0 * np.pi / longitudes)
    table = np.concatenate([np.cos(angle), -np.sin(angle)], axis=0) / np.sqrt(longitudes)
    return table.reshape(2 * slots, sections, phi_count).transpose(1, 0, 2).astype(np.float32)


def params(mib):
    return pltpu.CompilerParams(vmem_limit_bytes=mib * 1024 * 1024)


def vmem():
    return pl.BlockSpec(memory_space=pltpu.VMEM)


def smem():
    return pl.BlockSpec(memory_space=pltpu.SMEM)


def anywhere():
    return pl.BlockSpec(memory_space=pl.ANY)


def call(kernel, operands, out_shapes, mib=16, scalars=0, cost=None, scratch=()):
    single = not isinstance(out_shapes, (list, tuple))
    return pl.pallas_call(
        kernel,
        in_specs=[smem()] * scalars + [vmem()] * (len(operands) - scalars),
        out_specs=vmem() if single else [vmem()] * len(out_shapes),
        out_shape=out_shapes,
        scratch_shapes=scratch,
        compiler_params=params(mib),
        cost_estimate=cost,
    )(*operands)


def routes(sec, u, v, a, b):
    return (a + 2 * b, v, u) if sec == 0 else (2 * a + b, u, v)


relative = tuple(np.ndindex(2, 2, 2, 2))


def place(sec, u, v, a, b):
    at_sec = lax.axis_index("sec") ^ sec
    options = []
    for core in range(2):
        z, y, x = routes(core, u, v, a, b)
        options.append((z * 2 + y, x))
    row = lax.axis_index("row") ^ jnp.where(at_sec == 0, options[0][0], options[1][0])
    col = lax.axis_index("col") ^ jnp.where(at_sec == 0, options[0][1], options[1][1])
    return at_sec, row, col


def pair_at(sec, where):
    at_sec, row, col = place(sec, *where)
    return (at_sec * lax.axis_size("row") + row) * lax.axis_size("col") + col


def exchange(array, axis):
    sizes = tuple(lax.axis_size(name) for name in names)
    pairs = []
    for source in np.ndindex(*sizes):
        sec, row, col = source
        if axis == "sec":
            target = (sec ^ 1, row, col)
        else:
            z, y, x = routes(sec, *(int(axis == name) for name in "uvab"))
            target = (sec, row ^ (z * 2 + y), col ^ x)
        pairs.append(
            (int(np.ravel_multi_index(source, sizes)), int(np.ravel_multi_index(target, sizes)))
        )
    return lax.ppermute(array, names, pairs)


def cut_kernel(legendre_ref, keep_ref, send_ref, turned):
    parts, lat_rows, rows = turned.shape
    whole = jnp.pad(
        legendre_ref[0].astype(jnp.float32), ((0, rows - legendre_ref.shape[1]), (0, 0))
    ).T.astype(jnp.bfloat16)
    for at in range(parts):
        turned[at] = whole[at * lat_rows : (at + 1) * lat_rows]
    for where in relative:
        _, row, col = place(0, *where)
        (send_ref if where[0] else keep_ref)[where[1:]] = turned[row * lax.axis_size("col") + col]


def pass_kernel(keep_ref, take_ref, keep_out, send_out):
    for i, j in np.ndindex(2, 2):
        for source, ref in enumerate((keep_ref, take_ref)):
            keep_out[i, j, source] = ref[0, i, j]
            send_out[i, j, source] = ref[1, i, j]


def stack_kernel(keep_ref, take_ref, out_ref):
    out_ref[0] = keep_ref[...]
    out_ref[1] = take_ref[...]


def forward_kernel(table_ref, grid_ref, out_ref, held):
    blocks, rows, lat_block, radial = held.shape
    slots = rows // 2
    table = table_ref[lax.axis_index("sec")]

    def one_block(block, carry):
        for at in range(0, lat_block, 2):
            lat = block * lat_block + at
            two = jnp.concatenate(
                [grid_ref[lat].astype(jnp.bfloat16), grid_ref[lat + 1].astype(jnp.bfloat16)], axis=1
            )
            sums = jnp.dot(table, two, preferred_element_type=jnp.float32)
            held[block, :, at, :] = sums[:, :radial]
            held[block, :, at + 1, :] = sums[:, radial:]
        return carry

    lax.fori_loop(0, blocks, one_block, 0)
    for block in range(0, blocks, 2):
        for part in range(2):
            rows_of = pl.ds(part * slots, slots)
            both = jnp.concatenate([held[block, rows_of], held[block + 1, rows_of]], axis=1)
            out_ref[:, pl.ds(block * lat_block, 2 * lat_block), pl.ds(part * radial, radial)] = (
                both.astype(jnp.bfloat16)
            )


def forward_sums(table, grid_terms, lat_block):
    sections, rows, phi_count = table.shape
    lat_rows, _, radial = grid_terms.shape
    blocks = lat_rows // lat_block
    return pl.pallas_call(
        forward_kernel,
        in_specs=[vmem(), vmem()],
        out_specs=vmem(),
        out_shape=jax.ShapeDtypeStruct((rows // 2, lat_rows, 2 * radial), jnp.bfloat16),
        scratch_shapes=[pltpu.VMEM((blocks, rows, lat_block, radial), jnp.float32)],
        compiler_params=params(8),
        cost_estimate=pl.CostEstimate(
            flops=2 * rows * phi_count * lat_rows * radial,
            bytes_accessed=4 * lat_rows * phi_count * radial,
            transcendentals=0,
        ),
    )(table, pltpu.with_memory_space_constraint(grid_terms, pltpu.VMEM))


def masked(weights, order, degrees):
    row_index = lax.broadcasted_iota(jnp.int32, weights.shape, 1)
    leading = row_index < degrees - order
    zero = jnp.zeros_like(weights)
    return jnp.where(leading, weights, zero), jnp.where(leading, zero, weights)


def degrees_kernel(sec, degrees, orders_ref, legendre_ref, fourier_ref, out_ref):
    contract = (((0,), (0,)), ((), ()))
    for where in relative:
        order = orders_ref[pair_at(sec, where)]
        lower, upper = masked(legendre_ref[where[3:] + where[:3]], order, degrees)
        total = lax.dot_general(
            lower, fourier_ref[2 * order], contract, preferred_element_type=jnp.float32
        ) + lax.dot_general(
            upper, fourier_ref[2 * order + 1], contract, preferred_element_type=jnp.float32
        )
        out_ref[where] = total.astype(out_ref.dtype)


def halve_kernel(keep_ref, take_ref, keep_out, send_out):
    keep_out[...] = keep_ref[0] + take_ref[0].astype(jnp.float32)
    send_out[...] = (keep_ref[1] + take_ref[1].astype(jnp.float32)).astype(jnp.bfloat16)


def solve_kernel(
    orders_ref, keep_ref, take_ref, state_ref, kappa_ref, damping_ref, right_ref, left_ref, sent_ref
):
    rows = state_ref.shape[1]
    radial = right_ref.shape[0]
    degrees = rows - 1
    order = orders_ref[pair_at(0, (0, 0, 0, 0))]
    coefficient = keep_ref[...] + take_ref[...].astype(jnp.float32)
    right_side = state_ref[0].astype(jnp.float32) + time_step * coefficient[:rows]
    right_side = right_side.astype(jnp.bfloat16)
    row_index = lax.broadcasted_iota(jnp.int32, (rows, radial), 0)
    degree = jnp.where(row_index < degrees - order, order + row_index, row_index - 1)
    degree = degree.astype(jnp.float32)
    factor = damping_ref[...] / (
        1.0 + kappa_ref[...] + degree * (degree + 1.0) / (degrees * degrees)
    )
    sent_ref[...] = jnp.zeros_like(sent_ref)
    for part in range(2):
        columns = pl.ds(part * radial, radial)
        eigen = jnp.dot(
            right_side[:, part * radial : (part + 1) * radial],
            right_ref[...],
            preferred_element_type=jnp.float32,
        )
        scaled = (eigen * factor).astype(jnp.bfloat16)
        field = jnp.dot(scaled, left_ref[...], preferred_element_type=jnp.float32)
        field = field.astype(jnp.bfloat16)
        sent_ref[pl.ds(0, rows), columns] = field


def inverse_kernel(degrees, orders_ref, here_ref, there_ref, table_ref, *refs):
    fields, (out_ref, buffer, held, sems) = refs[:-4], refs[-4:]
    blocks, slot_rows, lat_block, radial = held.shape
    slots = slot_rows // 2
    for sec in range(2):
        for where in relative:
            order = orders_ref[pair_at(sec, where)]
            weights = masked((there_ref if sec else here_ref)[where[3:] + where[:3]], order, degrees)
            field = fields[2 * sec + where[0]][where[1:]]
            for half in range(2):
                rebuilt = jnp.dot(weights[half], field, preferred_element_type=jnp.float32)
                for part in range(2):
                    held[:, part * slots + 2 * order + half] = rebuilt[
                        :, part * radial : (part + 1) * radial
                    ].reshape(blocks, lat_block, radial)

    table = table_ref[lax.axis_index("sec")]

    def chunk(at):
        return pltpu.make_async_copy(
            buffer.at[pl.ds(2 * at, 2)], out_ref.at[pl.ds(2 * at, 2)], sems.at[at]
        )

    def one_block(block, carry):
        for at in range(0, lat_block, 2):
            two = jnp.concatenate(
                [
                    held[block, :, at, :].astype(jnp.bfloat16),
                    held[block, :, at + 1, :].astype(jnp.bfloat16),
                ],
                axis=1,
            )
            values = jnp.dot(table, two, preferred_element_type=jnp.float32)
            lat = block * lat_block + at
            buffer[lat] = values[:, :radial]
            buffer[lat + 1] = values[:, radial:]
            chunk(lat // 2).start()
        return carry

    lax.fori_loop(0, blocks, one_block, 0)
    for at in range(sems.shape[0]):
        chunk(at).wait()


def inverse_values(degrees, pair_orders, legendre, table, fields, lat_rows, lat_block):
    _, phi_count, slot_rows = table.shape
    radial = fields[0].shape[-1] // 2
    blocks = lat_rows // lat_block
    out = jax.ShapeDtypeStruct((lat_rows, phi_count, radial), jnp.float32)
    return pl.pallas_call(
        functools.partial(inverse_kernel, degrees),
        in_specs=[smem()] + [vmem()] * (1 + len(legendre) + len(fields)),
        out_specs=anywhere(),
        out_shape=out,
        scratch_shapes=[
            pltpu.VMEM(out.shape, jnp.float32),
            pltpu.VMEM((blocks, slot_rows, lat_block, radial), jnp.float32),
            pltpu.SemaphoreType.DMA((lat_rows // 2,)),
        ],
        compiler_params=params(36),
        cost_estimate=pl.CostEstimate(
            flops=2 * slot_rows * phi_count * lat_rows * radial,
            bytes_accessed=4 * lat_rows * phi_count * radial,
            transcendentals=0,
        ),
    )(pair_orders, *legendre, table, *fields)


def on_device_compact(grid_terms, pair_orders, legendre, state, kappa, right_op, left_op):
    lat_rows, phi_count, radial = grid_terms.shape
    rows = legendre.shape[1]
    degrees = rows - 1
    padded = -(-rows // 8) * 8
    columns = 2 * radial
    pair_total = pair_orders.shape[0]
    lat_block = 8
    table = natural_table(pair_total, lax.axis_size("sec"), phi_count)
    forward_table = jnp.asarray(table, jnp.bfloat16)
    inverse_table = jnp.asarray(table.transpose(0, 2, 1), jnp.bfloat16)

    def shape(*sizes, dtype=jnp.bfloat16):
        return jax.ShapeDtypeStruct(sizes, dtype)

    part = shape(2, 2, 2, lat_rows, padded)
    keep, send = call(
        cut_kernel,
        [legendre],
        [part, part],
        scratch=[pltpu.VMEM((2 * part.shape[0] * 4, lat_rows, padded), jnp.bfloat16)],
        cost=pl.CostEstimate(flops=int(1.3e10), bytes_accessed=0, transcendentals=0),
    )
    for axis in "uva":
        keep, send = call(pass_kernel, [keep, exchange(send, axis)], [part, part])
    here = call(stack_kernel, [keep, exchange(send, "b")], shape(2, 2, 2, 2, lat_rows, padded))
    legendres = (here, exchange(here, "sec"))

    fourier = forward_sums(forward_table, grid_terms, lat_block)

    def partial_sums(sec, dtype):
        return call(
            functools.partial(degrees_kernel, sec, degrees),
            [pair_orders, legendres[sec], fourier],
            shape(2, 2, 2, 2, padded, columns, dtype=dtype),
            mib=24,
            scalars=1,
            cost=pl.CostEstimate(
                flops=2 * pair_total * rows * lat_rows * columns,
                bytes_accessed=fourier.size * 2,
                transcendentals=0,
            ),
        )

    take = exchange(partial_sums(1, jnp.bfloat16), "sec")
    keep = partial_sums(0, jnp.float32)
    rest = (2, 2, 2, padded, columns)
    for axis in "uvab":
        keep, send = call(
            halve_kernel, [keep, take], [shape(*rest, dtype=jnp.float32), shape(*rest)]
        )
        take = exchange(send, axis)
        rest = rest[1:]

    radial_mode = np.arange(radial, dtype=np.float32) / np.float32(radial)
    damping = np.exp(-filter_strength * radial_mode**filter_power).astype(np.float32)
    field = call(
        solve_kernel,
        [pair_orders, keep, take, state, kappa[None, :], jnp.asarray(damping)[None, :], right_op, left_op],
        shape(padded, columns),
        scalars=1,
    )
    new_state = field[None, :rows]

    for axis in "bav":
        field = call(stack_kernel, [field, exchange(field, axis)], shape(2, *field.shape))
    far = exchange(field, "u")
    fields = (field, far, exchange(field, "sec"), exchange(far, "sec"))
    evolved = inverse_values(
        degrees, pair_orders, legendres, inverse_table, fields, lat_rows, lat_block
    )
    return (evolved, new_state)


def on_device(*args):
    lat_rows = args[0].shape[0]
    rows = args[2].shape[1]
    sections, side_row, side_x = (lax.axis_size(name) for name in names)
    fits = args[2].shape[0] == 1 and lat_rows % 16 == 0 and rows <= 2 * lat_rows
    fits = fits and args[0].size * 4 <= 24 * 1024 * 1024
    fits = fits and (sections, side_row, side_x) == (2, 8, 2)
    return on_device_compact(*args) if fits else on_device_wide(*args)


def solution(mesh):
    return jax.shard_map(
        on_device,
        mesh=mesh,
        in_specs=(
            P(("row", "col"), "sec", None),
            P(),
            P(("sec", "row", "col"), None, None),
            P(("sec", "row", "col"), None, None),
            P(),
            P(),
            P(),
        ),
        out_specs=(P(("row", "col"), "sec", None), P(("sec", "row", "col"), None, None)),
        check_vma=False,
    )
```

```python
import functools
import math

import jax
import jax.numpy as jnp
import numpy as np
from jax import lax
from jax.experimental import pallas as pl
from jax.experimental.pallas import tpu as pltpu
from jax.sharding import PartitionSpec as P

time_step = 0.5
filter_strength = 36.0
filter_power = 36.0


def slot_orders_of(pair_orders):
    order_total = 2 * pair_orders.shape[0]
    return jnp.stack([pair_orders, order_total - 1 - pair_orders], axis=1).reshape(order_total)


def fourier_table(orders, phi_start, phi_count, longitudes):
    longitude = phi_start + lax.iota(jnp.int32, phi_count)
    phase_turns = longitude[:, None] * orders[None, :] % longitudes
    phase_angle = phase_turns.astype(jnp.float32) * (2.0 * math.pi / longitudes)
    norm_scale = 1.0 / math.sqrt(longitudes)
    return jnp.stack(
        [jnp.cos(phase_angle) * norm_scale, -jnp.sin(phase_angle) * norm_scale], axis=-1
    )


def on_device_wide(grid_terms, pair_orders, legendre, state, kappa, right_op, left_op):
    lat_rows, phi_count, radial = grid_terms.shape
    pairs_here = legendre.shape[0]
    degrees = legendre.shape[1] - 1
    latitudes = legendre.shape[2]
    sections = lax.axis_size("sec")
    longitudes = phi_count * sections
    columns = 2 * radial
    section_slots = degrees // sections
    orders = slot_orders_of(pair_orders)
    sec_index = lax.axis_index("sec")
    highest = lax.Precision.HIGHEST
    phi_start = sec_index * phi_count
    sub_orders = orders
    phase_table = fourier_table(sub_orders, phi_start, phi_count, longitudes)
    term = jnp.einsum(
        "tpr,psc->stcr",
        grid_terms,
        phase_table,
        precision=highest,
        preferred_element_type=jnp.float32,
    )
    spectral = lax.psum_scatter(
        term.reshape(section_slots * lax.axis_size("sec"), lat_rows, columns),
        "sec",
        scatter_dimension=0,
        tiled=True,
    ).astype(jnp.bfloat16)
    device = lax.axis_index(("sec", "row", "col"))
    local_orders = lax.dynamic_slice_in_dim(pair_orders, device * pairs_here, pairs_here)
    row_index = lax.iota(jnp.int32, degrees + 1)
    leading = row_index[None, :] < (degrees - local_orders)[:, None]
    degree = jnp.where(leading, local_orders[:, None] + row_index[None, :], row_index[None, :] - 1)
    received = lax.all_to_all(spectral, ("row", "col"), split_axis=0, concat_axis=1, tiled=True)
    item_count = received.shape[2]
    paired = received.reshape(pairs_here, 2, latitudes, item_count)
    both_orders = jnp.einsum("pit,potx->piox", legendre, paired, preferred_element_type=jnp.float32)
    coefficient = jnp.where(leading[:, :, None], both_orders[:, :, 0], both_orders[:, :, 1])
    right_side = (state.astype(jnp.float32) + time_step * coefficient).astype(jnp.bfloat16)
    right_side = right_side.reshape(pairs_here, degrees + 1, 2, radial)
    eigen_part = jnp.einsum(
        "picr,rk->pick", right_side, right_op, preferred_element_type=jnp.float32
    )
    radial_mode = lax.iota(jnp.float32, radial) / radial
    damping = jnp.exp(-filter_strength * radial_mode**filter_power)
    degree_wide = degree.astype(jnp.float32)
    degree_term = degree_wide * (degree_wide + 1.0) / (degrees * degrees)
    factor = damping[None, None, :] / (1.0 + kappa[None, None, :] + degree_term[:, :, None])
    scaled = (eigen_part * factor[:, :, None, :]).astype(jnp.bfloat16)
    new_state = jnp.einsum("pick,kr->picr", scaled, left_op, preferred_element_type=jnp.float32)
    new_state = new_state.astype(jnp.bfloat16).reshape(pairs_here, degrees + 1, columns)
    zero_rows = jnp.zeros_like(new_state)
    split_state = jnp.stack(
        [
            jnp.where(leading[:, :, None], new_state, zero_rows),
            jnp.where(leading[:, :, None], zero_rows, new_state),
        ],
        axis=1,
    )
    synthesis_wide = jnp.einsum(
        "pit,poix->potx", legendre, split_state, preferred_element_type=jnp.float32
    )
    synthesis = synthesis_wide.astype(jnp.bfloat16).reshape(2 * pairs_here, latitudes, columns)
    returned = lax.all_to_all(synthesis, ("row", "col"), split_axis=1, concat_axis=0, tiled=True)
    sub_orders = lax.dynamic_slice_in_dim(orders, sec_index * section_slots, section_slots)
    phase_table = fourier_table(sub_orders, 0, longitudes, longitudes)
    values = returned.astype(jnp.float32).reshape(section_slots, lat_rows, 2, radial)
    partial_value = jnp.einsum(
        "stcr,psc->tpr", values, phase_table, precision=highest, preferred_element_type=jnp.float32
    )
    evolved = lax.psum_scatter(
        partial_value.astype(jnp.bfloat16), "sec", scatter_dimension=1, tiled=True
    ).astype(jnp.float32)
    return (evolved, new_state)


names = ("sec", "row", "col")


def natural_table(pair_total, sections, phi_count):
    slots = 2 * pair_total
    longitudes = sections * phi_count
    low = np.arange(pair_total)
    orders = np.stack([low, slots - 1 - low], axis=1).reshape(slots)
    turns = orders[:, None] * np.arange(longitudes)[None, :] % longitudes
    angle = turns * (2.0 * np.pi / longitudes)
    table = np.concatenate([np.cos(angle), -np.sin(angle)], axis=0) / np.sqrt(longitudes)
    return table.reshape(2 * slots, sections, phi_count).transpose(1, 0, 2).astype(np.float32)


def params(mib):
    return pltpu.CompilerParams(vmem_limit_bytes=mib * 1024 * 1024)


def vmem():
    return pl.BlockSpec(memory_space=pltpu.VMEM)


def smem():
    return pl.BlockSpec(memory_space=pltpu.SMEM)


def anywhere():
    return pl.BlockSpec(memory_space=pl.ANY)


def call(kernel, operands, out_shapes, mib=16, scalars=0, cost=None, scratch=()):
    single = not isinstance(out_shapes, (list, tuple))
    return pl.pallas_call(
        kernel,
        in_specs=[smem()] * scalars + [vmem()] * (len(operands) - scalars),
        out_specs=vmem() if single else [vmem()] * len(out_shapes),
        out_shape=out_shapes,
        scratch_shapes=scratch,
        compiler_params=params(mib),
        cost_estimate=cost,
    )(*operands)


four = range(4)


def plane_index():
    return lax.axis_index("row") % 2 * 2 + lax.axis_index("col")


def depth_index():
    return lax.axis_index("row") // 2


def pair_at(sec, deep, flat):
    row = lax.axis_index("row") ^ (2 * deep + flat // 2)
    col = lax.axis_index("col") ^ (flat % 2)
    at_sec = lax.axis_index("sec") ^ sec
    return (at_sec * lax.axis_size("row") + row) * lax.axis_size("col") + col


def exchange(array, sec=0, deep=0, flat=0):
    sizes = tuple(lax.axis_size(name) for name in names)
    pairs = []
    for source in np.ndindex(*sizes):
        target = (source[0] ^ sec, source[1] ^ (2 * deep + flat // 2), source[2] ^ (flat % 2))
        pairs.append(
            (int(np.ravel_multi_index(source, sizes)), int(np.ravel_multi_index(target, sizes)))
        )
    return lax.ppermute(array, names, pairs)


def cut_kernel(legendre_ref, *refs):
    outs, slabs = refs[:-1], refs[-1]
    count, rows, lats = slabs.shape
    given = legendre_ref.shape[1]
    slabs[...] = jnp.zeros_like(slabs)
    for at in range(count):
        slabs[at, :given] = legendre_ref[0, :, at * lats : (at + 1) * lats]
    for deep, out in enumerate(outs):
        out[...] = slabs[depth_index() ^ deep]


def forward_kernel(
    orders_ref, table_ref, grid_ref, keep_ref, send_ref, table, buffer, held, sems, table_sem
):
    blocks, rows, lat_block, radial = held.shape
    slots = rows // 2

    def chunk(at):
        return pltpu.make_async_copy(
            grid_ref.at[pl.ds(2 * at, 2)], buffer.at[pl.ds(2 * at, 2)], sems.at[at]
        )

    first = pltpu.make_async_copy(table_ref.at[lax.axis_index("sec")], table, table_sem)
    first.start()
    for at in range(sems.shape[0]):
        chunk(at).start()
    first.wait()

    def one_block(block, carry):
        for at in range(0, lat_block, 2):
            lat = block * lat_block + at
            chunk(lat // 2).wait()
            two = jnp.concatenate(
                [buffer[lat].astype(jnp.bfloat16), buffer[lat + 1].astype(jnp.bfloat16)], axis=1
            )
            sums = jnp.dot(table[...], two, preferred_element_type=jnp.float32)
            held[block, :, at, :] = sums[:, :radial]
            held[block, :, at + 1, :] = sums[:, radial:]
        return carry

    lax.fori_loop(0, blocks, one_block, 0)
    for sec, out in ((1, send_ref), (0, keep_ref)):
        for flat, deep in np.ndindex(4, 4):
            order = orders_ref[pair_at(sec, deep, flat)]
            for half, part in np.ndindex(2, 2):
                values = held[:, part * slots + 2 * order + half]
                out[flat, deep, half, :, pl.ds(part * radial, radial)] = values.reshape(
                    blocks * lat_block, radial
                ).astype(out.dtype)


def forward_sums(pair_orders, table, grid_terms, lat_block):
    sections, rows, phi_count = table.shape
    lat_rows, _, radial = grid_terms.shape
    blocks = lat_rows // lat_block
    sizes = (4, 4, 2, lat_rows, 2 * radial)
    in_memory = pl.BlockSpec(memory_space=pltpu.HBM)
    return pl.pallas_call(
        forward_kernel,
        in_specs=[smem(), in_memory, in_memory],
        out_specs=[vmem(), vmem()],
        out_shape=[
            jax.ShapeDtypeStruct(sizes, jnp.float32),
            jax.ShapeDtypeStruct(sizes, jnp.bfloat16),
        ],
        scratch_shapes=[
            pltpu.VMEM((rows, phi_count), table.dtype),
            pltpu.VMEM(grid_terms.shape, jnp.float32),
            pltpu.VMEM((blocks, rows, lat_block, radial), jnp.float32),
            pltpu.SemaphoreType.DMA((lat_rows // 2,)),
            pltpu.SemaphoreType.DMA,
        ],
        compiler_params=params(36),
        cost_estimate=pl.CostEstimate(
            flops=2 * rows * phi_count * lat_rows * radial,
            bytes_accessed=4 * lat_rows * phi_count * radial,
            transcendentals=0,
        ),
    )(pair_orders, table, grid_terms)


def add_kernel(keep_ref, take_ref, *outs):
    for flat, out in enumerate(outs):
        out[...] = (keep_ref[flat] + take_ref[flat].astype(jnp.float32)).astype(out.dtype)


def masked(weights, order, degrees):
    row_index = lax.broadcasted_iota(jnp.int32, weights.shape, 0)
    leading = row_index < degrees - order
    zero = jnp.zeros_like(weights)
    return jnp.where(leading, weights, zero), jnp.where(leading, zero, weights)


def degrees_kernel(degrees, orders_ref, *refs):
    weights, takes, outs, gathered = refs[:4], refs[4:8], refs[8:12], refs[12]
    _, _, _, lat_rows, columns = gathered.shape
    own = plane_index()
    for flat in four:
        for deep, half in np.ndindex(4, 2):
            gathered[deep, half, own ^ flat] = takes[flat][deep, half]
    for deep in four:
        chosen = masked(weights[deep][...], orders_ref[pair_at(0, deep, 0)], degrees)
        total = 0.0
        for half in range(2):
            total += jnp.dot(
                chosen[half],
                gathered[deep, half].reshape(4 * lat_rows, columns),
                preferred_element_type=jnp.float32,
            )
        outs[deep][...] = total.astype(outs[deep].dtype)


def synthesis_kernel(degrees, orders_ref, *refs):
    weights, fields, outs, spread = refs[:4], refs[4:8], refs[8:12], refs[12]
    _, _, _, lat_rows, columns = spread.shape
    contract = (((0,), (0,)), ((), ()))
    own = plane_index()
    for deep in four:
        chosen = masked(weights[deep][...], orders_ref[pair_at(0, deep, 0)], degrees)
        for half in range(2):
            values = lax.dot_general(
                chosen[half], fields[deep][...], contract, preferred_element_type=jnp.float32
            )
            spread[deep, half] = values.astype(spread.dtype).reshape(4, lat_rows, columns)
    for flat in (3, 1, 2, 0):
        for deep, half in np.ndindex(4, 2):
            outs[flat][deep, half] = spread[deep, half, own ^ flat]


def solve_kernel(
    orders_ref, one, two, three, last, state_ref, kappa_ref, damping_ref, right_ref, left_ref, sent_ref
):
    rows = state_ref.shape[1]
    radial = right_ref.shape[0]
    degrees = rows - 1
    order = orders_ref[pair_at(0, 0, 0)]
    coefficient = one[...]
    for other in (two, three, last):
        coefficient += other[...].astype(jnp.float32)
    right_side = state_ref[0].astype(jnp.float32) + time_step * coefficient[:rows]
    right_side = right_side.astype(jnp.bfloat16)
    row_index = lax.broadcasted_iota(jnp.int32, (rows, radial), 0)
    degree = jnp.where(row_index < degrees - order, order + row_index, row_index - 1)
    degree = degree.astype(jnp.float32)
    factor = damping_ref[...] / (
        1.0 + kappa_ref[...] + degree * (degree + 1.0) / (degrees * degrees)
    )
    sent_ref[...] = jnp.zeros_like(sent_ref)
    for part in range(2):
        columns = pl.ds(part * radial, radial)
        eigen = jnp.dot(
            right_side[:, part * radial : (part + 1) * radial],
            right_ref[...],
            preferred_element_type=jnp.float32,
        )
        scaled = (eigen * factor).astype(jnp.bfloat16)
        field = jnp.dot(scaled, left_ref[...], preferred_element_type=jnp.float32)
        field = field.astype(jnp.bfloat16)
        sent_ref[pl.ds(0, rows), columns] = field


def inverse_kernel(orders_ref, table_ref, *refs):
    takes, (out_ref, buffer, held, sems) = refs[:-4], refs[-4:]
    blocks, slot_rows, lat_block, radial = held.shape
    slots = slot_rows // 2

    for sec, flat, deep in np.ndindex(2, 4, 4):
        order = orders_ref[pair_at(sec, deep, flat)]
        for half, part in np.ndindex(2, 2):
            values = takes[4 * sec + flat][deep, half, :, pl.ds(part * radial, radial)]
            held[:, part * slots + 2 * order + half] = values.astype(jnp.float32).reshape(
                blocks, lat_block, radial
            )

    table = table_ref[lax.axis_index("sec")]

    def chunk(at):
        return pltpu.make_async_copy(
            buffer.at[pl.ds(2 * at, 2)], out_ref.at[pl.ds(2 * at, 2)], sems.at[at]
        )

    def one_block(block, carry):
        for at in range(0, lat_block, 2):
            two = jnp.concatenate(
                [
                    held[block, :, at, :].astype(jnp.bfloat16),
                    held[block, :, at + 1, :].astype(jnp.bfloat16),
                ],
                axis=1,
            )
            values = jnp.dot(table, two, preferred_element_type=jnp.float32)
            lat = block * lat_block + at
            buffer[lat] = values[:, :radial]
            buffer[lat + 1] = values[:, radial:]
            chunk(lat // 2).start()
        return carry

    lax.fori_loop(0, blocks, one_block, 0)
    for at in range(sems.shape[0]):
        chunk(at).wait()


def inverse_values(pair_orders, table, takes, lat_block):
    _, phi_count, slot_rows = table.shape
    lat_rows, radial = takes[0].shape[2], takes[0].shape[3] // 2
    blocks = lat_rows // lat_block
    out = jax.ShapeDtypeStruct((lat_rows, phi_count, radial), jnp.float32)
    return pl.pallas_call(
        inverse_kernel,
        in_specs=[smem()] + [vmem()] * (1 + len(takes)),
        out_specs=anywhere(),
        out_shape=out,
        scratch_shapes=[
            pltpu.VMEM(out.shape, jnp.float32),
            pltpu.VMEM((blocks, slot_rows, lat_block, radial), jnp.float32),
            pltpu.SemaphoreType.DMA((lat_rows // 2,)),
        ],
        compiler_params=params(36),
        cost_estimate=pl.CostEstimate(
            flops=2 * slot_rows * phi_count * lat_rows * radial,
            bytes_accessed=4 * lat_rows * phi_count * radial,
            transcendentals=0,
        ),
    )(pair_orders, table, *takes)


def on_device_compact(grid_terms, pair_orders, legendre, state, kappa, right_op, left_op):
    lat_rows, phi_count, radial = grid_terms.shape
    rows = legendre.shape[1]
    degrees = rows - 1
    padded = -(-rows // 8) * 8
    columns = 2 * radial
    pair_total = pair_orders.shape[0]
    lat_block = 8
    table = natural_table(pair_total, lax.axis_size("sec"), phi_count)
    forward_table = jnp.asarray(table, jnp.bfloat16)
    inverse_table = jnp.asarray(table.transpose(0, 2, 1), jnp.bfloat16)

    def shape(*sizes, dtype=jnp.bfloat16):
        return jax.ShapeDtypeStruct(sizes, dtype)

    slab = shape(padded, 4 * lat_rows)
    cuts = call(
        cut_kernel,
        [legendre],
        [slab] * 4,
        scratch=[pltpu.VMEM((4, padded, 4 * lat_rows), jnp.bfloat16)],
    )
    weights = [cuts[0]] + [exchange(cuts[deep], deep=deep) for deep in (1, 2, 3)]

    keep, send = forward_sums(pair_orders, forward_table, grid_terms, lat_block)
    block = shape(4, 2, lat_rows, columns)
    blocks = call(add_kernel, [keep, exchange(send, sec=1)], [block] * 4, mib=24)
    takes = [blocks[0]] + [exchange(blocks[flat], flat=flat) for flat in (1, 2, 3)]

    gathered = pltpu.VMEM((4, 2, 4, lat_rows, columns), jnp.bfloat16)
    sums = call(
        functools.partial(degrees_kernel, degrees),
        [pair_orders, *weights, *takes],
        [shape(padded, columns, dtype=jnp.float32)] + [shape(padded, columns)] * 3,
        scalars=1,
        scratch=[gathered],
    )
    sums = [sums[0]] + [exchange(sums[deep], deep=deep) for deep in (1, 2, 3)]

    radial_mode = np.arange(radial, dtype=np.float32) / np.float32(radial)
    damping = np.exp(-filter_strength * radial_mode**filter_power).astype(np.float32)
    field = call(
        solve_kernel,
        [pair_orders, *sums, state, kappa[None, :], jnp.asarray(damping)[None, :], right_op, left_op],
        shape(padded, columns),
        scalars=1,
    )
    new_state = field[None, :rows]

    fields = [field] + [exchange(field, deep=deep) for deep in (1, 2, 3)]
    blocks = call(
        functools.partial(synthesis_kernel, degrees),
        [pair_orders, *weights, *fields],
        [block] * 4,
        scalars=1,
        scratch=[gathered],
    )
    takes = [blocks[0]] + [exchange(blocks[flat], flat=flat) for flat in (1, 2, 3)]
    takes += [exchange(take, sec=1) for take in takes]
    evolved = inverse_values(pair_orders, inverse_table, takes, lat_block)
    return (evolved, new_state)


def on_device(*args):
    lat_rows = args[0].shape[0]
    rows = args[2].shape[1]
    sections, side_row, side_x = (lax.axis_size(name) for name in names)
    fits = args[2].shape[0] == 1 and lat_rows % 16 == 0 and rows <= 2 * lat_rows
    fits = fits and args[0].size * 4 <= 24 * 1024 * 1024
    fits = fits and (sections, side_row, side_x) == (2, 8, 2)
    return on_device_compact(*args) if fits else on_device_wide(*args)


def solution(mesh):
    return jax.shard_map(
        on_device,
        mesh=mesh,
        in_specs=(
            P(("row", "col"), "sec", None),
            P(),
            P(("sec", "row", "col"), None, None),
            P(("sec", "row", "col"), None, None),
            P(),
            P(),
            P(),
        ),
        out_specs=(P(("row", "col"), "sec", None), P(("sec", "row", "col"), None, None)),
        check_vma=False,
    )
```

```python
import functools
import math

import jax
import jax.numpy as jnp
import numpy as np
from jax import lax
from jax.experimental import pallas as pl
from jax.experimental.pallas import tpu as pltpu
from jax.sharding import PartitionSpec as P

time_step = 0.5
filter_strength = 36.0
filter_power = 36.0


def slot_orders_of(pair_orders):
    order_total = 2 * pair_orders.shape[0]
    return jnp.stack([pair_orders, order_total - 1 - pair_orders], axis=1).reshape(order_total)


def fourier_table(orders, phi_start, phi_count, longitudes):
    longitude = phi_start + lax.iota(jnp.int32, phi_count)
    phase_turns = longitude[:, None] * orders[None, :] % longitudes
    phase_angle = phase_turns.astype(jnp.float32) * (2.0 * math.pi / longitudes)
    norm_scale = 1.0 / math.sqrt(longitudes)
    return jnp.stack(
        [jnp.cos(phase_angle) * norm_scale, -jnp.sin(phase_angle) * norm_scale], axis=-1
    )


def on_device_wide(grid_terms, pair_orders, legendre, state, kappa, right_op, left_op):
    lat_rows, phi_count, radial = grid_terms.shape
    pairs_here = legendre.shape[0]
    degrees = legendre.shape[1] - 1
    latitudes = legendre.shape[2]
    sections = lax.axis_size("sec")
    longitudes = phi_count * sections
    columns = 2 * radial
    section_slots = degrees // sections
    orders = slot_orders_of(pair_orders)
    sec_index = lax.axis_index("sec")
    highest = lax.Precision.HIGHEST
    phi_start = sec_index * phi_count
    sub_orders = orders
    phase_table = fourier_table(sub_orders, phi_start, phi_count, longitudes)
    term = jnp.einsum(
        "tpr,psc->stcr",
        grid_terms,
        phase_table,
        precision=highest,
        preferred_element_type=jnp.float32,
    )
    spectral = lax.psum_scatter(
        term.reshape(section_slots * lax.axis_size("sec"), lat_rows, columns),
        "sec",
        scatter_dimension=0,
        tiled=True,
    ).astype(jnp.bfloat16)
    device = lax.axis_index(("sec", "row", "col"))
    local_orders = lax.dynamic_slice_in_dim(pair_orders, device * pairs_here, pairs_here)
    row_index = lax.iota(jnp.int32, degrees + 1)
    leading = row_index[None, :] < (degrees - local_orders)[:, None]
    degree = jnp.where(leading, local_orders[:, None] + row_index[None, :], row_index[None, :] - 1)
    received = lax.all_to_all(spectral, ("row", "col"), split_axis=0, concat_axis=1, tiled=True)
    item_count = received.shape[2]
    paired = received.reshape(pairs_here, 2, latitudes, item_count)
    both_orders = jnp.einsum("pit,potx->piox", legendre, paired, preferred_element_type=jnp.float32)
    coefficient = jnp.where(leading[:, :, None], both_orders[:, :, 0], both_orders[:, :, 1])
    right_side = (state.astype(jnp.float32) + time_step * coefficient).astype(jnp.bfloat16)
    right_side = right_side.reshape(pairs_here, degrees + 1, 2, radial)
    eigen_part = jnp.einsum(
        "picr,rk->pick", right_side, right_op, preferred_element_type=jnp.float32
    )
    radial_mode = lax.iota(jnp.float32, radial) / radial
    damping = jnp.exp(-filter_strength * radial_mode**filter_power)
    degree_wide = degree.astype(jnp.float32)
    degree_term = degree_wide * (degree_wide + 1.0) / (degrees * degrees)
    factor = damping[None, None, :] / (1.0 + kappa[None, None, :] + degree_term[:, :, None])
    scaled = (eigen_part * factor[:, :, None, :]).astype(jnp.bfloat16)
    new_state = jnp.einsum("pick,kr->picr", scaled, left_op, preferred_element_type=jnp.float32)
    new_state = new_state.astype(jnp.bfloat16).reshape(pairs_here, degrees + 1, columns)
    zero_rows = jnp.zeros_like(new_state)
    split_state = jnp.stack(
        [
            jnp.where(leading[:, :, None], new_state, zero_rows),
            jnp.where(leading[:, :, None], zero_rows, new_state),
        ],
        axis=1,
    )
    synthesis_wide = jnp.einsum(
        "pit,poix->potx", legendre, split_state, preferred_element_type=jnp.float32
    )
    synthesis = synthesis_wide.astype(jnp.bfloat16).reshape(2 * pairs_here, latitudes, columns)
    returned = lax.all_to_all(synthesis, ("row", "col"), split_axis=1, concat_axis=0, tiled=True)
    sub_orders = lax.dynamic_slice_in_dim(orders, sec_index * section_slots, section_slots)
    phase_table = fourier_table(sub_orders, 0, longitudes, longitudes)
    values = returned.astype(jnp.float32).reshape(section_slots, lat_rows, 2, radial)
    partial_value = jnp.einsum(
        "stcr,psc->tpr", values, phase_table, precision=highest, preferred_element_type=jnp.float32
    )
    evolved = lax.psum_scatter(
        partial_value.astype(jnp.bfloat16), "sec", scatter_dimension=1, tiled=True
    ).astype(jnp.float32)
    return (evolved, new_state)


names = ("sec", "row", "col")


def natural_table(pair_total, sections, phi_count):
    slots = 2 * pair_total
    longitudes = sections * phi_count
    low = np.arange(pair_total)
    orders = np.stack([low, slots - 1 - low], axis=1).reshape(slots)
    turns = orders[:, None] * np.arange(longitudes)[None, :] % longitudes
    angle = turns * (2.0 * np.pi / longitudes)
    table = np.concatenate([np.cos(angle), -np.sin(angle)], axis=0) / np.sqrt(longitudes)
    return table.reshape(2 * slots, sections, phi_count).transpose(1, 0, 2).astype(np.float32)


def params(mib):
    return pltpu.CompilerParams(vmem_limit_bytes=mib * 1024 * 1024)


def vmem():
    return pl.BlockSpec(memory_space=pltpu.VMEM)


def smem():
    return pl.BlockSpec(memory_space=pltpu.SMEM)


def anywhere():
    return pl.BlockSpec(memory_space=pl.ANY)


def call(kernel, operands, out_shapes, mib=16, scalars=0, cost=None, scratch=()):
    single = not isinstance(out_shapes, (list, tuple))
    return pl.pallas_call(
        kernel,
        in_specs=[smem()] * scalars + [vmem()] * (len(operands) - scalars),
        out_specs=vmem() if single else [vmem()] * len(out_shapes),
        out_shape=out_shapes,
        scratch_shapes=scratch,
        compiler_params=params(mib),
        cost_estimate=cost,
    )(*operands)


four = range(4)


def plane_index():
    return lax.axis_index("row") % 2 * 2 + lax.axis_index("col")


def depth_index():
    return lax.axis_index("row") // 2


def pair_at(sec, deep, flat):
    row = lax.axis_index("row") ^ (2 * deep + flat // 2)
    col = lax.axis_index("col") ^ (flat % 2)
    at_sec = lax.axis_index("sec") ^ sec
    return (at_sec * lax.axis_size("row") + row) * lax.axis_size("col") + col


def exchange(array, sec=0, deep=0, flat=0):
    sizes = tuple(lax.axis_size(name) for name in names)
    pairs = []
    for source in np.ndindex(*sizes):
        target = (source[0] ^ sec, source[1] ^ (2 * deep + flat // 2), source[2] ^ (flat % 2))
        pairs.append(
            (int(np.ravel_multi_index(source, sizes)), int(np.ravel_multi_index(target, sizes)))
        )
    return lax.ppermute(array, names, pairs)


def cut_kernel(legendre_ref, *refs):
    outs, slabs = refs[:-1], refs[-1]
    count, rows, lats = slabs.shape
    given = legendre_ref.shape[1]
    slabs[...] = jnp.zeros_like(slabs)
    for at in range(count):
        slabs[at, :given] = legendre_ref[0, :, at * lats : (at + 1) * lats]
    for deep, out in enumerate(outs):
        out[...] = slabs[depth_index() ^ deep]


def forward_kernel(
    orders_from, table_ref, grid_ref, keep_ref, send_ref, orders_ref, table, buffer, held, sems, more
):
    rows, lat_block, radial = held.shape
    slots = rows // 2

    def chunk(at):
        return pltpu.make_async_copy(
            grid_ref.at[pl.ds(2 * at, 2)], buffer.at[pl.ds(2 * at, 2)], sems.at[at]
        )

    table_copy = pltpu.make_async_copy(table_ref.at[lax.axis_index("sec")], table, more.at[0])
    orders_copy = pltpu.make_async_copy(orders_from, orders_ref, more.at[1])
    table_copy.start()
    orders_copy.start()
    for at in range(sems.shape[0]):
        chunk(at).start()
    table_copy.wait()
    orders_copy.wait()

    def one_block(block, carry):
        begin = pl.multiple_of(block * lat_block, lat_block)
        for at in range(0, lat_block, 2):
            lat = begin + at
            chunk(lat // 2).wait()
            two = jnp.concatenate(
                [buffer[lat].astype(jnp.bfloat16), buffer[lat + 1].astype(jnp.bfloat16)], axis=1
            )
            sums = jnp.dot(table[...], two, preferred_element_type=jnp.float32)
            held[:, at, :] = sums[:, :radial]
            held[:, at + 1, :] = sums[:, radial:]
        for sec, out in ((1, send_ref), (0, keep_ref)):
            for flat, deep in np.ndindex(4, 4):
                order = orders_ref[pair_at(sec, deep, flat)]
                for half, part in np.ndindex(2, 2):
                    values = held[part * slots + 2 * order + half]
                    out[flat, deep, half, pl.ds(begin, lat_block), pl.ds(part * radial, radial)] = (
                        values.astype(out.dtype)
                    )
        return carry

    lax.fori_loop(0, buffer.shape[0] // lat_block, one_block, 0)


def forward_sums(pair_orders, table, grid_terms, lat_block):
    sections, rows, phi_count = table.shape
    lat_rows, _, radial = grid_terms.shape
    sizes = (4, 4, 2, lat_rows, 2 * radial)
    in_memory = [pltpu.with_memory_space_constraint(x, pltpu.HBM) for x in (pair_orders, table)]
    return pl.pallas_call(
        forward_kernel,
        in_specs=[pl.BlockSpec(memory_space=pltpu.HBM)] * 2 + [anywhere()],
        out_specs=[vmem(), vmem()],
        out_shape=[
            jax.ShapeDtypeStruct(sizes, jnp.float32),
            jax.ShapeDtypeStruct(sizes, jnp.bfloat16),
        ],
        scratch_shapes=[
            pltpu.SMEM(pair_orders.shape, jnp.int32),
            pltpu.VMEM((rows, phi_count), table.dtype),
            pltpu.VMEM(grid_terms.shape, jnp.float32),
            pltpu.VMEM((rows, lat_block, radial), jnp.float32),
            pltpu.SemaphoreType.DMA((lat_rows // 2,)),
            pltpu.SemaphoreType.DMA((2,)),
        ],
        compiler_params=params(36),
        cost_estimate=pl.CostEstimate(
            flops=2 * rows * phi_count * lat_rows * radial,
            bytes_accessed=4 * lat_rows * phi_count * radial,
            transcendentals=0,
        ),
    )(*in_memory, grid_terms)


def add_kernel(keep_ref, take_ref, *outs):
    for flat, out in enumerate(outs):
        out[...] = (keep_ref[flat] + take_ref[flat].astype(jnp.float32)).astype(out.dtype)


def masked(weights, order, degrees):
    row_index = lax.broadcasted_iota(jnp.int32, weights.shape, 0)
    leading = row_index < degrees - order
    zero = jnp.zeros_like(weights)
    return jnp.where(leading, weights, zero), jnp.where(leading, zero, weights)


def degrees_kernel(degrees, orders_ref, *refs):
    weights, takes, outs, gathered = refs[:4], refs[4:8], refs[8:12], refs[12]
    _, _, _, lat_rows, columns = gathered.shape
    own = plane_index()
    for flat in four:
        for deep, half in np.ndindex(4, 2):
            gathered[deep, half, own ^ flat] = takes[flat][deep, half]
    for deep in four:
        chosen = masked(weights[deep][...], orders_ref[pair_at(0, deep, 0)], degrees)
        total = 0.0
        for half in range(2):
            total += jnp.dot(
                chosen[half],
                gathered[deep, half].reshape(4 * lat_rows, columns),
                preferred_element_type=jnp.float32,
            )
        outs[deep][...] = total.astype(outs[deep].dtype)


def synthesis_kernel(degrees, orders_ref, *refs):
    weights, fields, outs, spread = refs[:4], refs[4:8], refs[8:12], refs[12]
    _, _, _, lat_rows, columns = spread.shape
    contract = (((0,), (0,)), ((), ()))
    own = plane_index()
    for deep in four:
        chosen = masked(weights[deep][...], orders_ref[pair_at(0, deep, 0)], degrees)
        for half in range(2):
            values = lax.dot_general(
                chosen[half], fields[deep][...], contract, preferred_element_type=jnp.float32
            )
            spread[deep, half] = values.astype(spread.dtype).reshape(4, lat_rows, columns)
    for flat in (3, 1, 2, 0):
        for deep, half in np.ndindex(4, 2):
            outs[flat][deep, half] = spread[deep, half, own ^ flat]


def solve_kernel(
    orders_ref, one, two, three, last, state_ref, kappa_ref, damping_ref, right_ref, left_ref, sent_ref
):
    rows = state_ref.shape[1]
    radial = right_ref.shape[0]
    degrees = rows - 1
    order = orders_ref[pair_at(0, 0, 0)]
    coefficient = one[...]
    for other in (two, three, last):
        coefficient += other[...].astype(jnp.float32)
    right_side = state_ref[0].astype(jnp.float32) + time_step * coefficient[:rows]
    right_side = right_side.astype(jnp.bfloat16)
    row_index = lax.broadcasted_iota(jnp.int32, (rows, radial), 0)
    degree = jnp.where(row_index < degrees - order, order + row_index, row_index - 1)
    degree = degree.astype(jnp.float32)
    factor = damping_ref[...] / (
        1.0 + kappa_ref[...] + degree * (degree + 1.0) / (degrees * degrees)
    )
    sent_ref[...] = jnp.zeros_like(sent_ref)
    for part in range(2):
        columns = pl.ds(part * radial, radial)
        eigen = jnp.dot(
            right_side[:, part * radial : (part + 1) * radial],
            right_ref[...],
            preferred_element_type=jnp.float32,
        )
        scaled = (eigen * factor).astype(jnp.bfloat16)
        field = jnp.dot(scaled, left_ref[...], preferred_element_type=jnp.float32)
        field = field.astype(jnp.bfloat16)
        sent_ref[pl.ds(0, rows), columns] = field


def inverse_kernel(orders_ref, table_ref, *refs):
    takes, (out_ref, buffer, held, sems) = refs[:-4], refs[-4:]
    slot_rows, lat_block, radial = held.shape
    slots = slot_rows // 2
    table = table_ref[lax.axis_index("sec")]

    def chunk(at):
        return pltpu.make_async_copy(
            buffer.at[pl.ds(2 * at, 2)], out_ref.at[pl.ds(2 * at, 2)], sems.at[at]
        )

    def one_block(block, carry):
        begin = pl.multiple_of(block * lat_block, lat_block)
        for sec, flat, deep in np.ndindex(2, 4, 4):
            order = orders_ref[pair_at(sec, deep, flat)]
            for half, part in np.ndindex(2, 2):
                values = takes[4 * sec + flat][
                    deep, half, pl.ds(begin, lat_block), pl.ds(part * radial, radial)
                ]
                held[part * slots + 2 * order + half] = values.astype(jnp.float32)
        for at in range(0, lat_block, 2):
            two = jnp.concatenate(
                [held[:, at, :].astype(jnp.bfloat16), held[:, at + 1, :].astype(jnp.bfloat16)],
                axis=1,
            )
            values = jnp.dot(table, two, preferred_element_type=jnp.float32)
            lat = begin + at
            buffer[lat] = values[:, :radial]
            buffer[lat + 1] = values[:, radial:]
            chunk(lat // 2).start()
        return carry

    lax.fori_loop(0, buffer.shape[0] // lat_block, one_block, 0)
    for at in range(sems.shape[0]):
        chunk(at).wait()


def inverse_values(pair_orders, table, takes, lat_block):
    _, phi_count, slot_rows = table.shape
    lat_rows, radial = takes[0].shape[2], takes[0].shape[3] // 2
    out = jax.ShapeDtypeStruct((lat_rows, phi_count, radial), jnp.float32)
    return pl.pallas_call(
        inverse_kernel,
        in_specs=[smem()] + [vmem()] * (1 + len(takes)),
        out_specs=anywhere(),
        out_shape=out,
        scratch_shapes=[
            pltpu.VMEM(out.shape, jnp.float32),
            pltpu.VMEM((slot_rows, lat_block, radial), jnp.float32),
            pltpu.SemaphoreType.DMA((lat_rows // 2,)),
        ],
        compiler_params=params(36),
        cost_estimate=pl.CostEstimate(
            flops=2 * slot_rows * phi_count * lat_rows * radial,
            bytes_accessed=4 * lat_rows * phi_count * radial,
            transcendentals=0,
        ),
    )(pair_orders, table, *takes)


def on_device_compact(grid_terms, pair_orders, legendre, state, kappa, right_op, left_op):
    lat_rows, phi_count, radial = grid_terms.shape
    rows = legendre.shape[1]
    degrees = rows - 1
    padded = -(-rows // 8) * 8
    columns = 2 * radial
    pair_total = pair_orders.shape[0]
    lat_block = 16
    table = natural_table(pair_total, lax.axis_size("sec"), phi_count)
    forward_table = jnp.asarray(table, jnp.bfloat16)
    inverse_table = jnp.asarray(table.transpose(0, 2, 1), jnp.bfloat16)

    def shape(*sizes, dtype=jnp.bfloat16):
        return jax.ShapeDtypeStruct(sizes, dtype)

    slab = shape(padded, 4 * lat_rows)
    cuts = call(
        cut_kernel,
        [legendre],
        [slab] * 4,
        scratch=[pltpu.VMEM((4, padded, 4 * lat_rows), jnp.bfloat16)],
    )
    weights = [cuts[0]] + [exchange(cuts[deep], deep=deep) for deep in (1, 2, 3)]

    keep, send = forward_sums(pair_orders, forward_table, grid_terms, lat_block)
    block = shape(4, 2, lat_rows, columns)
    blocks = call(add_kernel, [keep, exchange(send, sec=1)], [block] * 4, mib=24)
    takes = [blocks[0]] + [exchange(blocks[flat], flat=flat) for flat in (1, 2, 3)]

    gathered = pltpu.VMEM((4, 2, 4, lat_rows, columns), jnp.bfloat16)
    sums = call(
        functools.partial(degrees_kernel, degrees),
        [pair_orders, *weights, *takes],
        [shape(padded, columns, dtype=jnp.float32)] + [shape(padded, columns)] * 3,
        scalars=1,
        scratch=[gathered],
    )
    sums = [sums[0]] + [exchange(sums[deep], deep=deep) for deep in (3, 2, 1)]

    radial_mode = np.arange(radial, dtype=np.float32) / np.float32(radial)
    damping = np.exp(-filter_strength * radial_mode**filter_power).astype(np.float32)
    field = call(
        solve_kernel,
        [pair_orders, *sums, state, kappa[None, :], jnp.asarray(damping)[None, :], right_op, left_op],
        shape(padded, columns),
        scalars=1,
    )
    new_state = field[None, :rows]

    fields = [field] + [exchange(field, deep=deep) for deep in (1, 2, 3)]
    blocks = call(
        functools.partial(synthesis_kernel, degrees),
        [pair_orders, *weights, *fields],
        [block] * 4,
        scalars=1,
        scratch=[gathered],
    )
    takes = [blocks[0]] + [exchange(blocks[flat], flat=flat) for flat in (1, 2, 3)]
    takes += [exchange(take, sec=1) for take in takes]
    evolved = inverse_values(pair_orders, inverse_table, takes, lat_block)
    return (evolved, new_state)


def on_device(*args):
    lat_rows = args[0].shape[0]
    rows = args[2].shape[1]
    sections, side_row, side_x = (lax.axis_size(name) for name in names)
    fits = args[2].shape[0] == 1 and lat_rows % 16 == 0 and rows <= 2 * lat_rows
    fits = fits and args[0].size * 4 <= 24 * 1024 * 1024
    fits = fits and (sections, side_row, side_x) == (2, 8, 2)
    return on_device_compact(*args) if fits else on_device_wide(*args)


def solution(mesh):
    return jax.shard_map(
        on_device,
        mesh=mesh,
        in_specs=(
            P(("row", "col"), "sec", None),
            P(),
            P(("sec", "row", "col"), None, None),
            P(("sec", "row", "col"), None, None),
            P(),
            P(),
            P(),
        ),
        out_specs=(P(("row", "col"), "sec", None), P(("sec", "row", "col"), None, None)),
        check_vma=False,
    )
```

```python
import functools
import math

import jax
import jax.numpy as jnp
import numpy as np
from jax import lax
from jax.experimental import pallas as pl
from jax.experimental.pallas import tpu as pltpu
from jax.sharding import PartitionSpec as P

time_step = 0.5
filter_strength = 36.0
filter_power = 36.0


def slot_orders_of(pair_orders):
    order_total = 2 * pair_orders.shape[0]
    return jnp.stack([pair_orders, order_total - 1 - pair_orders], axis=1).reshape(order_total)


def fourier_table(orders, phi_start, phi_count, longitudes):
    longitude = phi_start + lax.iota(jnp.int32, phi_count)
    phase_turns = longitude[:, None] * orders[None, :] % longitudes
    phase_angle = phase_turns.astype(jnp.float32) * (2.0 * math.pi / longitudes)
    norm_scale = 1.0 / math.sqrt(longitudes)
    return jnp.stack(
        [jnp.cos(phase_angle) * norm_scale, -jnp.sin(phase_angle) * norm_scale], axis=-1
    )


def on_device_wide(grid_terms, pair_orders, legendre, state, kappa, right_op, left_op):
    lat_rows, phi_count, radial = grid_terms.shape
    pairs_here = legendre.shape[0]
    degrees = legendre.shape[1] - 1
    latitudes = legendre.shape[2]
    sections = lax.axis_size("sec")
    longitudes = phi_count * sections
    columns = 2 * radial
    section_slots = degrees // sections
    orders = slot_orders_of(pair_orders)
    sec_index = lax.axis_index("sec")
    highest = lax.Precision.HIGHEST
    phi_start = sec_index * phi_count
    sub_orders = orders
    phase_table = fourier_table(sub_orders, phi_start, phi_count, longitudes)
    term = jnp.einsum(
        "tpr,psc->stcr",
        grid_terms,
        phase_table,
        precision=highest,
        preferred_element_type=jnp.float32,
    )
    spectral = lax.psum_scatter(
        term.reshape(section_slots * lax.axis_size("sec"), lat_rows, columns),
        "sec",
        scatter_dimension=0,
        tiled=True,
    ).astype(jnp.bfloat16)
    device = lax.axis_index(("sec", "row", "col"))
    local_orders = lax.dynamic_slice_in_dim(pair_orders, device * pairs_here, pairs_here)
    row_index = lax.iota(jnp.int32, degrees + 1)
    leading = row_index[None, :] < (degrees - local_orders)[:, None]
    degree = jnp.where(leading, local_orders[:, None] + row_index[None, :], row_index[None, :] - 1)
    received = lax.all_to_all(spectral, ("row", "col"), split_axis=0, concat_axis=1, tiled=True)
    item_count = received.shape[2]
    paired = received.reshape(pairs_here, 2, latitudes, item_count)
    both_orders = jnp.einsum("pit,potx->piox", legendre, paired, preferred_element_type=jnp.float32)
    coefficient = jnp.where(leading[:, :, None], both_orders[:, :, 0], both_orders[:, :, 1])
    right_side = (state.astype(jnp.float32) + time_step * coefficient).astype(jnp.bfloat16)
    right_side = right_side.reshape(pairs_here, degrees + 1, 2, radial)
    eigen_part = jnp.einsum(
        "picr,rk->pick", right_side, right_op, preferred_element_type=jnp.float32
    )
    radial_mode = lax.iota(jnp.float32, radial) / radial
    damping = jnp.exp(-filter_strength * radial_mode**filter_power)
    degree_wide = degree.astype(jnp.float32)
    degree_term = degree_wide * (degree_wide + 1.0) / (degrees * degrees)
    factor = damping[None, None, :] / (1.0 + kappa[None, None, :] + degree_term[:, :, None])
    scaled = (eigen_part * factor[:, :, None, :]).astype(jnp.bfloat16)
    new_state = jnp.einsum("pick,kr->picr", scaled, left_op, preferred_element_type=jnp.float32)
    new_state = new_state.astype(jnp.bfloat16).reshape(pairs_here, degrees + 1, columns)
    zero_rows = jnp.zeros_like(new_state)
    split_state = jnp.stack(
        [
            jnp.where(leading[:, :, None], new_state, zero_rows),
            jnp.where(leading[:, :, None], zero_rows, new_state),
        ],
        axis=1,
    )
    synthesis_wide = jnp.einsum(
        "pit,poix->potx", legendre, split_state, preferred_element_type=jnp.float32
    )
    synthesis = synthesis_wide.astype(jnp.bfloat16).reshape(2 * pairs_here, latitudes, columns)
    returned = lax.all_to_all(synthesis, ("row", "col"), split_axis=1, concat_axis=0, tiled=True)
    sub_orders = lax.dynamic_slice_in_dim(orders, sec_index * section_slots, section_slots)
    phase_table = fourier_table(sub_orders, 0, longitudes, longitudes)
    values = returned.astype(jnp.float32).reshape(section_slots, lat_rows, 2, radial)
    partial_value = jnp.einsum(
        "stcr,psc->tpr", values, phase_table, precision=highest, preferred_element_type=jnp.float32
    )
    evolved = lax.psum_scatter(
        partial_value.astype(jnp.bfloat16), "sec", scatter_dimension=1, tiled=True
    ).astype(jnp.float32)
    return (evolved, new_state)


names = ("sec", "row", "col")


def natural_table(pair_total, sections, phi_count):
    slots = 2 * pair_total
    longitudes = sections * phi_count
    low = np.arange(pair_total)
    orders = np.stack([low, slots - 1 - low], axis=1).reshape(slots)
    turns = orders[:, None] * np.arange(longitudes)[None, :] % longitudes
    angle = turns * (2.0 * np.pi / longitudes)
    table = np.concatenate([np.cos(angle), -np.sin(angle)], axis=0) / np.sqrt(longitudes)
    return table.reshape(2 * slots, sections, phi_count).transpose(1, 0, 2).astype(np.float32)


def params(mib):
    return pltpu.CompilerParams(vmem_limit_bytes=mib * 1024 * 1024)


def vmem():
    return pl.BlockSpec(memory_space=pltpu.VMEM)


def smem():
    return pl.BlockSpec(memory_space=pltpu.SMEM)


def anywhere():
    return pl.BlockSpec(memory_space=pl.ANY)


def call(kernel, operands, out_shapes, mib=16, scalars=0, cost=None, scratch=()):
    single = not isinstance(out_shapes, (list, tuple))
    return pl.pallas_call(
        kernel,
        in_specs=[smem()] * scalars + [vmem()] * (len(operands) - scalars),
        out_specs=vmem() if single else [vmem()] * len(out_shapes),
        out_shape=out_shapes,
        scratch_shapes=scratch,
        compiler_params=params(mib),
        cost_estimate=cost,
    )(*operands)


four = range(4)


def plane_index():
    return lax.axis_index("row") % 2 * 2 + lax.axis_index("col")


def depth_index():
    return lax.axis_index("row") // 2


def pair_at(sec, deep, flat):
    row = lax.axis_index("row") ^ (2 * deep + flat // 2)
    col = lax.axis_index("col") ^ (flat % 2)
    at_sec = lax.axis_index("sec") ^ sec
    return (at_sec * lax.axis_size("row") + row) * lax.axis_size("col") + col


def exchange(array, sec=0, deep=0, flat=0):
    sizes = tuple(lax.axis_size(name) for name in names)
    pairs = []
    for source in np.ndindex(*sizes):
        target = (source[0] ^ sec, source[1] ^ (2 * deep + flat // 2), source[2] ^ (flat % 2))
        pairs.append(
            (int(np.ravel_multi_index(source, sizes)), int(np.ravel_multi_index(target, sizes)))
        )
    return lax.ppermute(array, names, pairs)


def cut_kernel(legendre_ref, *refs):
    outs, parts = refs[:-1], refs[-1]
    count, rows, lats = parts.shape
    given = legendre_ref.shape[1]
    parts[...] = jnp.zeros_like(parts)
    for at in range(count):
        parts[at, :given] = legendre_ref[0, :, at * lats : (at + 1) * lats]
    for deep, out in enumerate(outs):
        first = (depth_index() ^ deep) * 4
        out[...] = jnp.concatenate([parts[first + (plane_index() ^ flat)] for flat in four], axis=1)


def forward_kernel(
    orders_from, table_ref, grid_ref, keep_ref, send_ref, orders_ref, table, buffer, held, sems, more
):
    blocks, rows, lat_block, radial = held.shape
    slots = rows // 2

    def chunk(at):
        return pltpu.make_async_copy(
            grid_ref.at[pl.ds(2 * at, 2)], buffer.at[pl.ds(2 * at, 2)], sems.at[at]
        )

    table_copy = pltpu.make_async_copy(table_ref.at[lax.axis_index("sec")], table, more.at[0])
    orders_copy = pltpu.make_async_copy(orders_from, orders_ref, more.at[1])
    table_copy.start()
    orders_copy.start()
    for at in range(sems.shape[0]):
        chunk(at).start()
    table_copy.wait()
    orders_copy.wait()

    def one_block(block, carry):
        for at in range(0, lat_block, 2):
            lat = block * lat_block + at
            chunk(lat // 2).wait()
            two = jnp.concatenate(
                [buffer[lat].astype(jnp.bfloat16), buffer[lat + 1].astype(jnp.bfloat16)], axis=1
            )
            sums = jnp.dot(table[...], two, preferred_element_type=jnp.float32)
            held[block, :, at, :] = sums[:, :radial]
            held[block, :, at + 1, :] = sums[:, radial:]
        return carry

    lax.fori_loop(0, blocks, one_block, 0)
    for sec, out in ((1, send_ref), (0, keep_ref)):
        for flat, deep in np.ndindex(4, 4):
            order = orders_ref[pair_at(sec, deep, flat)]
            for part in range(2):
                values = held[:, pl.ds(part * slots + 2 * order, 2)].astype(out.dtype)
                for half in range(2):
                    out[flat, deep, half, :, pl.ds(part * radial, radial)] = values[
                        :, half
                    ].reshape(blocks * lat_block, radial)


def forward_sums(pair_orders, table, grid_terms, lat_block):
    sections, rows, phi_count = table.shape
    lat_rows, _, radial = grid_terms.shape
    sizes = (4, 4, 2, lat_rows, 2 * radial)
    in_memory = [pltpu.with_memory_space_constraint(x, pltpu.HBM) for x in (pair_orders, table)]
    return pl.pallas_call(
        forward_kernel,
        in_specs=[pl.BlockSpec(memory_space=pltpu.HBM)] * 2 + [anywhere()],
        out_specs=[vmem(), vmem()],
        out_shape=[
            jax.ShapeDtypeStruct(sizes, jnp.float32),
            jax.ShapeDtypeStruct(sizes, jnp.bfloat16),
        ],
        scratch_shapes=[
            pltpu.SMEM(pair_orders.shape, jnp.int32),
            pltpu.VMEM((rows, phi_count), table.dtype),
            pltpu.VMEM(grid_terms.shape, jnp.float32),
            pltpu.VMEM((lat_rows // lat_block, rows, lat_block, radial), jnp.float32),
            pltpu.SemaphoreType.DMA((lat_rows // 2,)),
            pltpu.SemaphoreType.DMA((2,)),
        ],
        compiler_params=params(36),
        cost_estimate=pl.CostEstimate(
            flops=2 * rows * phi_count * lat_rows * radial,
            bytes_accessed=4 * lat_rows * phi_count * radial,
            transcendentals=0,
        ),
    )(*in_memory, grid_terms)


def add_kernel(keep_ref, take_ref, *outs):
    for flat, out in enumerate(outs):
        out[...] = (keep_ref[flat] + take_ref[flat].astype(jnp.float32)).astype(out.dtype)


def masked(weights, order, degrees):
    row_index = lax.broadcasted_iota(jnp.int32, weights.shape, 0)
    leading = row_index < degrees - order
    zero = jnp.zeros_like(weights)
    return jnp.where(leading, weights, zero), jnp.where(leading, zero, weights)


def degrees_kernel(degrees, orders_ref, *refs):
    weights, takes, outs = refs[:4], refs[4:8], refs[8:]
    for deep in four:
        chosen = masked(weights[deep][...], orders_ref[pair_at(0, deep, 0)], degrees)
        total = 0.0
        for half in range(2):
            rows = jnp.concatenate([take[deep, half] for take in takes], axis=0)
            total += jnp.dot(chosen[half], rows, preferred_element_type=jnp.float32)
        outs[deep][...] = total.astype(outs[deep].dtype)


def synthesis_kernel(degrees, orders_ref, *refs):
    weights, fields, outs = refs[:4], refs[4:8], refs[8:]
    lat_rows = outs[0].shape[2]
    contract = (((0,), (0,)), ((), ()))
    for deep in four:
        chosen = masked(weights[deep][...], orders_ref[pair_at(0, deep, 0)], degrees)
        for half in range(2):
            values = lax.dot_general(
                chosen[half], fields[deep][...], contract, preferred_element_type=jnp.float32
            ).astype(jnp.bfloat16)
            for flat, out in enumerate(outs):
                out[deep, half] = values[flat * lat_rows : (flat + 1) * lat_rows]


def factor_kernel(degrees, orders_ref, kappa_ref, damping_ref, factor_ref):
    order = orders_ref[pair_at(0, 0, 0)]
    row_index = lax.broadcasted_iota(jnp.int32, factor_ref.shape, 0)
    degree = jnp.where(row_index < degrees - order, order + row_index, row_index - 1)
    degree = degree.astype(jnp.float32)
    factor_ref[...] = damping_ref[...] / (
        1.0 + kappa_ref[...] + degree * (degree + 1.0) / (degrees * degrees)
    )


def solve_kernel(one, two, three, last, state_ref, factor_ref, right_ref, left_ref, sent_ref):
    rows = state_ref.shape[1]
    radial = right_ref.shape[0]
    coefficient = one[...]
    for other in (two, three, last):
        coefficient += other[...].astype(jnp.float32)
    right_side = state_ref[0].astype(jnp.float32) + time_step * coefficient[:rows]
    right_side = right_side.astype(jnp.bfloat16)
    sent_ref[...] = jnp.zeros_like(sent_ref)
    for part in range(2):
        columns = pl.ds(part * radial, radial)
        eigen = jnp.dot(
            right_side[:, part * radial : (part + 1) * radial],
            right_ref[...],
            preferred_element_type=jnp.float32,
        )
        scaled = (eigen * factor_ref[...]).astype(jnp.bfloat16)
        field = jnp.dot(scaled, left_ref[...], preferred_element_type=jnp.float32)
        sent_ref[pl.ds(0, rows), columns] = field.astype(jnp.bfloat16)


def inverse_kernel(orders_ref, table_ref, *refs):
    takes, (out_ref, buffer, held, sems) = refs[:-4], refs[-4:]
    slot_rows, lat_block, radial = held.shape
    slots = slot_rows // 2
    table = table_ref[lax.axis_index("sec")]

    def chunk(at):
        return pltpu.make_async_copy(
            buffer.at[pl.ds(2 * at, 2)], out_ref.at[pl.ds(2 * at, 2)], sems.at[at]
        )

    def one_block(block, carry):
        begin = pl.multiple_of(block * lat_block, lat_block)
        for sec, flat, deep in np.ndindex(2, 4, 4):
            order = orders_ref[pair_at(sec, deep, flat)]
            for half, part in np.ndindex(2, 2):
                values = takes[4 * sec + flat][
                    deep, half, pl.ds(begin, lat_block), pl.ds(part * radial, radial)
                ]
                held[part * slots + 2 * order + half] = values.astype(jnp.float32)
        for at in range(0, lat_block, 2):
            two = jnp.concatenate(
                [held[:, at, :].astype(jnp.bfloat16), held[:, at + 1, :].astype(jnp.bfloat16)],
                axis=1,
            )
            values = jnp.dot(table, two, preferred_element_type=jnp.float32)
            lat = begin + at
            buffer[lat] = values[:, :radial]
            buffer[lat + 1] = values[:, radial:]
            chunk(lat // 2).start()
        return carry

    lax.fori_loop(0, buffer.shape[0] // lat_block, one_block, 0)
    for at in range(sems.shape[0]):
        chunk(at).wait()


def inverse_values(pair_orders, table, takes, lat_block):
    _, phi_count, slot_rows = table.shape
    lat_rows, radial = takes[0].shape[2], takes[0].shape[3] // 2
    out = jax.ShapeDtypeStruct((lat_rows, phi_count, radial), jnp.float32)
    return pl.pallas_call(
        inverse_kernel,
        in_specs=[smem()] + [vmem()] * (1 + len(takes)),
        out_specs=anywhere(),
        out_shape=out,
        scratch_shapes=[
            pltpu.VMEM(out.shape, jnp.float32),
            pltpu.VMEM((slot_rows, lat_block, radial), jnp.float32),
            pltpu.SemaphoreType.DMA((lat_rows // 2,)),
        ],
        compiler_params=params(36),
        cost_estimate=pl.CostEstimate(
            flops=2 * slot_rows * phi_count * lat_rows * radial,
            bytes_accessed=4 * lat_rows * phi_count * radial,
            transcendentals=0,
        ),
    )(pair_orders, table, *takes)


def on_device_compact(grid_terms, pair_orders, legendre, state, kappa, right_op, left_op):
    lat_rows, phi_count, radial = grid_terms.shape
    rows = legendre.shape[1]
    degrees = rows - 1
    padded = -(-rows // 8) * 8
    columns = 2 * radial
    pair_total = pair_orders.shape[0]
    table = natural_table(pair_total, lax.axis_size("sec"), phi_count)
    forward_table = jnp.asarray(table, jnp.bfloat16)
    inverse_table = jnp.asarray(table.transpose(0, 2, 1), jnp.bfloat16)

    def shape(*sizes, dtype=jnp.bfloat16):
        return jax.ShapeDtypeStruct(sizes, dtype)

    slab = shape(padded, 4 * lat_rows)
    cuts = call(
        cut_kernel,
        [legendre],
        [slab] * 4,
        scratch=[pltpu.VMEM((16, padded, lat_rows), jnp.bfloat16)],
    )
    weights = [cuts[0]] + [exchange(cuts[deep], deep=deep) for deep in (1, 2, 3)]

    keep, send = forward_sums(pair_orders, forward_table, grid_terms, 8)
    block = shape(4, 2, lat_rows, columns)
    blocks = call(add_kernel, [keep, exchange(send, sec=1)], [block] * 4, mib=24)
    takes = [blocks[0]] + [exchange(blocks[flat], flat=flat) for flat in (1, 2, 3)]

    sums = call(
        functools.partial(degrees_kernel, degrees),
        [pair_orders, *weights, *takes],
        [shape(padded, columns, dtype=jnp.float32)] + [shape(padded, columns)] * 3,
        scalars=1,
    )
    sums = [sums[0]] + [exchange(sums[deep], deep=deep) for deep in (3, 2, 1)]

    radial_mode = np.arange(radial, dtype=np.float32) / np.float32(radial)
    damping = np.exp(-filter_strength * radial_mode**filter_power).astype(np.float32)
    factor = call(
        functools.partial(factor_kernel, degrees),
        [pair_orders, kappa[None, :], jnp.asarray(damping)[None, :]],
        shape(rows, radial, dtype=jnp.float32),
        scalars=1,
    )
    field = call(
        solve_kernel, [*sums, state, factor, right_op, left_op], shape(padded, columns)
    )
    new_state = field[None, :rows]

    fields = [field] + [exchange(field, deep=deep) for deep in (1, 2, 3)]
    blocks = call(
        functools.partial(synthesis_kernel, degrees),
        [pair_orders, *weights, *fields],
        [block] * 4,
        scalars=1,
    )
    takes = [blocks[0]] + [exchange(blocks[flat], flat=flat) for flat in (1, 2, 3)]
    takes += [exchange(take, sec=1) for take in takes]
    evolved = inverse_values(pair_orders, inverse_table, takes, 16)
    return (evolved, new_state)


def on_device(*args):
    lat_rows = args[0].shape[0]
    rows = args[2].shape[1]
    sections, side_row, side_x = (lax.axis_size(name) for name in names)
    fits = args[2].shape[0] == 1 and lat_rows % 16 == 0 and rows <= 2 * lat_rows
    fits = fits and args[0].size * 4 <= 24 * 1024 * 1024
    fits = fits and (sections, side_row, side_x) == (2, 8, 2)
    return on_device_compact(*args) if fits else on_device_wide(*args)


def solution(mesh):
    return jax.shard_map(
        on_device,
        mesh=mesh,
        in_specs=(
            P(("row", "col"), "sec", None),
            P(),
            P(("sec", "row", "col"), None, None),
            P(("sec", "row", "col"), None, None),
            P(),
            P(),
            P(),
        ),
        out_specs=(P(("row", "col"), "sec", None), P(("sec", "row", "col"), None, None)),
        check_vma=False,
    )
```

```python
import functools
import math

import jax
import jax.numpy as jnp
import numpy as np
from jax import lax
from jax.experimental import pallas as pl
from jax.experimental.pallas import tpu as pltpu
from jax.sharding import PartitionSpec as P

time_step = 0.5
filter_strength = 36.0
filter_power = 36.0


def slot_orders_of(pair_orders):
    order_total = 2 * pair_orders.shape[0]
    return jnp.stack([pair_orders, order_total - 1 - pair_orders], axis=1).reshape(order_total)


def fourier_table(orders, phi_start, phi_count, longitudes):
    longitude = phi_start + lax.iota(jnp.int32, phi_count)
    phase_turns = longitude[:, None] * orders[None, :] % longitudes
    phase_angle = phase_turns.astype(jnp.float32) * (2.0 * math.pi / longitudes)
    norm_scale = 1.0 / math.sqrt(longitudes)
    return jnp.stack(
        [jnp.cos(phase_angle) * norm_scale, -jnp.sin(phase_angle) * norm_scale], axis=-1
    )


def on_device_wide(grid_terms, pair_orders, legendre, state, kappa, right_op, left_op):
    lat_rows, phi_count, radial = grid_terms.shape
    pairs_here = legendre.shape[0]
    degrees = legendre.shape[1] - 1
    latitudes = legendre.shape[2]
    sections = lax.axis_size("sec")
    longitudes = phi_count * sections
    columns = 2 * radial
    section_slots = degrees // sections
    orders = slot_orders_of(pair_orders)
    sec_index = lax.axis_index("sec")
    highest = lax.Precision.HIGHEST
    phi_start = sec_index * phi_count
    sub_orders = orders
    phase_table = fourier_table(sub_orders, phi_start, phi_count, longitudes)
    term = jnp.einsum(
        "tpr,psc->stcr",
        grid_terms,
        phase_table,
        precision=highest,
        preferred_element_type=jnp.float32,
    )
    spectral = lax.psum_scatter(
        term.reshape(section_slots * lax.axis_size("sec"), lat_rows, columns),
        "sec",
        scatter_dimension=0,
        tiled=True,
    ).astype(jnp.bfloat16)
    device = lax.axis_index(("sec", "row", "col"))
    local_orders = lax.dynamic_slice_in_dim(pair_orders, device * pairs_here, pairs_here)
    row_index = lax.iota(jnp.int32, degrees + 1)
    leading = row_index[None, :] < (degrees - local_orders)[:, None]
    degree = jnp.where(leading, local_orders[:, None] + row_index[None, :], row_index[None, :] - 1)
    received = lax.all_to_all(spectral, ("row", "col"), split_axis=0, concat_axis=1, tiled=True)
    item_count = received.shape[2]
    paired = received.reshape(pairs_here, 2, latitudes, item_count)
    both_orders = jnp.einsum("pit,potx->piox", legendre, paired, preferred_element_type=jnp.float32)
    coefficient = jnp.where(leading[:, :, None], both_orders[:, :, 0], both_orders[:, :, 1])
    right_side = (state.astype(jnp.float32) + time_step * coefficient).astype(jnp.bfloat16)
    right_side = right_side.reshape(pairs_here, degrees + 1, 2, radial)
    eigen_part = jnp.einsum(
        "picr,rk->pick", right_side, right_op, preferred_element_type=jnp.float32
    )
    radial_mode = lax.iota(jnp.float32, radial) / radial
    damping = jnp.exp(-filter_strength * radial_mode**filter_power)
    degree_wide = degree.astype(jnp.float32)
    degree_term = degree_wide * (degree_wide + 1.0) / (degrees * degrees)
    factor = damping[None, None, :] / (1.0 + kappa[None, None, :] + degree_term[:, :, None])
    scaled = (eigen_part * factor[:, :, None, :]).astype(jnp.bfloat16)
    new_state = jnp.einsum("pick,kr->picr", scaled, left_op, preferred_element_type=jnp.float32)
    new_state = new_state.astype(jnp.bfloat16).reshape(pairs_here, degrees + 1, columns)
    zero_rows = jnp.zeros_like(new_state)
    split_state = jnp.stack(
        [
            jnp.where(leading[:, :, None], new_state, zero_rows),
            jnp.where(leading[:, :, None], zero_rows, new_state),
        ],
        axis=1,
    )
    synthesis_wide = jnp.einsum(
        "pit,poix->potx", legendre, split_state, preferred_element_type=jnp.float32
    )
    synthesis = synthesis_wide.astype(jnp.bfloat16).reshape(2 * pairs_here, latitudes, columns)
    returned = lax.all_to_all(synthesis, ("row", "col"), split_axis=1, concat_axis=0, tiled=True)
    sub_orders = lax.dynamic_slice_in_dim(orders, sec_index * section_slots, section_slots)
    phase_table = fourier_table(sub_orders, 0, longitudes, longitudes)
    values = returned.astype(jnp.float32).reshape(section_slots, lat_rows, 2, radial)
    partial_value = jnp.einsum(
        "stcr,psc->tpr", values, phase_table, precision=highest, preferred_element_type=jnp.float32
    )
    evolved = lax.psum_scatter(
        partial_value.astype(jnp.bfloat16), "sec", scatter_dimension=1, tiled=True
    ).astype(jnp.float32)
    return (evolved, new_state)


names = ("sec", "row", "col")


def natural_table(pair_total, sections, phi_count):
    slots = 2 * pair_total
    longitudes = sections * phi_count
    low = np.arange(pair_total)
    orders = np.stack([low, slots - 1 - low], axis=1).reshape(slots)
    turns = orders[:, None] * np.arange(longitudes)[None, :] % longitudes
    angle = turns * (2.0 * np.pi / longitudes)
    table = np.concatenate([np.cos(angle), -np.sin(angle)], axis=0) / np.sqrt(longitudes)
    return table.reshape(2 * slots, sections, phi_count).transpose(1, 0, 2).astype(np.float32)


def params(mib):
    return pltpu.CompilerParams(vmem_limit_bytes=mib * 1024 * 1024)


def vmem():
    return pl.BlockSpec(memory_space=pltpu.VMEM)


def smem():
    return pl.BlockSpec(memory_space=pltpu.SMEM)


def anywhere():
    return pl.BlockSpec(memory_space=pl.ANY)


def call(kernel, operands, out_shapes, mib=16, scalars=0, cost=None, scratch=()):
    single = not isinstance(out_shapes, (list, tuple))
    return pl.pallas_call(
        kernel,
        in_specs=[smem()] * scalars + [vmem()] * (len(operands) - scalars),
        out_specs=vmem() if single else [vmem()] * len(out_shapes),
        out_shape=out_shapes,
        scratch_shapes=scratch,
        compiler_params=params(mib),
        cost_estimate=cost,
    )(*operands)


four = range(4)


def plane_index():
    return lax.axis_index("row") % 2 * 2 + lax.axis_index("col")


def depth_index():
    return lax.axis_index("row") // 2


def pair_at(sec, deep, flat):
    row = lax.axis_index("row") ^ (2 * deep + flat // 2)
    col = lax.axis_index("col") ^ (flat % 2)
    at_sec = lax.axis_index("sec") ^ sec
    return (at_sec * lax.axis_size("row") + row) * lax.axis_size("col") + col


def exchange(array, sec=0, deep=0, flat=0):
    sizes = tuple(lax.axis_size(name) for name in names)
    pairs = []
    for source in np.ndindex(*sizes):
        target = (source[0] ^ sec, source[1] ^ (2 * deep + flat // 2), source[2] ^ (flat % 2))
        pairs.append(
            (int(np.ravel_multi_index(source, sizes)), int(np.ravel_multi_index(target, sizes)))
        )
    return lax.ppermute(array, names, pairs)


def cut_kernel(legendre_ref, *refs):
    outs, parts = refs[:-1], refs[-1]
    count, rows, lats = parts.shape
    given = legendre_ref.shape[1]
    parts[...] = jnp.zeros_like(parts)
    for at in range(count):
        parts[at, :given] = legendre_ref[0, :, at * lats : (at + 1) * lats]
    for deep, out in enumerate(outs):
        first = (depth_index() ^ deep) * 4
        out[...] = jnp.concatenate([parts[first + (plane_index() ^ flat)] for flat in four], axis=1)


def forward_kernel(
    orders_from, table_ref, grid_ref, keep_ref, send_ref, orders_ref, table, buffer, held, sems, more
):
    blocks, rows, lat_block, radial = held.shape
    slots = rows // 2

    def chunk(at):
        return pltpu.make_async_copy(
            grid_ref.at[pl.ds(2 * at, 2)], buffer.at[pl.ds(2 * at, 2)], sems.at[at]
        )

    table_copy = pltpu.make_async_copy(table_ref.at[lax.axis_index("sec")], table, more.at[0])
    orders_copy = pltpu.make_async_copy(orders_from, orders_ref, more.at[1])
    table_copy.start()
    orders_copy.start()
    for at in range(sems.shape[0]):
        chunk(at).start()
    table_copy.wait()

    def one_block(block, carry):
        for at in range(0, lat_block, 2):
            lat = block * lat_block + at
            chunk(lat // 2).wait()
            two = jnp.concatenate(
                [buffer[lat].astype(jnp.bfloat16), buffer[lat + 1].astype(jnp.bfloat16)], axis=1
            )
            sums = jnp.dot(table[...], two, preferred_element_type=jnp.float32)
            held[block, :, at, :] = sums[:, :radial]
            held[block, :, at + 1, :] = sums[:, radial:]
        return carry

    lax.fori_loop(0, blocks, one_block, 0)
    orders_copy.wait()
    for sec, out in ((1, send_ref), (0, keep_ref)):
        for flat, deep in np.ndindex(4, 4):
            order = orders_ref[pair_at(sec, deep, flat)]
            for part in range(2):
                values = held[:, pl.ds(part * slots + 2 * order, 2)].astype(out.dtype)
                for half in range(2):
                    out[flat, deep, half, :, pl.ds(part * radial, radial)] = values[
                        :, half
                    ].reshape(blocks * lat_block, radial)


def forward_sums(pair_orders, table, grid_terms, lat_block):
    sections, rows, phi_count = table.shape
    lat_rows, _, radial = grid_terms.shape
    sizes = (4, 4, 2, lat_rows, 2 * radial)
    in_memory = [pltpu.with_memory_space_constraint(x, pltpu.HBM) for x in (pair_orders, table)]
    return pl.pallas_call(
        forward_kernel,
        in_specs=[pl.BlockSpec(memory_space=pltpu.HBM)] * 2 + [anywhere()],
        out_specs=[vmem(), vmem()],
        out_shape=[
            jax.ShapeDtypeStruct(sizes, jnp.float32),
            jax.ShapeDtypeStruct(sizes, jnp.bfloat16),
        ],
        scratch_shapes=[
            pltpu.SMEM(pair_orders.shape, jnp.int32),
            pltpu.VMEM((rows, phi_count), table.dtype),
            pltpu.VMEM(grid_terms.shape, jnp.float32),
            pltpu.VMEM((lat_rows // lat_block, rows, lat_block, radial), jnp.float32),
            pltpu.SemaphoreType.DMA((lat_rows // 2,)),
            pltpu.SemaphoreType.DMA((2,)),
        ],
        compiler_params=params(36),
        cost_estimate=pl.CostEstimate(
            flops=2 * rows * phi_count * lat_rows * radial,
            bytes_accessed=4 * lat_rows * phi_count * radial,
            transcendentals=0,
        ),
    )(*in_memory, grid_terms)


def add_kernel(keep_ref, take_ref, *outs):
    for flat, out in enumerate(outs):
        out[...] = (keep_ref[flat] + take_ref[flat].astype(jnp.float32)).astype(out.dtype)


def masked(weights, order, degrees):
    row_index = lax.broadcasted_iota(jnp.int32, weights.shape, 0)
    leading = row_index < degrees - order
    zero = jnp.zeros_like(weights)
    return jnp.where(leading, weights, zero), jnp.where(leading, zero, weights)


def degrees_kernel(degrees, orders_ref, *refs):
    weights, takes, outs = refs[:4], refs[4:8], refs[8:]
    for deep in four:
        chosen = masked(weights[deep][...], orders_ref[pair_at(0, deep, 0)], degrees)
        total = 0.0
        for half in range(2):
            rows = jnp.concatenate([take[deep, half] for take in takes], axis=0)
            total += jnp.dot(chosen[half], rows, preferred_element_type=jnp.float32)
        outs[deep][...] = total.astype(outs[deep].dtype)


def synthesis_kernel(degrees, orders_ref, *refs):
    weights, fields, outs = refs[:4], refs[4:8], refs[8:]
    lat_rows = outs[0].shape[2]
    contract = (((0,), (0,)), ((), ()))
    for deep in four:
        chosen = masked(weights[deep][...], orders_ref[pair_at(0, deep, 0)], degrees)
        for half in range(2):
            values = lax.dot_general(
                chosen[half], fields[deep][...], contract, preferred_element_type=jnp.float32
            ).astype(jnp.bfloat16)
            for flat, out in enumerate(outs):
                out[deep, half] = values[flat * lat_rows : (flat + 1) * lat_rows]


def factor_kernel(degrees, orders_ref, kappa_ref, damping_ref, factor_ref):
    order = orders_ref[pair_at(0, 0, 0)]
    row_index = lax.broadcasted_iota(jnp.int32, factor_ref.shape, 0)
    degree = jnp.where(row_index < degrees - order, order + row_index, row_index - 1)
    degree = degree.astype(jnp.float32)
    factor_ref[...] = damping_ref[...] / (
        1.0 + kappa_ref[...] + degree * (degree + 1.0) / (degrees * degrees)
    )


def solve_kernel(one, two, three, last, state_ref, factor_ref, right_ref, left_ref, sent_ref):
    rows = state_ref.shape[1]
    radial = right_ref.shape[0]
    coefficient = one[...]
    for other in (two, three, last):
        coefficient += other[...].astype(jnp.float32)
    right_side = state_ref[0].astype(jnp.float32) + time_step * coefficient[:rows]
    right_side = right_side.astype(jnp.bfloat16)
    sent_ref[...] = jnp.zeros_like(sent_ref)
    for part in range(2):
        columns = pl.ds(part * radial, radial)
        eigen = jnp.dot(
            right_side[:, part * radial : (part + 1) * radial],
            right_ref[...],
            preferred_element_type=jnp.float32,
        )
        scaled = (eigen * factor_ref[...]).astype(jnp.bfloat16)
        field = jnp.dot(scaled, left_ref[...], preferred_element_type=jnp.float32)
        sent_ref[pl.ds(0, rows), columns] = field.astype(jnp.bfloat16)


def inverse_kernel(orders_ref, table_ref, *refs):
    takes, (out_ref, buffer, held, sems) = refs[:-4], refs[-4:]
    slot_rows, lat_block, radial = held.shape
    slots = slot_rows // 2
    table = table_ref[lax.axis_index("sec")]

    def chunk(at):
        return pltpu.make_async_copy(
            buffer.at[pl.ds(2 * at, 2)], out_ref.at[pl.ds(2 * at, 2)], sems.at[at]
        )

    def one_block(block, carry):
        begin = pl.multiple_of(block * lat_block, lat_block)
        for sec, flat, deep in np.ndindex(2, 4, 4):
            order = orders_ref[pair_at(sec, deep, flat)]
            for half, part in np.ndindex(2, 2):
                values = takes[4 * sec + flat][
                    deep, half, pl.ds(begin, lat_block), pl.ds(part * radial, radial)
                ]
                held[part * slots + 2 * order + half] = values.astype(jnp.float32)
        for at in range(0, lat_block, 2):
            two = jnp.concatenate(
                [held[:, at, :].astype(jnp.bfloat16), held[:, at + 1, :].astype(jnp.bfloat16)],
                axis=1,
            )
            values = jnp.dot(table, two, preferred_element_type=jnp.float32)
            lat = begin + at
            buffer[lat] = values[:, :radial]
            buffer[lat + 1] = values[:, radial:]
            chunk(lat // 2).start()
        return carry

    lax.fori_loop(0, buffer.shape[0] // lat_block, one_block, 0)
    for at in range(sems.shape[0]):
        chunk(at).wait()


def inverse_values(pair_orders, table, takes, lat_block):
    _, phi_count, slot_rows = table.shape
    lat_rows, radial = takes[0].shape[2], takes[0].shape[3] // 2
    out = jax.ShapeDtypeStruct((lat_rows, phi_count, radial), jnp.float32)
    return pl.pallas_call(
        inverse_kernel,
        in_specs=[smem()] + [vmem()] * (1 + len(takes)),
        out_specs=anywhere(),
        out_shape=out,
        scratch_shapes=[
            pltpu.VMEM(out.shape, jnp.float32),
            pltpu.VMEM((slot_rows, lat_block, radial), jnp.float32),
            pltpu.SemaphoreType.DMA((lat_rows // 2,)),
        ],
        compiler_params=params(36),
        cost_estimate=pl.CostEstimate(
            flops=2 * slot_rows * phi_count * lat_rows * radial,
            bytes_accessed=4 * lat_rows * phi_count * radial,
            transcendentals=0,
        ),
    )(pair_orders, table, *takes)


def on_device_compact(grid_terms, pair_orders, legendre, state, kappa, right_op, left_op):
    lat_rows, phi_count, radial = grid_terms.shape
    rows = legendre.shape[1]
    degrees = rows - 1
    padded = -(-rows // 8) * 8
    columns = 2 * radial
    pair_total = pair_orders.shape[0]
    table = natural_table(pair_total, lax.axis_size("sec"), phi_count)
    forward_table = jnp.asarray(table, jnp.bfloat16)
    inverse_table = jnp.asarray(table.transpose(0, 2, 1), jnp.bfloat16)

    def shape(*sizes, dtype=jnp.bfloat16):
        return jax.ShapeDtypeStruct(sizes, dtype)

    slab = shape(padded, 4 * lat_rows)
    cuts = call(
        cut_kernel,
        [legendre],
        [slab] * 4,
        scratch=[pltpu.VMEM((16, padded, lat_rows), jnp.bfloat16)],
    )
    near = exchange(cuts[1], deep=1)

    keep, send = forward_sums(pair_orders, forward_table, grid_terms, 8)
    block = shape(4, 2, lat_rows, columns)
    taken, near = lax.optimization_barrier((exchange(send, sec=1), near))
    blocks = call(add_kernel, [keep, taken], [block] * 4, mib=24)
    weights = [cuts[0], near] + [exchange(cuts[deep], deep=deep) for deep in (2, 3)]
    takes = [blocks[0]] + [exchange(blocks[flat], flat=flat) for flat in (1, 2, 3)]

    sums = call(
        functools.partial(degrees_kernel, degrees),
        [pair_orders, *weights, *takes],
        [shape(padded, columns, dtype=jnp.float32)] + [shape(padded, columns)] * 3,
        scalars=1,
    )
    sums = [sums[0]] + [exchange(sums[deep], deep=deep) for deep in (3, 2, 1)]

    radial_mode = np.arange(radial, dtype=np.float32) / np.float32(radial)
    damping = np.exp(-filter_strength * radial_mode**filter_power).astype(np.float32)
    factor = call(
        functools.partial(factor_kernel, degrees),
        [pair_orders, kappa[None, :], jnp.asarray(damping)[None, :]],
        shape(rows, radial, dtype=jnp.float32),
        scalars=1,
    )
    field = call(
        solve_kernel, [*sums, state, factor, right_op, left_op], shape(padded, columns)
    )
    new_state = field[None, :rows]

    fields = [field] + [exchange(field, deep=deep) for deep in (1, 2, 3)]
    blocks = call(
        functools.partial(synthesis_kernel, degrees),
        [pair_orders, *weights, *fields],
        [block] * 4,
        scalars=1,
    )
    takes = [blocks[0]] + [exchange(blocks[flat], flat=flat) for flat in (1, 2, 3)]
    takes += [exchange(take, sec=1) for take in takes]
    evolved = inverse_values(pair_orders, inverse_table, takes, 16)
    return (evolved, new_state)


def on_device(*args):
    lat_rows = args[0].shape[0]
    rows = args[2].shape[1]
    sections, side_row, side_x = (lax.axis_size(name) for name in names)
    fits = args[2].shape[0] == 1 and lat_rows % 16 == 0 and rows <= 2 * lat_rows
    fits = fits and args[0].size * 4 <= 24 * 1024 * 1024
    fits = fits and (sections, side_row, side_x) == (2, 8, 2)
    return on_device_compact(*args) if fits else on_device_wide(*args)


def solution(mesh):
    return jax.shard_map(
        on_device,
        mesh=mesh,
        in_specs=(
            P(("row", "col"), "sec", None),
            P(),
            P(("sec", "row", "col"), None, None),
            P(("sec", "row", "col"), None, None),
            P(),
            P(),
            P(),
        ),
        out_specs=(P(("row", "col"), "sec", None), P(("sec", "row", "col"), None, None)),
        check_vma=False,
    )
```

```python
import functools
import math

import jax
import jax.numpy as jnp
import numpy as np
from jax import lax
from jax.experimental import pallas as pl
from jax.experimental.pallas import tpu as pltpu
from jax.sharding import PartitionSpec as P

time_step = 0.5
filter_strength = 36.0
filter_power = 36.0


def slot_orders_of(pair_orders):
    order_total = 2 * pair_orders.shape[0]
    return jnp.stack([pair_orders, order_total - 1 - pair_orders], axis=1).reshape(order_total)


def fourier_table(orders, phi_start, phi_count, longitudes):
    longitude = phi_start + lax.iota(jnp.int32, phi_count)
    phase_turns = longitude[:, None] * orders[None, :] % longitudes
    phase_angle = phase_turns.astype(jnp.float32) * (2.0 * math.pi / longitudes)
    norm_scale = 1.0 / math.sqrt(longitudes)
    return jnp.stack(
        [jnp.cos(phase_angle) * norm_scale, -jnp.sin(phase_angle) * norm_scale], axis=-1
    )


def on_device_wide(grid_terms, pair_orders, legendre, state, kappa, right_op, left_op):
    lat_rows, phi_count, radial = grid_terms.shape
    pairs_here = legendre.shape[0]
    degrees = legendre.shape[1] - 1
    latitudes = legendre.shape[2]
    sections = lax.axis_size("sec")
    longitudes = phi_count * sections
    columns = 2 * radial
    section_slots = degrees // sections
    orders = slot_orders_of(pair_orders)
    sec_index = lax.axis_index("sec")
    highest = lax.Precision.HIGHEST
    phi_start = sec_index * phi_count
    sub_orders = orders
    phase_table = fourier_table(sub_orders, phi_start, phi_count, longitudes)
    term = jnp.einsum(
        "tpr,psc->stcr",
        grid_terms,
        phase_table,
        precision=highest,
        preferred_element_type=jnp.float32,
    )
    spectral = lax.psum_scatter(
        term.reshape(section_slots * lax.axis_size("sec"), lat_rows, columns),
        "sec",
        scatter_dimension=0,
        tiled=True,
    ).astype(jnp.bfloat16)
    device = lax.axis_index(("sec", "row", "col"))
    local_orders = lax.dynamic_slice_in_dim(pair_orders, device * pairs_here, pairs_here)
    row_index = lax.iota(jnp.int32, degrees + 1)
    leading = row_index[None, :] < (degrees - local_orders)[:, None]
    degree = jnp.where(leading, local_orders[:, None] + row_index[None, :], row_index[None, :] - 1)
    received = lax.all_to_all(spectral, ("row", "col"), split_axis=0, concat_axis=1, tiled=True)
    item_count = received.shape[2]
    paired = received.reshape(pairs_here, 2, latitudes, item_count)
    both_orders = jnp.einsum("pit,potx->piox", legendre, paired, preferred_element_type=jnp.float32)
    coefficient = jnp.where(leading[:, :, None], both_orders[:, :, 0], both_orders[:, :, 1])
    right_side = (state.astype(jnp.float32) + time_step * coefficient).astype(jnp.bfloat16)
    right_side = right_side.reshape(pairs_here, degrees + 1, 2, radial)
    eigen_part = jnp.einsum(
        "picr,rk->pick", right_side, right_op, preferred_element_type=jnp.float32
    )
    radial_mode = lax.iota(jnp.float32, radial) / radial
    damping = jnp.exp(-filter_strength * radial_mode**filter_power)
    degree_wide = degree.astype(jnp.float32)
    degree_term = degree_wide * (degree_wide + 1.0) / (degrees * degrees)
    factor = damping[None, None, :] / (1.0 + kappa[None, None, :] + degree_term[:, :, None])
    scaled = (eigen_part * factor[:, :, None, :]).astype(jnp.bfloat16)
    new_state = jnp.einsum("pick,kr->picr", scaled, left_op, preferred_element_type=jnp.float32)
    new_state = new_state.astype(jnp.bfloat16).reshape(pairs_here, degrees + 1, columns)
    zero_rows = jnp.zeros_like(new_state)
    split_state = jnp.stack(
        [
            jnp.where(leading[:, :, None], new_state, zero_rows),
            jnp.where(leading[:, :, None], zero_rows, new_state),
        ],
        axis=1,
    )
    synthesis_wide = jnp.einsum(
        "pit,poix->potx", legendre, split_state, preferred_element_type=jnp.float32
    )
    synthesis = synthesis_wide.astype(jnp.bfloat16).reshape(2 * pairs_here, latitudes, columns)
    returned = lax.all_to_all(synthesis, ("row", "col"), split_axis=1, concat_axis=0, tiled=True)
    sub_orders = lax.dynamic_slice_in_dim(orders, sec_index * section_slots, section_slots)
    phase_table = fourier_table(sub_orders, 0, longitudes, longitudes)
    values = returned.astype(jnp.float32).reshape(section_slots, lat_rows, 2, radial)
    partial_value = jnp.einsum(
        "stcr,psc->tpr", values, phase_table, precision=highest, preferred_element_type=jnp.float32
    )
    evolved = lax.psum_scatter(
        partial_value.astype(jnp.bfloat16), "sec", scatter_dimension=1, tiled=True
    ).astype(jnp.float32)
    return (evolved, new_state)


names = ("sec", "row", "col")


def natural_table(pair_total, sections, phi_count):
    slots = 2 * pair_total
    longitudes = sections * phi_count
    low = np.arange(pair_total)
    orders = np.stack([low, slots - 1 - low], axis=1).reshape(slots)
    turns = orders[:, None] * np.arange(longitudes)[None, :] % longitudes
    angle = turns * (2.0 * np.pi / longitudes)
    table = np.concatenate([np.cos(angle), -np.sin(angle)], axis=0) / np.sqrt(longitudes)
    return table.reshape(2 * slots, sections, phi_count).transpose(1, 0, 2).astype(np.float32)


def params(mib):
    return pltpu.CompilerParams(vmem_limit_bytes=mib * 1024 * 1024)


def vmem():
    return pl.BlockSpec(memory_space=pltpu.VMEM)


def smem():
    return pl.BlockSpec(memory_space=pltpu.SMEM)


def anywhere():
    return pl.BlockSpec(memory_space=pl.ANY)


def call(kernel, operands, out_shapes, mib=16, scalars=0, cost=None, scratch=()):
    single = not isinstance(out_shapes, (list, tuple))
    return pl.pallas_call(
        kernel,
        in_specs=[smem()] * scalars + [vmem()] * (len(operands) - scalars),
        out_specs=vmem() if single else [vmem()] * len(out_shapes),
        out_shape=out_shapes,
        scratch_shapes=scratch,
        compiler_params=params(mib),
        cost_estimate=cost,
    )(*operands)


four = range(4)


def plane_index():
    return lax.axis_index("row") % 2 * 2 + lax.axis_index("col")


def depth_index():
    return lax.axis_index("row") // 2


def pair_at(sec, deep, flat):
    row = lax.axis_index("row") ^ (2 * deep + flat // 2)
    col = lax.axis_index("col") ^ (flat % 2)
    at_sec = lax.axis_index("sec") ^ sec
    return (at_sec * lax.axis_size("row") + row) * lax.axis_size("col") + col


def exchange(array, sec=0, deep=0, flat=0):
    sizes = tuple(lax.axis_size(name) for name in names)
    pairs = []
    for source in np.ndindex(*sizes):
        target = (source[0] ^ sec, source[1] ^ (2 * deep + flat // 2), source[2] ^ (flat % 2))
        pairs.append(
            (int(np.ravel_multi_index(source, sizes)), int(np.ravel_multi_index(target, sizes)))
        )
    return lax.ppermute(array, names, pairs)


def cut_kernel(legendre_ref, *refs):
    outs, parts = refs[:-1], refs[-1]
    count, rows, lats = parts.shape
    given = legendre_ref.shape[1]
    parts[...] = jnp.zeros_like(parts)
    for at in range(count):
        parts[at, :given] = legendre_ref[0, :, at * lats : (at + 1) * lats]
    for deep, out in enumerate(outs):
        first = (depth_index() ^ deep) * 4
        out[...] = jnp.concatenate([parts[first + (plane_index() ^ flat)] for flat in four], axis=1)


def arrange_kernel(sec, orders_ref, held, out_ref):
    blocks, rows, lat_block, radial = held.shape
    slots = rows // 2
    for flat, deep in np.ndindex(4, 4):
        order = orders_ref[pair_at(sec, deep, flat)]
        for part in range(2):
            values = held[:, pl.ds(part * slots + 2 * order, 2)].astype(out_ref.dtype)
            for half in range(2):
                out_ref[flat, deep, half, :, pl.ds(part * radial, radial)] = values[
                    :, half
                ].reshape(blocks * lat_block, radial)


def forward_kernel(
    orders_from, table_ref, grid_ref, held, send_ref, orders_ref, wide, table, buffer, sems, more
):
    blocks, rows, lat_block, radial = held.shape

    def chunk(at):
        return pltpu.make_async_copy(
            grid_ref.at[pl.ds(2 * at, 2)], buffer.at[pl.ds(2 * at, 2)], sems.at[at]
        )

    table_copy = pltpu.make_async_copy(table_ref.at[lax.axis_index("sec")], wide, more.at[0])
    orders_copy = pltpu.make_async_copy(orders_from, orders_ref, more.at[1])
    table_copy.start()
    orders_copy.start()
    for at in range(sems.shape[0]):
        chunk(at).start()
    table_copy.wait()
    table[...] = wide[...].astype(table.dtype)

    def one_block(block, carry):
        for at in range(0, lat_block, 2):
            lat = block * lat_block + at
            chunk(lat // 2).wait()
            two = jnp.concatenate(
                [buffer[lat].astype(jnp.bfloat16), buffer[lat + 1].astype(jnp.bfloat16)], axis=1
            )
            sums = jnp.dot(table[...], two, preferred_element_type=jnp.float32)
            held[block, :, at, :] = sums[:, :radial]
            held[block, :, at + 1, :] = sums[:, radial:]
        return carry

    lax.fori_loop(0, blocks, one_block, 0)
    orders_copy.wait()
    arrange_kernel(1, orders_ref, held, send_ref)


def forward_sums(pair_orders, table, grid_terms, lat_block):
    sections, rows, phi_count = table.shape
    lat_rows, _, radial = grid_terms.shape
    sizes = (4, 4, 2, lat_rows, 2 * radial)
    in_memory = [pltpu.with_memory_space_constraint(x, pltpu.HBM) for x in (pair_orders, table)]
    return pl.pallas_call(
        forward_kernel,
        in_specs=[pl.BlockSpec(memory_space=pltpu.HBM)] * 2 + [anywhere()],
        out_specs=[vmem(), vmem()],
        out_shape=[
            jax.ShapeDtypeStruct((lat_rows // lat_block, rows, lat_block, radial), jnp.float32),
            jax.ShapeDtypeStruct(sizes, jnp.bfloat16),
        ],
        scratch_shapes=[
            pltpu.SMEM(pair_orders.shape, jnp.int32),
            pltpu.VMEM((rows, phi_count), jnp.float32),
            pltpu.VMEM((rows, phi_count), jnp.bfloat16),
            pltpu.VMEM(grid_terms.shape, jnp.float32),
            pltpu.SemaphoreType.DMA((lat_rows // 2,)),
            pltpu.SemaphoreType.DMA((2,)),
        ],
        compiler_params=params(36),
        cost_estimate=pl.CostEstimate(
            flops=2 * rows * phi_count * lat_rows * radial,
            bytes_accessed=4 * lat_rows * phi_count * radial,
            transcendentals=0,
        ),
    )(*in_memory, grid_terms)


def add_kernel(keep_ref, take_ref, *outs):
    for flat, out in enumerate(outs):
        out[...] = (keep_ref[flat] + take_ref[flat].astype(jnp.float32)).astype(out.dtype)


def masked(weights, order, degrees):
    row_index = lax.broadcasted_iota(jnp.int32, weights.shape, 0)
    leading = row_index < degrees - order
    zero = jnp.zeros_like(weights)
    return jnp.where(leading, weights, zero), jnp.where(leading, zero, weights)


def degrees_kernel(degrees, orders_ref, *refs):
    weights, takes, outs = refs[:4], refs[4:8], refs[8:]
    for deep in four:
        chosen = masked(weights[deep][...], orders_ref[pair_at(0, deep, 0)], degrees)
        total = 0.0
        for half in range(2):
            rows = jnp.concatenate([take[deep, half] for take in takes], axis=0)
            total += jnp.dot(chosen[half], rows, preferred_element_type=jnp.float32)
        outs[deep][...] = total.astype(outs[deep].dtype)


def synthesis_kernel(degrees, orders_ref, *refs):
    weights, fields, outs = refs[:4], refs[4:8], refs[8:]
    lat_rows = outs[0].shape[2]
    contract = (((0,), (0,)), ((), ()))
    for deep in four:
        chosen = masked(weights[deep][...], orders_ref[pair_at(0, deep, 0)], degrees)
        for half in range(2):
            values = lax.dot_general(
                chosen[half], fields[deep][...], contract, preferred_element_type=jnp.float32
            ).astype(jnp.bfloat16)
            for flat, out in enumerate(outs):
                out[deep, half] = values[flat * lat_rows : (flat + 1) * lat_rows]


def factor_kernel(degrees, orders_ref, kappa_ref, damping_ref, factor_ref):
    order = orders_ref[pair_at(0, 0, 0)]
    row_index = lax.broadcasted_iota(jnp.int32, factor_ref.shape, 0)
    degree = jnp.where(row_index < degrees - order, order + row_index, row_index - 1)
    degree = degree.astype(jnp.float32)
    factor_ref[...] = damping_ref[...] / (
        1.0 + kappa_ref[...] + degree * (degree + 1.0) / (degrees * degrees)
    )


def solve_kernel(one, two, three, last, state_ref, factor_ref, right_ref, left_ref, sent_ref):
    rows = state_ref.shape[1]
    radial = right_ref.shape[0]
    coefficient = one[...]
    for other in (two, three, last):
        coefficient += other[...].astype(jnp.float32)
    right_side = state_ref[0].astype(jnp.float32) + time_step * coefficient[:rows]
    right_side = right_side.astype(jnp.bfloat16)
    sent_ref[...] = jnp.zeros_like(sent_ref)
    for part in range(2):
        columns = pl.ds(part * radial, radial)
        eigen = jnp.dot(
            right_side[:, part * radial : (part + 1) * radial],
            right_ref[...],
            preferred_element_type=jnp.float32,
        )
        scaled = (eigen * factor_ref[...]).astype(jnp.bfloat16)
        field = jnp.dot(scaled, left_ref[...], preferred_element_type=jnp.float32)
        sent_ref[pl.ds(0, rows), columns] = field.astype(jnp.bfloat16)


def inverse_kernel(orders_ref, table_ref, *refs):
    takes, (out_ref, buffer, held, sems) = refs[:-4], refs[-4:]
    slot_rows, lat_block, radial = held.shape
    slots = slot_rows // 2
    table = table_ref[lax.axis_index("sec")]

    def chunk(at):
        return pltpu.make_async_copy(
            buffer.at[pl.ds(2 * at, 2)], out_ref.at[pl.ds(2 * at, 2)], sems.at[at]
        )

    def one_block(block, carry):
        begin = pl.multiple_of(block * lat_block, lat_block)
        for sec, flat, deep in np.ndindex(2, 4, 4):
            order = orders_ref[pair_at(sec, deep, flat)]
            for half, part in np.ndindex(2, 2):
                values = takes[4 * sec + flat][
                    deep, half, pl.ds(begin, lat_block), pl.ds(part * radial, radial)
                ]
                held[part * slots + 2 * order + half] = values.astype(jnp.float32)
        for at in range(0, lat_block, 2):
            two = jnp.concatenate(
                [held[:, at, :].astype(jnp.bfloat16), held[:, at + 1, :].astype(jnp.bfloat16)],
                axis=1,
            )
            values = jnp.dot(table, two, preferred_element_type=jnp.float32)
            lat = begin + at
            buffer[lat] = values[:, :radial]
            buffer[lat + 1] = values[:, radial:]
            chunk(lat // 2).start()
        return carry

    lax.fori_loop(0, buffer.shape[0] // lat_block, one_block, 0)
    for at in range(sems.shape[0]):
        chunk(at).wait()


def inverse_values(pair_orders, table, takes, lat_block):
    _, phi_count, slot_rows = table.shape
    lat_rows, radial = takes[0].shape[2], takes[0].shape[3] // 2
    out = jax.ShapeDtypeStruct((lat_rows, phi_count, radial), jnp.float32)
    return pl.pallas_call(
        inverse_kernel,
        in_specs=[smem()] + [vmem()] * (1 + len(takes)),
        out_specs=anywhere(),
        out_shape=out,
        scratch_shapes=[
            pltpu.VMEM(out.shape, jnp.float32),
            pltpu.VMEM((slot_rows, lat_block, radial), jnp.float32),
            pltpu.SemaphoreType.DMA((lat_rows // 2,)),
        ],
        compiler_params=params(36),
        cost_estimate=pl.CostEstimate(
            flops=2 * slot_rows * phi_count * lat_rows * radial,
            bytes_accessed=4 * lat_rows * phi_count * radial,
            transcendentals=0,
        ),
    )(pair_orders, table, *takes)


def on_device_compact(grid_terms, pair_orders, legendre, state, kappa, right_op, left_op):
    lat_rows, phi_count, radial = grid_terms.shape
    rows = legendre.shape[1]
    degrees = rows - 1
    padded = -(-rows // 8) * 8
    columns = 2 * radial
    pair_total = pair_orders.shape[0]
    table = natural_table(pair_total, lax.axis_size("sec"), phi_count)
    forward_table = jnp.asarray(table)
    inverse_table = jnp.asarray(table.transpose(0, 2, 1), jnp.bfloat16)

    def shape(*sizes, dtype=jnp.bfloat16):
        return jax.ShapeDtypeStruct(sizes, dtype)

    slab = shape(padded, 4 * lat_rows)
    cuts = call(
        cut_kernel,
        [legendre],
        [slab] * 4,
        scratch=[pltpu.VMEM((16, padded, lat_rows), jnp.bfloat16)],
    )
    weights = [cuts[0]] + [exchange(cuts[deep], deep=deep) for deep in (1, 2, 3)]

    held, send = forward_sums(pair_orders, forward_table, grid_terms, 8)
    block = shape(4, 2, lat_rows, columns)
    taken = exchange(send, sec=1)
    sizes = (4, 4, 2, lat_rows, columns)
    keep = call(
        functools.partial(arrange_kernel, 0),
        [pair_orders, held],
        shape(*sizes, dtype=jnp.float32),
        mib=24,
        scalars=1,
    )
    blocks = call(add_kernel, [keep, taken], [block] * 4, mib=24)
    takes = [blocks[0]] + [exchange(blocks[flat], flat=flat) for flat in (1, 2, 3)]

    sums = call(
        functools.partial(degrees_kernel, degrees),
        [pair_orders, *weights, *takes],
        [shape(padded, columns, dtype=jnp.float32)] + [shape(padded, columns)] * 3,
        scalars=1,
    )
    sums = [sums[0]] + [exchange(sums[deep], deep=deep) for deep in (3, 2, 1)]

    radial_mode = np.arange(radial, dtype=np.float32) / np.float32(radial)
    damping = np.exp(-filter_strength * radial_mode**filter_power).astype(np.float32)
    factor = call(
        functools.partial(factor_kernel, degrees),
        [pair_orders, kappa[None, :], jnp.asarray(damping)[None, :]],
        shape(rows, radial, dtype=jnp.float32),
        scalars=1,
    )
    field = call(
        solve_kernel, [*sums, state, factor, right_op, left_op], shape(padded, columns)
    )
    new_state = field[None, :rows]

    moved, new_state = lax.optimization_barrier((exchange(field, deep=1), new_state))
    fields = [field, moved] + [exchange(field, deep=deep) for deep in (2, 3)]
    blocks = call(
        functools.partial(synthesis_kernel, degrees),
        [pair_orders, *weights, *fields],
        [block] * 4,
        scalars=1,
    )
    takes = [blocks[0]] + [exchange(blocks[flat], flat=flat) for flat in (1, 2, 3)]
    takes += [exchange(take, sec=1) for take in takes]
    evolved = inverse_values(pair_orders, inverse_table, takes, 16)
    return (evolved, new_state)


def on_device(*args):
    lat_rows = args[0].shape[0]
    rows = args[2].shape[1]
    sections, side_row, side_x = (lax.axis_size(name) for name in names)
    fits = args[2].shape[0] == 1 and lat_rows % 16 == 0 and rows <= 2 * lat_rows
    fits = fits and args[0].size * 4 <= 24 * 1024 * 1024
    fits = fits and (sections, side_row, side_x) == (2, 8, 2)
    return on_device_compact(*args) if fits else on_device_wide(*args)


def solution(mesh):
    return jax.shard_map(
        on_device,
        mesh=mesh,
        in_specs=(
            P(("row", "col"), "sec", None),
            P(),
            P(("sec", "row", "col"), None, None),
            P(("sec", "row", "col"), None, None),
            P(),
            P(),
            P(),
        ),
        out_specs=(P(("row", "col"), "sec", None), P(("sec", "row", "col"), None, None)),
        check_vma=False,
    )
```

```python
import functools
import math

import jax
import jax.numpy as jnp
import numpy as np
from jax import lax
from jax.experimental import pallas as pl
from jax.experimental.pallas import tpu as pltpu
from jax.sharding import PartitionSpec as P

time_step = 0.5
filter_strength = 36.0
filter_power = 36.0


def slot_orders_of(pair_orders):
    order_total = 2 * pair_orders.shape[0]
    return jnp.stack([pair_orders, order_total - 1 - pair_orders], axis=1).reshape(order_total)


def fourier_table(orders, phi_start, phi_count, longitudes):
    longitude = phi_start + lax.iota(jnp.int32, phi_count)
    phase_turns = longitude[:, None] * orders[None, :] % longitudes
    phase_angle = phase_turns.astype(jnp.float32) * (2.0 * math.pi / longitudes)
    norm_scale = 1.0 / math.sqrt(longitudes)
    return jnp.stack(
        [jnp.cos(phase_angle) * norm_scale, -jnp.sin(phase_angle) * norm_scale], axis=-1
    )


def on_device_wide(grid_terms, pair_orders, legendre, state, kappa, right_op, left_op):
    lat_rows, phi_count, radial = grid_terms.shape
    pairs_here = legendre.shape[0]
    degrees = legendre.shape[1] - 1
    latitudes = legendre.shape[2]
    sections = lax.axis_size("sec")
    longitudes = phi_count * sections
    columns = 2 * radial
    section_slots = degrees // sections
    orders = slot_orders_of(pair_orders)
    sec_index = lax.axis_index("sec")
    highest = lax.Precision.HIGHEST
    phi_start = sec_index * phi_count
    sub_orders = orders
    phase_table = fourier_table(sub_orders, phi_start, phi_count, longitudes)
    term = jnp.einsum(
        "tpr,psc->stcr",
        grid_terms,
        phase_table,
        precision=highest,
        preferred_element_type=jnp.float32,
    )
    spectral = lax.psum_scatter(
        term.reshape(section_slots * lax.axis_size("sec"), lat_rows, columns),
        "sec",
        scatter_dimension=0,
        tiled=True,
    ).astype(jnp.bfloat16)
    device = lax.axis_index(("sec", "row", "col"))
    local_orders = lax.dynamic_slice_in_dim(pair_orders, device * pairs_here, pairs_here)
    row_index = lax.iota(jnp.int32, degrees + 1)
    leading = row_index[None, :] < (degrees - local_orders)[:, None]
    degree = jnp.where(leading, local_orders[:, None] + row_index[None, :], row_index[None, :] - 1)
    received = lax.all_to_all(spectral, ("row", "col"), split_axis=0, concat_axis=1, tiled=True)
    item_count = received.shape[2]
    paired = received.reshape(pairs_here, 2, latitudes, item_count)
    both_orders = jnp.einsum("pit,potx->piox", legendre, paired, preferred_element_type=jnp.float32)
    coefficient = jnp.where(leading[:, :, None], both_orders[:, :, 0], both_orders[:, :, 1])
    right_side = (state.astype(jnp.float32) + time_step * coefficient).astype(jnp.bfloat16)
    right_side = right_side.reshape(pairs_here, degrees + 1, 2, radial)
    eigen_part = jnp.einsum(
        "picr,rk->pick", right_side, right_op, preferred_element_type=jnp.float32
    )
    radial_mode = lax.iota(jnp.float32, radial) / radial
    damping = jnp.exp(-filter_strength * radial_mode**filter_power)
    degree_wide = degree.astype(jnp.float32)
    degree_term = degree_wide * (degree_wide + 1.0) / (degrees * degrees)
    factor = damping[None, None, :] / (1.0 + kappa[None, None, :] + degree_term[:, :, None])
    scaled = (eigen_part * factor[:, :, None, :]).astype(jnp.bfloat16)
    new_state = jnp.einsum("pick,kr->picr", scaled, left_op, preferred_element_type=jnp.float32)
    new_state = new_state.astype(jnp.bfloat16).reshape(pairs_here, degrees + 1, columns)
    zero_rows = jnp.zeros_like(new_state)
    split_state = jnp.stack(
        [
            jnp.where(leading[:, :, None], new_state, zero_rows),
            jnp.where(leading[:, :, None], zero_rows, new_state),
        ],
        axis=1,
    )
    synthesis_wide = jnp.einsum(
        "pit,poix->potx", legendre, split_state, preferred_element_type=jnp.float32
    )
    synthesis = synthesis_wide.astype(jnp.bfloat16).reshape(2 * pairs_here, latitudes, columns)
    returned = lax.all_to_all(synthesis, ("row", "col"), split_axis=1, concat_axis=0, tiled=True)
    sub_orders = lax.dynamic_slice_in_dim(orders, sec_index * section_slots, section_slots)
    phase_table = fourier_table(sub_orders, 0, longitudes, longitudes)
    values = returned.astype(jnp.float32).reshape(section_slots, lat_rows, 2, radial)
    partial_value = jnp.einsum(
        "stcr,psc->tpr", values, phase_table, precision=highest, preferred_element_type=jnp.float32
    )
    evolved = lax.psum_scatter(
        partial_value.astype(jnp.bfloat16), "sec", scatter_dimension=1, tiled=True
    ).astype(jnp.float32)
    return (evolved, new_state)


names = ("sec", "row", "col")


def natural_table(pair_total, sections, phi_count):
    slots = 2 * pair_total
    longitudes = sections * phi_count
    low = np.arange(pair_total)
    orders = np.stack([low, slots - 1 - low], axis=1).reshape(slots)
    turns = orders[:, None] * np.arange(longitudes)[None, :] % longitudes
    angle = turns * (2.0 * np.pi / longitudes)
    table = np.concatenate([np.cos(angle), -np.sin(angle)], axis=0) / np.sqrt(longitudes)
    return table.reshape(2 * slots, sections, phi_count).transpose(1, 0, 2).astype(np.float32)


def params(mib):
    return pltpu.CompilerParams(vmem_limit_bytes=mib * 1024 * 1024)


def vmem():
    return pl.BlockSpec(memory_space=pltpu.VMEM)


def smem():
    return pl.BlockSpec(memory_space=pltpu.SMEM)


def anywhere():
    return pl.BlockSpec(memory_space=pl.ANY)


def call(kernel, operands, out_shapes, mib=16, scalars=0, cost=None, scratch=()):
    single = not isinstance(out_shapes, (list, tuple))
    return pl.pallas_call(
        kernel,
        in_specs=[smem()] * scalars + [vmem()] * (len(operands) - scalars),
        out_specs=vmem() if single else [vmem()] * len(out_shapes),
        out_shape=out_shapes,
        scratch_shapes=scratch,
        compiler_params=params(mib),
        cost_estimate=cost,
    )(*operands)


four = range(4)


def plane_index():
    return lax.axis_index("row") % 2 * 2 + lax.axis_index("col")


def depth_index():
    return lax.axis_index("row") // 2


def pair_at(sec, deep, flat):
    row = lax.axis_index("row") ^ (2 * deep + flat // 2)
    col = lax.axis_index("col") ^ (flat % 2)
    at_sec = lax.axis_index("sec") ^ sec
    return (at_sec * lax.axis_size("row") + row) * lax.axis_size("col") + col


def exchange(array, sec=0, deep=0, flat=0):
    sizes = tuple(lax.axis_size(name) for name in names)
    pairs = []
    for source in np.ndindex(*sizes):
        target = (source[0] ^ sec, source[1] ^ (2 * deep + flat // 2), source[2] ^ (flat % 2))
        pairs.append(
            (int(np.ravel_multi_index(source, sizes)), int(np.ravel_multi_index(target, sizes)))
        )
    return lax.ppermute(array, names, pairs)


def cut_kernel(legendre_ref, *refs):
    outs, parts = refs[:-1], refs[-1]
    count, rows, lats = parts.shape
    given = legendre_ref.shape[1]
    parts[...] = jnp.zeros_like(parts)
    for at in range(count):
        parts[at, :given] = legendre_ref[0, :, at * lats : (at + 1) * lats]
    for deep, out in enumerate(outs):
        first = (depth_index() ^ deep) * 4
        out[...] = jnp.concatenate([parts[first + (plane_index() ^ flat)] for flat in four], axis=1)


def arrange_kernel(sec, orders_ref, held, out_ref):
    blocks, rows, lat_block, radial = held.shape
    slots = rows // 2
    for flat, deep in np.ndindex(4, 4):
        order = orders_ref[pair_at(sec, deep, flat)]
        for part in range(2):
            values = held[:, pl.ds(part * slots + 2 * order, 2)].astype(out_ref.dtype)
            for half in range(2):
                out_ref[flat, deep, half, :, pl.ds(part * radial, radial)] = values[
                    :, half
                ].reshape(blocks * lat_block, radial)


def forward_kernel(table_ref, grid_ref, held, buffer, sems):
    blocks, rows, lat_block, radial = held.shape

    def chunk(at):
        return pltpu.make_async_copy(
            grid_ref.at[pl.ds(2 * at, 2)], buffer.at[pl.ds(2 * at, 2)], sems.at[at]
        )

    for at in range(sems.shape[0]):
        chunk(at).start()
    table = table_ref[lax.axis_index("sec")]

    def one_block(block, carry):
        for at in range(0, lat_block, 2):
            lat = block * lat_block + at
            chunk(lat // 2).wait()
            two = jnp.concatenate(
                [buffer[lat].astype(jnp.bfloat16), buffer[lat + 1].astype(jnp.bfloat16)], axis=1
            )
            sums = jnp.dot(table, two, preferred_element_type=jnp.float32)
            held[block, :, at, :] = sums[:, :radial]
            held[block, :, at + 1, :] = sums[:, radial:]
        return carry

    lax.fori_loop(0, blocks, one_block, 0)


def forward_sums(table, grid_terms, lat_block):
    sections, rows, phi_count = table.shape
    lat_rows, _, radial = grid_terms.shape
    return pl.pallas_call(
        forward_kernel,
        in_specs=[vmem(), anywhere()],
        out_specs=vmem(),
        out_shape=jax.ShapeDtypeStruct((lat_rows // lat_block, rows, lat_block, radial), jnp.float32),
        scratch_shapes=[
            pltpu.VMEM(grid_terms.shape, jnp.float32),
            pltpu.SemaphoreType.DMA((lat_rows // 2,)),
        ],
        compiler_params=params(36),
        cost_estimate=pl.CostEstimate(
            flops=2 * rows * phi_count * lat_rows * radial,
            bytes_accessed=4 * lat_rows * phi_count * radial,
            transcendentals=0,
        ),
    )(table, grid_terms)


def add_kernel(keep_ref, take_ref, *outs):
    for flat, out in enumerate(outs):
        out[...] = (keep_ref[flat] + take_ref[flat].astype(jnp.float32)).astype(out.dtype)


def masked(weights, order, degrees):
    row_index = lax.broadcasted_iota(jnp.int32, weights.shape, 0)
    leading = row_index < degrees - order
    zero = jnp.zeros_like(weights)
    return jnp.where(leading, weights, zero), jnp.where(leading, zero, weights)


def degrees_kernel(degrees, orders_ref, *refs):
    weights, takes, outs = refs[:4], refs[4:8], refs[8:]
    for deep in four:
        chosen = masked(weights[deep][...], orders_ref[pair_at(0, deep, 0)], degrees)
        total = 0.0
        for half in range(2):
            rows = jnp.concatenate([take[deep, half] for take in takes], axis=0)
            total += jnp.dot(chosen[half], rows, preferred_element_type=jnp.float32)
        outs[deep][...] = total.astype(outs[deep].dtype)


def synthesis_kernel(degrees, orders_ref, *refs):
    weights, fields, outs = refs[:4], refs[4:8], refs[8:]
    lat_rows = outs[0].shape[2]
    contract = (((0,), (0,)), ((), ()))
    for deep in four:
        chosen = masked(weights[deep][...], orders_ref[pair_at(0, deep, 0)], degrees)
        for half in range(2):
            values = lax.dot_general(
                chosen[half], fields[deep][...], contract, preferred_element_type=jnp.float32
            ).astype(jnp.bfloat16)
            for flat, out in enumerate(outs):
                out[deep, half] = values[flat * lat_rows : (flat + 1) * lat_rows]


def factor_kernel(degrees, orders_ref, kappa_ref, damping_ref, factor_ref):
    order = orders_ref[pair_at(0, 0, 0)]
    row_index = lax.broadcasted_iota(jnp.int32, factor_ref.shape, 0)
    degree = jnp.where(row_index < degrees - order, order + row_index, row_index - 1)
    degree = degree.astype(jnp.float32)
    factor_ref[...] = damping_ref[...] / (
        1.0 + kappa_ref[...] + degree * (degree + 1.0) / (degrees * degrees)
    )


def solve_kernel(one, two, three, last, state_ref, factor_ref, right_ref, left_ref, sent_ref):
    rows = state_ref.shape[1]
    radial = right_ref.shape[0]
    coefficient = one[...]
    for other in (two, three, last):
        coefficient += other[...].astype(jnp.float32)
    right_side = state_ref[0].astype(jnp.float32) + time_step * coefficient[:rows]
    right_side = right_side.astype(jnp.bfloat16)
    sent_ref[...] = jnp.zeros_like(sent_ref)
    for part in range(2):
        columns = pl.ds(part * radial, radial)
        eigen = jnp.dot(
            right_side[:, part * radial : (part + 1) * radial],
            right_ref[...],
            preferred_element_type=jnp.float32,
        )
        scaled = (eigen * factor_ref[...]).astype(jnp.bfloat16)
        field = jnp.dot(scaled, left_ref[...], preferred_element_type=jnp.float32)
        sent_ref[pl.ds(0, rows), columns] = field.astype(jnp.bfloat16)


def inverse_kernel(orders_ref, table_ref, *refs):
    takes, (out_ref, buffer, held, sems) = refs[:-4], refs[-4:]
    slot_rows, lat_block, radial = held.shape
    slots = slot_rows // 2
    table = table_ref[lax.axis_index("sec")]

    def chunk(at):
        return pltpu.make_async_copy(
            buffer.at[pl.ds(2 * at, 2)], out_ref.at[pl.ds(2 * at, 2)], sems.at[at]
        )

    def one_block(block, carry):
        begin = pl.multiple_of(block * lat_block, lat_block)
        for sec, flat, deep in np.ndindex(2, 4, 4):
            order = orders_ref[pair_at(sec, deep, flat)]
            for half, part in np.ndindex(2, 2):
                values = takes[4 * sec + flat][
                    deep, half, pl.ds(begin, lat_block), pl.ds(part * radial, radial)
                ]
                held[part * slots + 2 * order + half] = values.astype(jnp.float32)
        for at in range(0, lat_block, 2):
            two = jnp.concatenate(
                [held[:, at, :].astype(jnp.bfloat16), held[:, at + 1, :].astype(jnp.bfloat16)],
                axis=1,
            )
            values = jnp.dot(table, two, preferred_element_type=jnp.float32)
            lat = begin + at
            buffer[lat] = values[:, :radial]
            buffer[lat + 1] = values[:, radial:]
            chunk(lat // 2).start()
        return carry

    lax.fori_loop(0, buffer.shape[0] // lat_block, one_block, 0)
    for at in range(sems.shape[0]):
        chunk(at).wait()


def inverse_values(pair_orders, table, takes, lat_block):
    _, phi_count, slot_rows = table.shape
    lat_rows, radial = takes[0].shape[2], takes[0].shape[3] // 2
    out = jax.ShapeDtypeStruct((lat_rows, phi_count, radial), jnp.float32)
    return pl.pallas_call(
        inverse_kernel,
        in_specs=[smem()] + [vmem()] * (1 + len(takes)),
        out_specs=anywhere(),
        out_shape=out,
        scratch_shapes=[
            pltpu.VMEM(out.shape, jnp.float32),
            pltpu.VMEM((slot_rows, lat_block, radial), jnp.float32),
            pltpu.SemaphoreType.DMA((lat_rows // 2,)),
        ],
        compiler_params=params(36),
        cost_estimate=pl.CostEstimate(
            flops=2 * slot_rows * phi_count * lat_rows * radial,
            bytes_accessed=4 * lat_rows * phi_count * radial,
            transcendentals=0,
        ),
    )(pair_orders, table, *takes)


def on_device_compact(grid_terms, pair_orders, legendre, state, kappa, right_op, left_op):
    lat_rows, phi_count, radial = grid_terms.shape
    rows = legendre.shape[1]
    degrees = rows - 1
    padded = -(-rows // 8) * 8
    columns = 2 * radial
    pair_total = pair_orders.shape[0]
    table = natural_table(pair_total, lax.axis_size("sec"), phi_count)
    forward_table = jnp.asarray(table, jnp.bfloat16)
    inverse_table = jnp.asarray(table.transpose(0, 2, 1), jnp.bfloat16)

    def shape(*sizes, dtype=jnp.bfloat16):
        return jax.ShapeDtypeStruct(sizes, dtype)

    slab = shape(padded, 4 * lat_rows)
    cuts = call(
        cut_kernel,
        [legendre],
        [slab] * 4,
        scratch=[pltpu.VMEM((16, padded, lat_rows), jnp.bfloat16)],
    )
    weights = [cuts[0]] + [exchange(cuts[deep], deep=deep) for deep in (1, 2, 3)]

    held = forward_sums(forward_table, grid_terms, 8)
    block = shape(4, 2, lat_rows, columns)

    def arranged(sec, dtype):
        return call(
            functools.partial(arrange_kernel, sec),
            [pair_orders, held],
            shape(4, 4, 2, lat_rows, columns, dtype=dtype),
            mib=24,
            scalars=1,
        )

    taken = exchange(arranged(1, jnp.bfloat16), sec=1)
    keep = arranged(0, jnp.float32)
    blocks = call(add_kernel, [keep, taken], [block] * 4, mib=24)
    takes = [blocks[0]] + [exchange(blocks[flat], flat=flat) for flat in (1, 2, 3)]

    sums = call(
        functools.partial(degrees_kernel, degrees),
        [pair_orders, *weights, *takes],
        [shape(padded, columns, dtype=jnp.float32)] + [shape(padded, columns)] * 3,
        scalars=1,
    )
    sums = [sums[0]] + [exchange(sums[deep], deep=deep) for deep in (3, 2, 1)]

    radial_mode = np.arange(radial, dtype=np.float32) / np.float32(radial)
    damping = np.exp(-filter_strength * radial_mode**filter_power).astype(np.float32)
    factor = call(
        functools.partial(factor_kernel, degrees),
        [pair_orders, kappa[None, :], jnp.asarray(damping)[None, :]],
        shape(rows, radial, dtype=jnp.float32),
        scalars=1,
    )
    field = call(
        solve_kernel, [*sums, state, factor, right_op, left_op], shape(padded, columns)
    )
    new_state = field[None, :rows]

    moved, new_state = lax.optimization_barrier((exchange(field, deep=1), new_state))
    fields = [field, moved] + [exchange(field, deep=deep) for deep in (2, 3)]
    blocks = call(
        functools.partial(synthesis_kernel, degrees),
        [pair_orders, *weights, *fields],
        [block] * 4,
        scalars=1,
    )
    takes = [blocks[0]] + [exchange(blocks[flat], flat=flat) for flat in (1, 2, 3)]
    takes += [exchange(take, sec=1) for take in takes]
    evolved = inverse_values(pair_orders, inverse_table, takes, 16)
    return (evolved, new_state)


def on_device(*args):
    lat_rows = args[0].shape[0]
    rows = args[2].shape[1]
    sections, side_row, side_x = (lax.axis_size(name) for name in names)
    fits = args[2].shape[0] == 1 and lat_rows % 16 == 0 and rows <= 2 * lat_rows
    fits = fits and args[0].size * 4 <= 24 * 1024 * 1024
    fits = fits and (sections, side_row, side_x) == (2, 8, 2)
    return on_device_compact(*args) if fits else on_device_wide(*args)


def solution(mesh):
    return jax.shard_map(
        on_device,
        mesh=mesh,
        in_specs=(
            P(("row", "col"), "sec", None),
            P(),
            P(("sec", "row", "col"), None, None),
            P(("sec", "row", "col"), None, None),
            P(),
            P(),
            P(),
        ),
        out_specs=(P(("row", "col"), "sec", None), P(("sec", "row", "col"), None, None)),
        check_vma=False,
    )
```

```python
import functools
import math

import jax
import jax.numpy as jnp
import numpy as np
from jax import lax
from jax.experimental import pallas as pl
from jax.experimental.pallas import tpu as pltpu
from jax.sharding import PartitionSpec as P

time_step = 0.5
filter_strength = 36.0
filter_power = 36.0


def slot_orders_of(pair_orders):
    order_total = 2 * pair_orders.shape[0]
    return jnp.stack([pair_orders, order_total - 1 - pair_orders], axis=1).reshape(order_total)


def fourier_table(orders, phi_start, phi_count, longitudes):
    longitude = phi_start + lax.iota(jnp.int32, phi_count)
    phase_turns = longitude[:, None] * orders[None, :] % longitudes
    phase_angle = phase_turns.astype(jnp.float32) * (2.0 * math.pi / longitudes)
    norm_scale = 1.0 / math.sqrt(longitudes)
    return jnp.stack(
        [jnp.cos(phase_angle) * norm_scale, -jnp.sin(phase_angle) * norm_scale], axis=-1
    )


def on_device_wide(grid_terms, pair_orders, legendre, state, kappa, right_op, left_op):
    lat_rows, phi_count, radial = grid_terms.shape
    pairs_here = legendre.shape[0]
    degrees = legendre.shape[1] - 1
    latitudes = legendre.shape[2]
    sections = lax.axis_size("sec")
    longitudes = phi_count * sections
    columns = 2 * radial
    section_slots = degrees // sections
    orders = slot_orders_of(pair_orders)
    sec_index = lax.axis_index("sec")
    highest = lax.Precision.HIGHEST
    phi_start = sec_index * phi_count
    sub_orders = orders
    phase_table = fourier_table(sub_orders, phi_start, phi_count, longitudes)
    term = jnp.einsum(
        "tpr,psc->stcr",
        grid_terms,
        phase_table,
        precision=highest,
        preferred_element_type=jnp.float32,
    )
    spectral = lax.psum_scatter(
        term.reshape(section_slots * lax.axis_size("sec"), lat_rows, columns),
        "sec",
        scatter_dimension=0,
        tiled=True,
    ).astype(jnp.bfloat16)
    device = lax.axis_index(("sec", "row", "col"))
    local_orders = lax.dynamic_slice_in_dim(pair_orders, device * pairs_here, pairs_here)
    row_index = lax.iota(jnp.int32, degrees + 1)
    leading = row_index[None, :] < (degrees - local_orders)[:, None]
    degree = jnp.where(leading, local_orders[:, None] + row_index[None, :], row_index[None, :] - 1)
    received = lax.all_to_all(spectral, ("row", "col"), split_axis=0, concat_axis=1, tiled=True)
    item_count = received.shape[2]
    paired = received.reshape(pairs_here, 2, latitudes, item_count)
    both_orders = jnp.einsum("pit,potx->piox", legendre, paired, preferred_element_type=jnp.float32)
    coefficient = jnp.where(leading[:, :, None], both_orders[:, :, 0], both_orders[:, :, 1])
    right_side = (state.astype(jnp.float32) + time_step * coefficient).astype(jnp.bfloat16)
    right_side = right_side.reshape(pairs_here, degrees + 1, 2, radial)
    eigen_part = jnp.einsum(
        "picr,rk->pick", right_side, right_op, preferred_element_type=jnp.float32
    )
    radial_mode = lax.iota(jnp.float32, radial) / radial
    damping = jnp.exp(-filter_strength * radial_mode**filter_power)
    degree_wide = degree.astype(jnp.float32)
    degree_term = degree_wide * (degree_wide + 1.0) / (degrees * degrees)
    factor = damping[None, None, :] / (1.0 + kappa[None, None, :] + degree_term[:, :, None])
    scaled = (eigen_part * factor[:, :, None, :]).astype(jnp.bfloat16)
    new_state = jnp.einsum("pick,kr->picr", scaled, left_op, preferred_element_type=jnp.float32)
    new_state = new_state.astype(jnp.bfloat16).reshape(pairs_here, degrees + 1, columns)
    zero_rows = jnp.zeros_like(new_state)
    split_state = jnp.stack(
        [
            jnp.where(leading[:, :, None], new_state, zero_rows),
            jnp.where(leading[:, :, None], zero_rows, new_state),
        ],
        axis=1,
    )
    synthesis_wide = jnp.einsum(
        "pit,poix->potx", legendre, split_state, preferred_element_type=jnp.float32
    )
    synthesis = synthesis_wide.astype(jnp.bfloat16).reshape(2 * pairs_here, latitudes, columns)
    returned = lax.all_to_all(synthesis, ("row", "col"), split_axis=1, concat_axis=0, tiled=True)
    sub_orders = lax.dynamic_slice_in_dim(orders, sec_index * section_slots, section_slots)
    phase_table = fourier_table(sub_orders, 0, longitudes, longitudes)
    values = returned.astype(jnp.float32).reshape(section_slots, lat_rows, 2, radial)
    partial_value = jnp.einsum(
        "stcr,psc->tpr", values, phase_table, precision=highest, preferred_element_type=jnp.float32
    )
    evolved = lax.psum_scatter(
        partial_value.astype(jnp.bfloat16), "sec", scatter_dimension=1, tiled=True
    ).astype(jnp.float32)
    return (evolved, new_state)


names = ("sec", "row", "col")


def natural_table(pair_total, sections, phi_count):
    slots = 2 * pair_total
    longitudes = sections * phi_count
    low = np.arange(pair_total)
    orders = np.stack([low, slots - 1 - low], axis=1).reshape(slots)
    turns = orders[:, None] * np.arange(longitudes)[None, :] % longitudes
    angle = turns * (2.0 * np.pi / longitudes)
    table = np.concatenate([np.cos(angle), -np.sin(angle)], axis=0) / np.sqrt(longitudes)
    return table.reshape(2 * slots, sections, phi_count).transpose(1, 0, 2).astype(np.float32)


def params(mib):
    return pltpu.CompilerParams(vmem_limit_bytes=mib * 1024 * 1024)


def vmem():
    return pl.BlockSpec(memory_space=pltpu.VMEM)


def smem():
    return pl.BlockSpec(memory_space=pltpu.SMEM)


def anywhere():
    return pl.BlockSpec(memory_space=pl.ANY)


def call(kernel, operands, out_shapes, mib=16, scalars=0, cost=None, scratch=()):
    single = not isinstance(out_shapes, (list, tuple))
    return pl.pallas_call(
        kernel,
        in_specs=[smem()] * scalars + [vmem()] * (len(operands) - scalars),
        out_specs=vmem() if single else [vmem()] * len(out_shapes),
        out_shape=out_shapes,
        scratch_shapes=scratch,
        compiler_params=params(mib),
        cost_estimate=cost,
    )(*operands)


four = range(4)


def plane_index():
    return lax.axis_index("row") % 2 * 2 + lax.axis_index("col")


def depth_index():
    return lax.axis_index("row") // 2


def pair_at(sec, deep, flat):
    row = lax.axis_index("row") ^ (2 * deep + flat // 2)
    col = lax.axis_index("col") ^ (flat % 2)
    at_sec = lax.axis_index("sec") ^ sec
    return (at_sec * lax.axis_size("row") + row) * lax.axis_size("col") + col


def exchange(array, sec=0, deep=0, flat=0):
    sizes = tuple(lax.axis_size(name) for name in names)
    pairs = []
    for source in np.ndindex(*sizes):
        target = (source[0] ^ sec, source[1] ^ (2 * deep + flat // 2), source[2] ^ (flat % 2))
        pairs.append(
            (int(np.ravel_multi_index(source, sizes)), int(np.ravel_multi_index(target, sizes)))
        )
    return lax.ppermute(array, names, pairs)


def cut_kernel(legendre_ref, *refs):
    outs, parts = refs[:-1], refs[-1]
    count, rows, lats = parts.shape
    given = legendre_ref.shape[1]
    parts[...] = jnp.zeros_like(parts)
    for at in range(count):
        parts[at, :given] = legendre_ref[0, :, at * lats : (at + 1) * lats]
    for deep, out in enumerate(outs):
        first = (depth_index() ^ deep) * 4
        out[...] = jnp.concatenate([parts[first + (plane_index() ^ flat)] for flat in four], axis=1)


def arrange_kernel(sec, orders_ref, held, out_ref):
    blocks, rows, lat_block, radial = held.shape
    slots = rows // 2
    for flat, deep in np.ndindex(4, 4):
        order = orders_ref[pair_at(sec, deep, flat)]
        for part in range(2):
            values = held[:, pl.ds(part * slots + 2 * order, 2)].astype(out_ref.dtype)
            for half in range(2):
                out_ref[flat, deep, half, :, pl.ds(part * radial, radial)] = values[
                    :, half
                ].reshape(blocks * lat_block, radial)


def forward_kernel(table_ref, grid_ref, held, wide, table_held, buffer, sems, table_sem):
    blocks, rows, lat_block, radial = held.shape

    def chunk(at):
        return pltpu.make_async_copy(
            grid_ref.at[pl.ds(2 * at, 2)], buffer.at[pl.ds(2 * at, 2)], sems.at[at]
        )

    table_copy = pltpu.make_async_copy(table_ref.at[lax.axis_index("sec")], wide, table_sem)
    table_copy.start()
    for at in range(sems.shape[0]):
        chunk(at).start()
    table_copy.wait()
    table_held[...] = wide[...].astype(table_held.dtype)
    table = table_held[...]

    def one_block(block, carry):
        for at in range(0, lat_block, 2):
            lat = block * lat_block + at
            chunk(lat // 2).wait()
            two = jnp.concatenate(
                [buffer[lat].astype(jnp.bfloat16), buffer[lat + 1].astype(jnp.bfloat16)], axis=1
            )
            sums = jnp.dot(table, two, preferred_element_type=jnp.float32)
            held[block, :, at, :] = sums[:, :radial]
            held[block, :, at + 1, :] = sums[:, radial:]
        return carry

    lax.fori_loop(0, blocks, one_block, 0)


def forward_sums(table, grid_terms, lat_block):
    sections, rows, phi_count = table.shape
    lat_rows, _, radial = grid_terms.shape
    return pl.pallas_call(
        forward_kernel,
        in_specs=[pl.BlockSpec(memory_space=pltpu.HBM), anywhere()],
        out_specs=vmem(),
        out_shape=jax.ShapeDtypeStruct((lat_rows // lat_block, rows, lat_block, radial), jnp.float32),
        scratch_shapes=[
            pltpu.VMEM((rows, phi_count), jnp.float32),
            pltpu.VMEM((rows, phi_count), jnp.bfloat16),
            pltpu.VMEM(grid_terms.shape, jnp.float32),
            pltpu.SemaphoreType.DMA((lat_rows // 2,)),
            pltpu.SemaphoreType.DMA,
        ],
        compiler_params=params(36),
        cost_estimate=pl.CostEstimate(
            flops=2 * rows * phi_count * lat_rows * radial,
            bytes_accessed=4 * lat_rows * phi_count * radial,
            transcendentals=0,
        ),
    )(pltpu.with_memory_space_constraint(table, pltpu.HBM), grid_terms)


def add_kernel(keep_ref, take_ref, *outs):
    for flat, out in enumerate(outs):
        out[...] = (keep_ref[flat] + take_ref[flat].astype(jnp.float32)).astype(out.dtype)


def masked(weights, order, degrees):
    row_index = lax.broadcasted_iota(jnp.int32, weights.shape, 0)
    leading = row_index < degrees - order
    zero = jnp.zeros_like(weights)
    return jnp.where(leading, weights, zero), jnp.where(leading, zero, weights)


def degrees_kernel(degrees, orders_ref, *refs):
    weights, takes, outs = refs[:4], refs[4:8], refs[8:]
    for deep in four:
        chosen = masked(weights[deep][...], orders_ref[pair_at(0, deep, 0)], degrees)
        total = 0.0
        for half in range(2):
            rows = jnp.concatenate([take[deep, half] for take in takes], axis=0)
            total += jnp.dot(chosen[half], rows, preferred_element_type=jnp.float32)
        outs[deep][...] = total.astype(outs[deep].dtype)


def synthesis_kernel(degrees, orders_ref, *refs):
    weights, fields, outs = refs[:4], refs[4:8], refs[8:]
    lat_rows = outs[0].shape[2]
    contract = (((0,), (0,)), ((), ()))
    for deep in four:
        chosen = masked(weights[deep][...], orders_ref[pair_at(0, deep, 0)], degrees)
        for half in range(2):
            values = lax.dot_general(
                chosen[half], fields[deep][...], contract, preferred_element_type=jnp.float32
            ).astype(jnp.bfloat16)
            for flat, out in enumerate(outs):
                out[deep, half] = values[flat * lat_rows : (flat + 1) * lat_rows]


def factor_kernel(degrees, orders_ref, kappa_ref, damping_ref, factor_ref):
    order = orders_ref[pair_at(0, 0, 0)]
    row_index = lax.broadcasted_iota(jnp.int32, factor_ref.shape, 0)
    degree = jnp.where(row_index < degrees - order, order + row_index, row_index - 1)
    degree = degree.astype(jnp.float32)
    factor_ref[...] = damping_ref[...] / (
        1.0 + kappa_ref[...] + degree * (degree + 1.0) / (degrees * degrees)
    )


def solve_kernel(one, two, three, last, state_ref, factor_ref, right_ref, left_ref, sent_ref):
    rows = state_ref.shape[1]
    radial = right_ref.shape[0]
    coefficient = one[...]
    for other in (two, three, last):
        coefficient += other[...].astype(jnp.float32)
    right_side = state_ref[0].astype(jnp.float32) + time_step * coefficient[:rows]
    right_side = right_side.astype(jnp.bfloat16)
    sent_ref[...] = jnp.zeros_like(sent_ref)
    for part in range(2):
        columns = pl.ds(part * radial, radial)
        eigen = jnp.dot(
            right_side[:, part * radial : (part + 1) * radial],
            right_ref[...],
            preferred_element_type=jnp.float32,
        )
        scaled = (eigen * factor_ref[...]).astype(jnp.bfloat16)
        field = jnp.dot(scaled, left_ref[...], preferred_element_type=jnp.float32)
        sent_ref[pl.ds(0, rows), columns] = field.astype(jnp.bfloat16)


def inverse_kernel(orders_ref, table_ref, *refs):
    takes, (out_ref, buffer, held, sems) = refs[:-4], refs[-4:]
    slot_rows, lat_block, radial = held.shape
    slots = slot_rows // 2
    table = table_ref[lax.axis_index("sec")]

    def chunk(at):
        return pltpu.make_async_copy(
            buffer.at[pl.ds(2 * at, 2)], out_ref.at[pl.ds(2 * at, 2)], sems.at[at]
        )

    def one_block(block, carry):
        begin = pl.multiple_of(block * lat_block, lat_block)
        for sec, flat, deep in np.ndindex(2, 4, 4):
            order = orders_ref[pair_at(sec, deep, flat)]
            for half, part in np.ndindex(2, 2):
                values = takes[4 * sec + flat][
                    deep, half, pl.ds(begin, lat_block), pl.ds(part * radial, radial)
                ]
                held[part * slots + 2 * order + half] = values.astype(jnp.float32)
        for at in range(0, lat_block, 2):
            two = jnp.concatenate(
                [held[:, at, :].astype(jnp.bfloat16), held[:, at + 1, :].astype(jnp.bfloat16)],
                axis=1,
            )
            values = jnp.dot(table, two, preferred_element_type=jnp.float32)
            lat = begin + at
            buffer[lat] = values[:, :radial]
            buffer[lat + 1] = values[:, radial:]
            chunk(lat // 2).start()
        return carry

    lax.fori_loop(0, buffer.shape[0] // lat_block, one_block, 0)
    for at in range(sems.shape[0]):
        chunk(at).wait()


def inverse_values(pair_orders, table, takes, lat_block):
    _, phi_count, slot_rows = table.shape
    lat_rows, radial = takes[0].shape[2], takes[0].shape[3] // 2
    out = jax.ShapeDtypeStruct((lat_rows, phi_count, radial), jnp.float32)
    return pl.pallas_call(
        inverse_kernel,
        in_specs=[smem()] + [vmem()] * (1 + len(takes)),
        out_specs=anywhere(),
        out_shape=out,
        scratch_shapes=[
            pltpu.VMEM(out.shape, jnp.float32),
            pltpu.VMEM((slot_rows, lat_block, radial), jnp.float32),
            pltpu.SemaphoreType.DMA((lat_rows // 2,)),
        ],
        compiler_params=params(36),
        cost_estimate=pl.CostEstimate(
            flops=2 * slot_rows * phi_count * lat_rows * radial,
            bytes_accessed=4 * lat_rows * phi_count * radial,
            transcendentals=0,
        ),
    )(pair_orders, table, *takes)


def on_device_compact(grid_terms, pair_orders, legendre, state, kappa, right_op, left_op):
    lat_rows, phi_count, radial = grid_terms.shape
    rows = legendre.shape[1]
    degrees = rows - 1
    padded = -(-rows // 8) * 8
    columns = 2 * radial
    pair_total = pair_orders.shape[0]
    table = natural_table(pair_total, lax.axis_size("sec"), phi_count)
    forward_table = jnp.asarray(table)
    inverse_table = jnp.asarray(table.transpose(0, 2, 1), jnp.bfloat16)

    def shape(*sizes, dtype=jnp.bfloat16):
        return jax.ShapeDtypeStruct(sizes, dtype)

    slab = shape(padded, 4 * lat_rows)
    cuts = call(
        cut_kernel,
        [legendre],
        [slab] * 4,
        scratch=[pltpu.VMEM((16, padded, lat_rows), jnp.bfloat16)],
    )
    weights = [cuts[0]] + [exchange(cuts[deep], deep=deep) for deep in (1, 2, 3)]

    held = forward_sums(forward_table, grid_terms, 8)
    block = shape(4, 2, lat_rows, columns)

    def arranged(sec, dtype):
        return call(
            functools.partial(arrange_kernel, sec),
            [pair_orders, held],
            shape(4, 4, 2, lat_rows, columns, dtype=dtype),
            mib=24,
            scalars=1,
        )

    taken = exchange(arranged(1, jnp.bfloat16), sec=1)
    keep = arranged(0, jnp.float32)
    blocks = call(add_kernel, [keep, taken], [block] * 4, mib=24)
    takes = [blocks[0]] + [exchange(blocks[flat], flat=flat) for flat in (1, 2, 3)]

    sums = call(
        functools.partial(degrees_kernel, degrees),
        [pair_orders, *weights, *takes],
        [shape(padded, columns, dtype=jnp.float32)] + [shape(padded, columns)] * 3,
        scalars=1,
    )
    sums = [sums[0]] + [exchange(sums[deep], deep=deep) for deep in (3, 2, 1)]

    radial_mode = np.arange(radial, dtype=np.float32) / np.float32(radial)
    damping = np.exp(-filter_strength * radial_mode**filter_power).astype(np.float32)
    factor = call(
        functools.partial(factor_kernel, degrees),
        [pair_orders, kappa[None, :], jnp.asarray(damping)[None, :]],
        shape(rows, radial, dtype=jnp.float32),
        scalars=1,
    )
    field = call(
        solve_kernel, [*sums, state, factor, right_op, left_op], shape(padded, columns)
    )
    new_state = field[None, :rows]

    moved, new_state = lax.optimization_barrier((exchange(field, deep=1), new_state))
    fields = [field, moved] + [exchange(field, deep=deep) for deep in (2, 3)]
    blocks = call(
        functools.partial(synthesis_kernel, degrees),
        [pair_orders, *weights, *fields],
        [block] * 4,
        scalars=1,
    )
    takes = [blocks[0]] + [exchange(blocks[flat], flat=flat) for flat in (1, 2, 3)]
    takes += [exchange(take, sec=1) for take in takes]
    evolved = inverse_values(pair_orders, inverse_table, takes, 16)
    return (evolved, new_state)


def on_device(*args):
    lat_rows = args[0].shape[0]
    rows = args[2].shape[1]
    sections, side_row, side_x = (lax.axis_size(name) for name in names)
    fits = args[2].shape[0] == 1 and lat_rows % 16 == 0 and rows <= 2 * lat_rows
    fits = fits and args[0].size * 4 <= 24 * 1024 * 1024
    fits = fits and (sections, side_row, side_x) == (2, 8, 2)
    return on_device_compact(*args) if fits else on_device_wide(*args)


def solution(mesh):
    return jax.shard_map(
        on_device,
        mesh=mesh,
        in_specs=(
            P(("row", "col"), "sec", None),
            P(),
            P(("sec", "row", "col"), None, None),
            P(("sec", "row", "col"), None, None),
            P(),
            P(),
            P(),
        ),
        out_specs=(P(("row", "col"), "sec", None), P(("sec", "row", "col"), None, None)),
        check_vma=False,
    )
```

```python
import functools
import math

import jax
import jax.numpy as jnp
import numpy as np
from jax import lax
from jax.experimental import pallas as pl
from jax.experimental.pallas import tpu as pltpu
from jax.sharding import PartitionSpec as P

time_step = 0.5
filter_strength = 36.0
filter_power = 36.0


def slot_orders_of(pair_orders):
    order_total = 2 * pair_orders.shape[0]
    return jnp.stack([pair_orders, order_total - 1 - pair_orders], axis=1).reshape(order_total)


def fourier_table(orders, phi_start, phi_count, longitudes):
    longitude = phi_start + lax.iota(jnp.int32, phi_count)
    phase_turns = longitude[:, None] * orders[None, :] % longitudes
    phase_angle = phase_turns.astype(jnp.float32) * (2.0 * math.pi / longitudes)
    norm_scale = 1.0 / math.sqrt(longitudes)
    return jnp.stack(
        [jnp.cos(phase_angle) * norm_scale, -jnp.sin(phase_angle) * norm_scale], axis=-1
    )


def on_device_wide(grid_terms, pair_orders, legendre, state, kappa, right_op, left_op):
    lat_rows, phi_count, radial = grid_terms.shape
    pairs_here = legendre.shape[0]
    degrees = legendre.shape[1] - 1
    latitudes = legendre.shape[2]
    sections = lax.axis_size("sec")
    longitudes = phi_count * sections
    columns = 2 * radial
    section_slots = degrees // sections
    orders = slot_orders_of(pair_orders)
    sec_index = lax.axis_index("sec")
    highest = lax.Precision.HIGHEST
    phi_start = sec_index * phi_count
    sub_orders = orders
    phase_table = fourier_table(sub_orders, phi_start, phi_count, longitudes)
    term = jnp.einsum(
        "tpr,psc->stcr",
        grid_terms,
        phase_table,
        precision=highest,
        preferred_element_type=jnp.float32,
    )
    spectral = lax.psum_scatter(
        term.reshape(section_slots * lax.axis_size("sec"), lat_rows, columns),
        "sec",
        scatter_dimension=0,
        tiled=True,
    ).astype(jnp.bfloat16)
    device = lax.axis_index(("sec", "row", "col"))
    local_orders = lax.dynamic_slice_in_dim(pair_orders, device * pairs_here, pairs_here)
    row_index = lax.iota(jnp.int32, degrees + 1)
    leading = row_index[None, :] < (degrees - local_orders)[:, None]
    degree = jnp.where(leading, local_orders[:, None] + row_index[None, :], row_index[None, :] - 1)
    received = lax.all_to_all(spectral, ("row", "col"), split_axis=0, concat_axis=1, tiled=True)
    item_count = received.shape[2]
    paired = received.reshape(pairs_here, 2, latitudes, item_count)
    both_orders = jnp.einsum("pit,potx->piox", legendre, paired, preferred_element_type=jnp.float32)
    coefficient = jnp.where(leading[:, :, None], both_orders[:, :, 0], both_orders[:, :, 1])
    right_side = (state.astype(jnp.float32) + time_step * coefficient).astype(jnp.bfloat16)
    right_side = right_side.reshape(pairs_here, degrees + 1, 2, radial)
    eigen_part = jnp.einsum(
        "picr,rk->pick", right_side, right_op, preferred_element_type=jnp.float32
    )
    radial_mode = lax.iota(jnp.float32, radial) / radial
    damping = jnp.exp(-filter_strength * radial_mode**filter_power)
    degree_wide = degree.astype(jnp.float32)
    degree_term = degree_wide * (degree_wide + 1.0) / (degrees * degrees)
    factor = damping[None, None, :] / (1.0 + kappa[None, None, :] + degree_term[:, :, None])
    scaled = (eigen_part * factor[:, :, None, :]).astype(jnp.bfloat16)
    new_state = jnp.einsum("pick,kr->picr", scaled, left_op, preferred_element_type=jnp.float32)
    new_state = new_state.astype(jnp.bfloat16).reshape(pairs_here, degrees + 1, columns)
    zero_rows = jnp.zeros_like(new_state)
    split_state = jnp.stack(
        [
            jnp.where(leading[:, :, None], new_state, zero_rows),
            jnp.where(leading[:, :, None], zero_rows, new_state),
        ],
        axis=1,
    )
    synthesis_wide = jnp.einsum(
        "pit,poix->potx", legendre, split_state, preferred_element_type=jnp.float32
    )
    synthesis = synthesis_wide.astype(jnp.bfloat16).reshape(2 * pairs_here, latitudes, columns)
    returned = lax.all_to_all(synthesis, ("row", "col"), split_axis=1, concat_axis=0, tiled=True)
    sub_orders = lax.dynamic_slice_in_dim(orders, sec_index * section_slots, section_slots)
    phase_table = fourier_table(sub_orders, 0, longitudes, longitudes)
    values = returned.astype(jnp.float32).reshape(section_slots, lat_rows, 2, radial)
    partial_value = jnp.einsum(
        "stcr,psc->tpr", values, phase_table, precision=highest, preferred_element_type=jnp.float32
    )
    evolved = lax.psum_scatter(
        partial_value.astype(jnp.bfloat16), "sec", scatter_dimension=1, tiled=True
    ).astype(jnp.float32)
    return (evolved, new_state)


names = ("sec", "row", "col")


def natural_table(pair_total, sections, phi_count):
    slots = 2 * pair_total
    longitudes = sections * phi_count
    low = np.arange(pair_total)
    orders = np.stack([low, slots - 1 - low], axis=1).reshape(slots)
    turns = orders[:, None] * np.arange(longitudes)[None, :] % longitudes
    angle = turns * (2.0 * np.pi / longitudes)
    table = np.concatenate([np.cos(angle), -np.sin(angle)], axis=0) / np.sqrt(longitudes)
    return table.reshape(2 * slots, sections, phi_count).transpose(1, 0, 2).astype(np.float32)


def params(mib):
    return pltpu.CompilerParams(vmem_limit_bytes=mib * 1024 * 1024)


def vmem():
    return pl.BlockSpec(memory_space=pltpu.VMEM)


def smem():
    return pl.BlockSpec(memory_space=pltpu.SMEM)


def anywhere():
    return pl.BlockSpec(memory_space=pl.ANY)


def call(kernel, operands, out_shapes, mib=16, scalars=0, cost=None, scratch=()):
    single = not isinstance(out_shapes, (list, tuple))
    return pl.pallas_call(
        kernel,
        in_specs=[smem()] * scalars + [vmem()] * (len(operands) - scalars),
        out_specs=vmem() if single else [vmem()] * len(out_shapes),
        out_shape=out_shapes,
        scratch_shapes=scratch,
        compiler_params=params(mib),
        cost_estimate=cost,
    )(*operands)


four = range(4)


def plane_index():
    return lax.axis_index("row") % 2 * 2 + lax.axis_index("col")


def depth_index():
    return lax.axis_index("row") // 2


def pair_at(sec, deep, flat):
    row = lax.axis_index("row") ^ (2 * deep + flat // 2)
    col = lax.axis_index("col") ^ (flat % 2)
    at_sec = lax.axis_index("sec") ^ sec
    return (at_sec * lax.axis_size("row") + row) * lax.axis_size("col") + col


def exchange(array, sec=0, deep=0, flat=0):
    sizes = tuple(lax.axis_size(name) for name in names)
    pairs = []
    for source in np.ndindex(*sizes):
        target = (source[0] ^ sec, source[1] ^ (2 * deep + flat // 2), source[2] ^ (flat % 2))
        pairs.append(
            (int(np.ravel_multi_index(source, sizes)), int(np.ravel_multi_index(target, sizes)))
        )
    return lax.ppermute(array, names, pairs)


def cut_kernel(legendre_ref, *refs):
    outs, parts = refs[:-1], refs[-1]
    count, rows, lats = parts.shape
    given = legendre_ref.shape[1]
    parts[...] = jnp.zeros_like(parts)
    for at in range(count):
        parts[at, :given] = legendre_ref[0, :, at * lats : (at + 1) * lats]
    for deep, out in enumerate(outs):
        first = (depth_index() ^ deep) * 4
        out[...] = jnp.concatenate([parts[first + (plane_index() ^ flat)] for flat in four], axis=1)


def arrange_kernel(sec, orders_ref, held, out_ref):
    blocks, rows, lat_block, radial = held.shape
    slots = rows // 2
    for flat, deep in np.ndindex(4, 4):
        order = orders_ref[pair_at(sec, deep, flat)]
        for part in range(2):
            values = held[:, pl.ds(part * slots + 2 * order, 2)].astype(out_ref.dtype)
            for half in range(2):
                out_ref[flat, deep, half, :, pl.ds(part * radial, radial)] = values[
                    :, half
                ].reshape(blocks * lat_block, radial)


def forward_kernel(table_ref, grid_ref, held, buffer, sems):
    blocks, rows, lat_block, radial = held.shape

    def chunk(at):
        return pltpu.make_async_copy(
            grid_ref.at[pl.ds(2 * at, 2)], buffer.at[pl.ds(2 * at, 2)], sems.at[at]
        )

    for at in range(sems.shape[0]):
        chunk(at).start()
    table = table_ref[lax.axis_index("sec")]

    def one_block(block, carry):
        for at in range(0, lat_block, 2):
            lat = block * lat_block + at
            chunk(lat // 2).wait()
            two = jnp.concatenate(
                [buffer[lat].astype(jnp.bfloat16), buffer[lat + 1].astype(jnp.bfloat16)], axis=1
            )
            sums = jnp.dot(table, two, preferred_element_type=jnp.float32)
            held[block, :, at, :] = sums[:, :radial]
            held[block, :, at + 1, :] = sums[:, radial:]
        return carry

    lax.fori_loop(0, blocks, one_block, 0)


def forward_sums(table, grid_terms, lat_block):
    sections, rows, phi_count = table.shape
    lat_rows, _, radial = grid_terms.shape
    return pl.pallas_call(
        forward_kernel,
        in_specs=[vmem(), anywhere()],
        out_specs=vmem(),
        out_shape=jax.ShapeDtypeStruct((lat_rows // lat_block, rows, lat_block, radial), jnp.float32),
        scratch_shapes=[
            pltpu.VMEM(grid_terms.shape, jnp.float32),
            pltpu.SemaphoreType.DMA((lat_rows // 2,)),
        ],
        compiler_params=params(36),
        cost_estimate=pl.CostEstimate(
            flops=2 * rows * phi_count * lat_rows * radial,
            bytes_accessed=4 * lat_rows * phi_count * radial,
            transcendentals=0,
        ),
    )(table, grid_terms)


def add_kernel(keep_ref, take_ref, *outs):
    for flat, out in enumerate(outs):
        out[...] = (keep_ref[flat] + take_ref[flat].astype(jnp.float32)).astype(out.dtype)


def masked(weights, order, degrees):
    row_index = lax.broadcasted_iota(jnp.int32, weights.shape, 0)
    leading = row_index < degrees - order
    zero = jnp.zeros_like(weights)
    return jnp.where(leading, weights, zero), jnp.where(leading, zero, weights)


def degrees_kernel(degrees, orders_ref, *refs):
    weights, takes, outs = refs[:4], refs[4:8], refs[8:]
    for deep in four:
        chosen = masked(weights[deep][...], orders_ref[pair_at(0, deep, 0)], degrees)
        total = 0.0
        for half in range(2):
            rows = jnp.concatenate([take[deep, half] for take in takes], axis=0)
            total += jnp.dot(chosen[half], rows, preferred_element_type=jnp.float32)
        outs[deep][...] = total.astype(outs[deep].dtype)


def synthesis_kernel(degrees, orders_ref, *refs):
    weights, fields, outs = refs[:4], refs[4:8], refs[8:]
    lat_rows = outs[0].shape[2]
    contract = (((0,), (0,)), ((), ()))
    for deep in four:
        chosen = masked(weights[deep][...], orders_ref[pair_at(0, deep, 0)], degrees)
        for half in range(2):
            values = lax.dot_general(
                chosen[half], fields[deep][...], contract, preferred_element_type=jnp.float32
            ).astype(jnp.bfloat16)
            for flat, out in enumerate(outs):
                out[deep, half] = values[flat * lat_rows : (flat + 1) * lat_rows]


def factor_kernel(degrees, orders_ref, kappa_ref, damping_ref, factor_ref):
    order = orders_ref[pair_at(0, 0, 0)]
    row_index = lax.broadcasted_iota(jnp.int32, factor_ref.shape, 0)
    degree = jnp.where(row_index < degrees - order, order + row_index, row_index - 1)
    degree = degree.astype(jnp.float32)
    factor_ref[...] = damping_ref[...] / (
        1.0 + kappa_ref[...] + degree * (degree + 1.0) / (degrees * degrees)
    )


def solve_kernel(one, two, three, last, state_ref, factor_ref, right_ref, left_ref, sent_ref):
    rows = state_ref.shape[1]
    radial = right_ref.shape[0]
    coefficient = one[...]
    for other in (two, three, last):
        coefficient += other[...].astype(jnp.float32)
    right_side = state_ref[0].astype(jnp.float32) + time_step * coefficient[:rows]
    right_side = right_side.astype(jnp.bfloat16)
    sent_ref[...] = jnp.zeros_like(sent_ref)
    for part in range(2):
        columns = pl.ds(part * radial, radial)
        eigen = jnp.dot(
            right_side[:, part * radial : (part + 1) * radial],
            right_ref[...],
            preferred_element_type=jnp.float32,
        )
        scaled = (eigen * factor_ref[...]).astype(jnp.bfloat16)
        field = jnp.dot(scaled, left_ref[...], preferred_element_type=jnp.float32)
        sent_ref[pl.ds(0, rows), columns] = field.astype(jnp.bfloat16)


def inverse_kernel(orders_ref, table_ref, *refs):
    takes, (out_ref, buffer, held, sems) = refs[:-4], refs[-4:]
    slot_rows, lat_block, radial = held.shape
    slots = slot_rows // 2
    table = table_ref[lax.axis_index("sec")]

    def chunk(at):
        return pltpu.make_async_copy(
            buffer.at[pl.ds(2 * at, 2)], out_ref.at[pl.ds(2 * at, 2)], sems.at[at]
        )

    def one_block(block, carry):
        begin = pl.multiple_of(block * lat_block, lat_block)
        for sec, flat, deep in np.ndindex(2, 4, 4):
            order = orders_ref[pair_at(sec, deep, flat)]
            for half, part in np.ndindex(2, 2):
                values = takes[4 * sec + flat][
                    deep, half, pl.ds(begin, lat_block), pl.ds(part * radial, radial)
                ]
                held[part * slots + 2 * order + half] = values.astype(jnp.float32)
        for at in range(0, lat_block, 2):
            two = jnp.concatenate(
                [held[:, at, :].astype(jnp.bfloat16), held[:, at + 1, :].astype(jnp.bfloat16)],
                axis=1,
            )
            values = jnp.dot(table, two, preferred_element_type=jnp.float32)
            lat = begin + at
            buffer[lat] = values[:, :radial]
            buffer[lat + 1] = values[:, radial:]
            chunk(lat // 2).start()
        return carry

    lax.fori_loop(0, buffer.shape[0] // lat_block, one_block, 0)
    for at in range(sems.shape[0]):
        chunk(at).wait()


def inverse_values(pair_orders, table, takes, lat_block):
    _, phi_count, slot_rows = table.shape
    lat_rows, radial = takes[0].shape[2], takes[0].shape[3] // 2
    out = jax.ShapeDtypeStruct((lat_rows, phi_count, radial), jnp.float32)
    return pl.pallas_call(
        inverse_kernel,
        in_specs=[smem()] + [vmem()] * (1 + len(takes)),
        out_specs=anywhere(),
        out_shape=out,
        scratch_shapes=[
            pltpu.VMEM(out.shape, jnp.float32),
            pltpu.VMEM((slot_rows, lat_block, radial), jnp.float32),
            pltpu.SemaphoreType.DMA((lat_rows // 2,)),
        ],
        compiler_params=params(36),
        cost_estimate=pl.CostEstimate(
            flops=2 * slot_rows * phi_count * lat_rows * radial,
            bytes_accessed=4 * lat_rows * phi_count * radial,
            transcendentals=0,
        ),
    )(pair_orders, table, *takes)


def on_device_compact(grid_terms, pair_orders, legendre, state, kappa, right_op, left_op):
    lat_rows, phi_count, radial = grid_terms.shape
    rows = legendre.shape[1]
    degrees = rows - 1
    padded = -(-rows // 8) * 8
    columns = 2 * radial
    pair_total = pair_orders.shape[0]
    table = natural_table(pair_total, lax.axis_size("sec"), phi_count)
    forward_table = jnp.asarray(table, jnp.bfloat16)
    inverse_table = jnp.asarray(table.transpose(0, 2, 1), jnp.bfloat16)

    def shape(*sizes, dtype=jnp.bfloat16):
        return jax.ShapeDtypeStruct(sizes, dtype)

    slab = shape(padded, 4 * lat_rows)
    cuts = call(
        cut_kernel,
        [legendre],
        [slab] * 4,
        scratch=[pltpu.VMEM((16, padded, lat_rows), jnp.bfloat16)],
    )

    held = forward_sums(forward_table, grid_terms, 8)
    block = shape(4, 2, lat_rows, columns)

    def arranged(sec, dtype):
        return call(
            functools.partial(arrange_kernel, sec),
            [pair_orders, held],
            shape(4, 4, 2, lat_rows, columns, dtype=dtype),
            mib=24,
            scalars=1,
        )

    taken = exchange(arranged(1, jnp.bfloat16), sec=1)
    keep = arranged(0, jnp.float32)
    taken, cuts = lax.optimization_barrier((taken, tuple(cuts)))
    weights = [cuts[0]] + [exchange(cuts[deep], deep=deep) for deep in (1, 2, 3)]
    blocks = call(add_kernel, [keep, taken], [block] * 4, mib=24)
    takes = [blocks[0]] + [exchange(blocks[flat], flat=flat) for flat in (1, 2, 3)]

    sums = call(
        functools.partial(degrees_kernel, degrees),
        [pair_orders, *weights, *takes],
        [shape(padded, columns, dtype=jnp.float32)] + [shape(padded, columns)] * 3,
        scalars=1,
    )
    sums = [sums[0]] + [exchange(sums[deep], deep=deep) for deep in (3, 2, 1)]

    radial_mode = np.arange(radial, dtype=np.float32) / np.float32(radial)
    damping = np.exp(-filter_strength * radial_mode**filter_power).astype(np.float32)
    factor = call(
        functools.partial(factor_kernel, degrees),
        [pair_orders, kappa[None, :], jnp.asarray(damping)[None, :]],
        shape(rows, radial, dtype=jnp.float32),
        scalars=1,
    )
    field = call(
        solve_kernel, [*sums, state, factor, right_op, left_op], shape(padded, columns)
    )
    new_state = field[None, :rows]

    moved, new_state = lax.optimization_barrier((exchange(field, deep=1), new_state))
    fields = [field, moved] + [exchange(field, deep=deep) for deep in (2, 3)]
    blocks = call(
        functools.partial(synthesis_kernel, degrees),
        [pair_orders, *weights, *fields],
        [block] * 4,
        scalars=1,
    )
    takes = [blocks[0]] + [exchange(blocks[flat], flat=flat) for flat in (1, 2, 3)]
    takes += [exchange(take, sec=1) for take in takes]
    evolved = inverse_values(pair_orders, inverse_table, takes, 16)
    return (evolved, new_state)


def on_device(*args):
    lat_rows = args[0].shape[0]
    rows = args[2].shape[1]
    sections, side_row, side_x = (lax.axis_size(name) for name in names)
    fits = args[2].shape[0] == 1 and lat_rows % 16 == 0 and rows <= 2 * lat_rows
    fits = fits and args[0].size * 4 <= 24 * 1024 * 1024
    fits = fits and (sections, side_row, side_x) == (2, 8, 2)
    return on_device_compact(*args) if fits else on_device_wide(*args)


def solution(mesh):
    return jax.shard_map(
        on_device,
        mesh=mesh,
        in_specs=(
            P(("row", "col"), "sec", None),
            P(),
            P(("sec", "row", "col"), None, None),
            P(("sec", "row", "col"), None, None),
            P(),
            P(),
            P(),
        ),
        out_specs=(P(("row", "col"), "sec", None), P(("sec", "row", "col"), None, None)),
        check_vma=False,
    )
```
